32 devices in a mesh: len: 8 (over z, x), xs: 4 (over y, core).
Axes of the slice: x: 2, y: 2, z: 4, core: 2. Of those that a mesh axis runs over, the one named last changes fastest.
Arguments:
- right_side: float32 [3, 16, 64, 4096], P(None, None, None, ('len', 'xs')), may hold values from -19 to 19
- mass_field: float32 [16, 64, 4096], P(None, None, ('len', 'xs')), may hold values from 0.5 to 2
- span_lengths: int32 [32], replicated, may hold values from 1 to 256, 4096 in all
- stick_flags: int32 [64], replicated, may hold values from 0 to 1
- normal_load: float32 [64], replicated, may hold values from 0.5 to 4
- prior_friction: float32 [2, 64], replicated, may hold values from -4 to 4
Outputs:
- increment: float32 [3, 16, 64, 4096], P(None, None, None, ('len', 'xs'))
- residual: float32 [3, 16, 64, 4096], P(None, None, None, ('len', 'xs'))
- friction: float32 [2, 64], replicated
The draws below stay inside these ranges and needn't reach their ends.
Inputs may be any that keep to these rules, and one draw needn't show every extreme that they name: `span_lengths`: the spans sum to 4096; the longest is exactly 256. `stick_flags`: 1 marks a sticking bearing, 0 a sliding one.
All inputs are finite; a program needn't handle non-finite values.
Results may differ from the reference program's by a relative error of at most 0.0003.
Values sent between devices are 32-bit elements; how exact they have to be, the bound alone decides.
No kernel may reach another device: no remote copies, remote signals or barrier semaphores. Data moves between devices by JAX's collectives and lax.ppermute only.
A program may use at most 64 MiB of HBM per device.

```python
import math
import jax
import jax.numpy as jnp
import numpy as np
from jax import lax

DEPTH = 16
NS = 64
ITERS = 3
NL = 4096
NPIER = 32
NB = 64
SPAN_MOST = 256


def draw_right_side(key, part):
    first = jax.random.fold_in(key, 0)
    along = jnp.arange(NL, dtype=jnp.float32) / max(NL - 1, 1)
    rough = jnp.clip(jax.random.normal(first, (3, DEPTH, NS, NL), jnp.float32), -3.0, 3.0)
    return rough * (1.0 + 2.0 * along)


def set_ends(values, rng, least, high):
    index_at = [jax.random.randint(jax.random.fold_in(rng, axis), (), 0, length) for axis, length in enumerate(values.shape)]
    widest = values.shape.index(max(values.shape))
    next_to = index_at[:widest] + [(index_at[widest] + 1) % values.shape[widest]] + index_at[widest + 1:]
    return values.at[tuple(index_at)].set(least).at[tuple(next_to)].set(high)


def shard_levels(own_key, shape, cuts, smallest, high):
    factor_of, own = 1.0, jax.random.fold_in(own_key, 6)
    for axis_at, blocks in cuts:
        heights = jnp.exp(jax.random.uniform(jax.random.fold_in(own, axis_at), (blocks,), jnp.float32, smallest / len(cuts), high / len(cuts)))
        factor_of = factor_of * jnp.repeat(heights, shape[axis_at] // blocks).reshape([-1 if axis == axis_at else 1 for axis in range(len(shape))])
    return factor_of


def length_profile(amount, total, most, lean):
    loads = [(1 << 20) // math.isqrt(rank ** lean) + 1 for rank in range(2, amount + 1)]
    spare, holding = total - most - (amount - 1), [1] * (amount - 1)
    while spare > 0:
        candidates = [i for i in range(amount - 1) if holding[i] < most]
        whole, budget = sum([loads[i] for i in candidates]), spare
        for i in candidates:
            more = min(most - holding[i], max(1, budget * loads[i] // whole), spare)
            holding[i] = holding[i] + more
            spare = spare - more
    return np.array([most] + holding)


def ragged(stream_key, number_of, total, limit, slope):
    if number_of == 2:
        one = jax.random.randint(stream_key, (), max(1, total - limit), min(limit, total - 1) + 1)
        return jnp.stack([one, total - one])
    tallies = jnp.asarray(length_profile(number_of, total, limit, slope), jnp.int32)
    couples = (number_of - 1) // 2
    source_of, sink = tallies[1:1 + 2 * couples:2], tallies[2:2 + 2 * couples:2]
    room = jnp.minimum(source_of - 1, limit - sink)
    moved = jax.random.randint(jax.random.fold_in(stream_key, 1), (couples,), 0, 1 << 20) % (room + 1)
    tallies = tallies.at[1:1 + 2 * couples:2].set(source_of - moved).at[2:2 + 2 * couples:2].set(sink + moved)
    return tallies[jax.random.permutation(jax.random.fold_in(stream_key, 2), number_of)]


def centred(rng, extent, scale, limit, kind=jnp.bfloat16):
    return jnp.clip(scale * jax.random.normal(rng, extent, jnp.float32), -limit, limit).astype(kind)


def setup_inputs(seed: int = 0) -> dict:
    splits = jax.random.split(jax.random.key(seed), 7)
    return {
        "right_side": draw_right_side(jax.random.fold_in(splits[6], 71), 0),
        "mass_field": jnp.clip(jnp.exp(math.log(2.0) - 1.3862944 * jax.random.uniform(splits[1], (DEPTH, NS, NL), jnp.float32) ** shard_levels(splits[1], (DEPTH, NS, NL), ((2, 32),), -0.2, 0.2)), 0.5, 2.0),
        "span_lengths": ragged(splits[2], NPIER, NL, SPAN_MOST, 2).astype(jnp.int32),
        "stick_flags": set_ends(jax.random.randint(splits[3], (NB,), 0, 2), jax.random.fold_in(splits[3], 1), 0, 1).astype(jnp.int32),
        "normal_load": jnp.clip(jnp.exp(jax.random.uniform(splits[4], (NB,), jnp.float32, math.log(0.5), math.log(4.0))), 0.5, 4.0),
        "prior_friction": centred(splits[5], (2, NB), 1.0, 4.0, jnp.float32),
    }


shear_modulus = 1.0
bulk_modulus = 1.5
elastic_stiffness = 8.0
pendulum_radius = 4.0
vertical_stiffness = 5.0
static_friction = 0.6
kinetic_friction = 0.45

def central(array, along_dim):
    widths = [(0, 0)] * array.ndim
    widths[along_dim] = (1, 1)
    padded = jnp.pad(array, widths)
    count = array.shape[along_dim]
    upper = lax.slice_in_dim(padded, 2, count + 2, axis=along_dim)
    lower = lax.slice_in_dim(padded, 0, count, axis=along_dim)
    return 0.5 * (upper - lower)

def laplace(array):
    padded = jnp.pad(array, 1)
    total = 6.0 * array
    total = total - padded[2:, 1:-1, 1:-1] - padded[:-2, 1:-1, 1:-1]
    total = total - padded[1:-1, 2:, 1:-1] - padded[1:-1, :-2, 1:-1]
    total = total - padded[1:-1, 1:-1, 2:] - padded[1:-1, 1:-1, :-2]
    return total

def operate(field, mass_field):
    dims_of = (2, 1, 0)
    divergence = central(field[0], 2) + central(field[1], 1) + central(field[2], 0)
    pieces = []
    for component in range(3):
        pieces.append(mass_field * field[component] + shear_modulus * laplace(field[component]) - bulk_modulus * central(divergence, dims_of[component]))
    return jnp.stack(pieces)

def bearing_sites(span_lengths):
    ends = (jnp.cumsum(span_lengths) - 1).astype(jnp.int32)
    along = jnp.repeat(ends, 2).astype(jnp.int32)
    across = jnp.tile(jnp.array([NS // 4, 3 * NS // 4], dtype=jnp.int32), NPIER)
    return (along, across)

def return_map(readout, stick_flags, normal_load, prior_friction):
    coeff = jnp.where(stick_flags == 1, static_friction, kinetic_friction)
    radius = coeff * normal_load
    trial = prior_friction + elastic_stiffness * readout[0:2]
    magnitude = jnp.sqrt(trial[0] * trial[0] + trial[1] * trial[1])
    friction = trial * (radius / jnp.maximum(magnitude, radius))
    horizontal = friction + normal_load / pendulum_radius * readout[0:2]
    vertical = vertical_stiffness * readout[2]
    force = jnp.concatenate([horizontal, vertical[None]], axis=0)
    return (friction, force)

def reference(right_side, mass_field, span_lengths, stick_flags, normal_load, prior_friction):
    increment = jnp.zeros_like(right_side)
    solved = right_side
    direction = right_side
    norm_now = jnp.sum(solved * solved)
    for iteration in range(ITERS):
        image = operate(direction, mass_field)
        alpha = norm_now / jnp.sum(direction * image)
        increment = increment + alpha * direction
        solved = solved - alpha * image
        norm_next = jnp.sum(solved * solved)
        direction = solved + norm_next / norm_now * direction
        norm_now = norm_next
    along, across = bearing_sites(span_lengths)
    readout = increment[:, 0, across, along]
    friction, force = return_map(readout, stick_flags, normal_load, prior_friction)
    residual = solved.at[:, 0, across, along].add(-force)
    return (increment, residual, friction)
```

```python
import functools

import jax
import jax.numpy as jnp
from jax import lax
from jax.experimental import pallas as pl
from jax.experimental.pallas import tpu as pltpu
from jax.sharding import PartitionSpec as P

ITERS = 3
SHIFT = 4.0
BULK = 1.5
ELASTIC = 8.0
RADIUS = 4.0
VERTICAL = 5.0
STATIC = 0.6
KINETIC = 0.45

AXES = ("len", "xs")
LANES = 128
PAD = 8
GROUP = 8
CHUNK = 16
HIGH = lax.Precision.HIGHEST


def turn(x, amount):
    return pltpu.roll(x, amount % LANES, x.ndim - 1)


def lane_iota(shape):
    return lax.broadcasted_iota(jnp.int32, shape, len(shape) - 1)


def pack_kernel(
    right_hbm, mass_hbm, spans, even,
    field, mass, message_a, message_b, ends,
    sems,
):
    depth, across = mass.shape[0], mass.shape[1]
    copies = [
        pltpu.make_async_copy(
            right_hbm.at[c], field.at[c, pl.ds(1, depth), pl.ds(PAD, across)], sems.at[c]
        )
        for c in range(3)
    ]
    copies.append(pltpu.make_async_copy(mass_hbm, mass, sems.at[3]))
    for copy in copies:
        copy.start()
    for c in range(3):
        for slab in (0, depth + 1):
            field[c, slab] = jnp.zeros(field.shape[2:], jnp.float32)

        def clear(d, carry, c=c):
            blank = jnp.zeros((PAD, LANES), jnp.float32)
            field[c, d, 0:PAD, :] = blank
            field[c, d, PAD + across :, :] = blank
            return carry

        lax.fori_loop(1, depth + 1, clear, 0)
    piers = spans.shape[1]
    bearings = 2 * piers
    variants = ends.shape[0]
    lane = lane_iota((piers, LANES))
    pier = lax.broadcasted_iota(jnp.int32, (piers, LANES), 0)
    lengths = jnp.broadcast_to(spans[...].astype(jnp.float32), (8, piers))
    for z in range(variants):
        if bearings <= LANES:
            bearing = lane - z * bearings
        else:
            bearing = lane + z * LANES
        upto = jnp.where(pier * 2 <= bearing, 1.0, 0.0)
        total = jnp.dot(lengths, upto, precision=HIGH, preferred_element_type=jnp.float32)
        inside = (bearing[0:1] >= 0) & (bearing[0:1] < bearings)
        ends[z : z + 1, :] = jnp.where(inside, total[0:1] - 1.0, -1e9)
    spot = lane_iota((across, LANES))
    is_even = even[0, 0] == 1
    for c in range(4):
        copies[c].wait()
        upper = jnp.zeros((across, LANES), jnp.float32)
        lower = jnp.zeros((across, LANES), jnp.float32)
        for d in range(depth):
            slab = field[c, d + 1, PAD : PAD + across, :] if c < 3 else mass[d]
            mine = (spot >= GROUP * d) & (spot < GROUP * (d + 1))
            upper = jnp.where(mine, turn(slab, GROUP * d + 6), upper)
            lower = jnp.where(mine, turn(slab, GROUP * d + 2), lower)
        message_a[c] = jnp.where(is_even, upper, lower)
        message_b[c] = jnp.where(is_even, lower, upper)


def basis_kernel(
    info, field, mass, message_a, message_b, got_a, got_b, ends,
    first, second, third, payload,
    div, packed, packed_div, edge, inner, packed_diag, sums, picked,
):
    depth, across = mass.shape[0], mass.shape[1]
    is_even = info[0, 0] == 1
    has = (info[0, 1].astype(jnp.float32), info[0, 2].astype(jnp.float32))
    start = info[0, 3].astype(jnp.float32)
    rows = pl.ds(PAD, across)
    above = pl.ds(PAD + 1, across)
    below = pl.ds(PAD - 1, across)
    spot = lane_iota((across, LANES))
    plane = spot % GROUP

    def blank_edges(ref, leading):
        for at in leading:
            ref[at + (slice(0, PAD),)] = jnp.zeros((PAD, LANES), jnp.float32)
            ref[at + (slice(PAD + across, None),)] = jnp.zeros((PAD, LANES), jnp.float32)

    blank_edges(packed, [(s, c) for s in range(2) for c in range(3)])
    blank_edges(packed_div, [(s,) for s in range(2)])
    for ref in (first, second):
        for c in range(3):
            ref[c, 0] = jnp.zeros(ref.shape[2:], jnp.float32)
            ref[c, depth + 1] = jnp.zeros(ref.shape[2:], jnp.float32)
    div[0] = jnp.zeros(div.shape[1:], jnp.float32)
    div[depth + 1] = jnp.zeros(div.shape[1:], jnp.float32)

    def clear(d, carry):
        blank = jnp.zeros((PAD, LANES), jnp.float32)
        for c in range(3):
            for ref in (first, second):
                ref[c, d, 0:PAD, :] = blank
                ref[c, d, PAD + across :, :] = blank
        div[d, 0:PAD, :] = blank
        div[d, PAD + across :, :] = blank
        return carry

    lax.fori_loop(1, depth + 1, clear, 0)

    for c in range(4):
        mine_a, mine_b, from_a, from_b = message_a[c], message_b[c], got_a[c], got_b[c]
        own_upper = jnp.where(is_even, mine_a, mine_b)
        own_lower = jnp.where(is_even, mine_b, mine_a)
        left = jnp.where(plane < 6, jnp.where(is_even, from_b, from_a), own_upper)
        right = jnp.where(plane < 2, own_lower, jnp.where(is_even, from_a, from_b))
        if c < 3:
            packed[0, c, rows, :] = left
            packed[1, c, rows, :] = right
        else:
            packed_diag[0] = left + (6.0 - SHIFT)
            packed_diag[1] = right + (6.0 - SHIFT)

    def deeper(x):
        return jnp.where(spot < LANES - GROUP, turn(x, -GROUP), 0.0)

    def shallower(x):
        return jnp.where(spot >= GROUP, turn(x, GROUP), 0.0)

    def packed_divergence():
        for s in range(2):
            x0 = packed[s, 0, rows, :]
            x2 = packed[s, 2, rows, :]
            w = turn(x0, -1) - turn(x0, 1)
            w = w + (packed[s, 1, above, :] - packed[s, 1, below, :])
            w = w + (deeper(x2) - shallower(x2))
            packed_div[s, rows, :] = w * (0.25 * BULK * has[s])

    def fill_edge():
        for c in range(3):
            edge[c] = jnp.where(plane == 5, packed[0, c, rows, :], turn(packed[1, c, rows, :], 2))
        edge[3] = jnp.where(plane == 5, packed_div[0, rows, :], turn(packed_div[1, rows, :], 2))

    def packed_step():
        for s in range(2):
            w = packed_div[s, rows, :]
            slopes = (
                turn(w, -1) - turn(w, 1),
                packed_div[s, above, :] - packed_div[s, below, :],
                deeper(w) - shallower(w),
            )
            for c in range(3):
                x = packed[s, c, rows, :]
                total = (turn(x, -1) + turn(x, 1)) + (deeper(x) + shallower(x))
                total = total + (packed[s, c, above, :] + packed[s, c, below, :])
                image = packed_diag[s] * x - total - slopes[c]
                packed[s, c, rows, :] = image * has[s]

    def insert_inner():
        for c in range(3):
            own = inner[c]
            packed[0, c, rows, :] = jnp.where(plane < 6, packed[0, c, rows, :], own)
            packed[1, c, rows, :] = jnp.where(plane < 2, turn(own, -4), packed[1, c, rows, :])

    zero_sum = jnp.zeros((8, LANES), jnp.float32)
    chunks = range(0, across, CHUNK)

    def folded(x):
        return sum(x[i : i + 8] for i in range(0, CHUNK, 8))

    def step(source, target, target_pad, last):
        lane = lane_iota((CHUNK, LANES))
        at_left = lane == 0
        at_right = lane == LANES - 1

        def both(x, beside):
            return (
                jnp.where(at_left, beside, turn(x, 1)),
                jnp.where(at_right, beside, turn(x, -1)),
            )

        def divergence(d, carry):
            amount = LANES - 5 - GROUP * d
            for r in chunks:
                here = pl.ds(PAD + r, CHUNK)
                beside = pltpu.roll(edge[0, r : r + CHUNK, :], amount, 1)
                left, right = both(source[0, d + 1, here, :], beside)
                w = right - left
                w = w + (
                    source[1, d + 1, pl.ds(PAD + r + 1, CHUNK), :]
                    - source[1, d + 1, pl.ds(PAD + r - 1, CHUNK), :]
                )
                w = w + (source[2, d + 2, here, :] - source[2, d, here, :])
                div[d + 1, here, :] = w * (0.25 * BULK)
            return carry

        lax.fori_loop(0, depth, divergence, 0)

        def image(d, carry):
            norm, cross = carry
            amount = LANES - 5 - GROUP * d
            place = GROUP * d + 6
            mine = (lane >= GROUP * d + 4) & (lane < GROUP * d + 8)
            for r in chunks:
                here = pl.ds(PAD + r, CHUNK)
                up = pl.ds(PAD + r + 1, CHUNK)
                down = pl.ds(PAD + r - 1, CHUNK)
                diag = mass[d, r : r + CHUNK, :] + (6.0 - SHIFT)
                w_left, w_right = both(
                    div[d + 1, here, :], pltpu.roll(edge[3, r : r + CHUNK, :], amount, 1)
                )
                slopes = (
                    w_right - w_left,
                    div[d + 1, up, :] - div[d + 1, down, :],
                    div[d + 2, here, :] - div[d, here, :],
                )
                for c in range(3):
                    x = source[c, d + 1, here, :]
                    left, right = both(x, pltpu.roll(edge[c, r : r + CHUNK, :], amount, 1))
                    total = (left + right) + (source[c, d, here, :] + source[c, d + 2, here, :])
                    total = total + (source[c, d + 1, up, :] + source[c, d + 1, down, :])
                    out = diag * x - total - slopes[c]
                    target[c, d + target_pad[0], pl.ds(target_pad[1] + r, CHUNK), :] = out
                    if not last:
                        inner[c, r : r + CHUNK, :] = jnp.where(
                            mine, pltpu.roll(out, lax.rem(place, LANES), 1), inner[c, r : r + CHUNK, :]
                        )
                    norm = norm + folded(x * x)
                    cross = cross + folded(x * out)
            return norm, cross

        return lax.fori_loop(0, depth, image, (zero_sum, zero_sum))

    packed_divergence()
    fill_edge()
    moments = list(step(field, first, (1, PAD), False))
    packed_step()
    insert_inner()
    packed_divergence()
    fill_edge()
    moments += step(first, second, (1, PAD), False)
    packed_step()
    insert_inner()
    packed_divergence()
    fill_edge()
    moments += step(second, third, (0, 0), True)

    variants = ends.shape[0]
    per = payload_per(variants, info)
    pieces = 1 if per > 1 else variants
    blocks = 9 * pieces
    bearing_rows = -(-blocks // per)
    picked[...] = jnp.zeros(picked.shape, jnp.float32)
    for block in range(blocks):
        value, piece = block // pieces, block % pieces
        row, z = block // per, (block % per if per > 1 else piece)
        ref, c = (field, first, second)[value // 3], value % 3
        for side in range(2):
            at = PAD + (1 + 2 * side) * across // 4
            column = (2 * z + side) * LANES
            picked[row : row + 1, column : column + LANES] = ref[c, 1, at : at + 1, :]
    along = lax.broadcasted_iota(jnp.int32, (LANES, LANES), 0).astype(jnp.float32) + start
    parity = lane_iota((LANES, LANES)) % 2
    total = jnp.zeros((picked.shape[0], LANES), jnp.float32)
    for z in range(variants):
        site = jnp.broadcast_to(ends[z : z + 1, :], (LANES, LANES)) == along
        for side in range(2):
            column = (2 * z + side) * LANES
            hit = jnp.where(site & (parity == side), 1.0, 0.0)
            total = total + jnp.dot(
                picked[:, column : column + LANES], hit,
                precision=HIGH, preferred_element_type=jnp.float32,
            )
    sums[...] = jnp.zeros(sums.shape, jnp.float32)
    sums[0:bearing_rows, :] = total[0:bearing_rows]
    low = lane_iota((1, LANES)) < LANES // 2
    for pair in range(3):
        halves = []
        for moment in moments[2 * pair : 2 * pair + 2]:
            flat = jnp.sum(moment, axis=0, keepdims=True)
            halves.append(flat + turn(flat, LANES // 2))
        sums[bearing_rows + pair : bearing_rows + pair + 1, :] = jnp.where(low, *halves)
    out = sums[...]
    for device in range(payload.shape[0]):
        payload[device] = out


def payload_per(variants, info):
    return info.shape[1] - 4


def coefficients(moment):
    def dot(a, b):
        total = None
        for i, left in enumerate(a):
            for j, right in enumerate(b):
                term = left * right * moment[i + j]
                total = term if total is None else total + term
        return total

    one = jnp.ones_like(moment[0])
    solved, direction, increment = [one], [one], []
    norm = moment[0]
    for iteration in range(ITERS):
        image = [SHIFT * p for p in direction] + [jnp.zeros_like(one)]
        for i, p in enumerate(direction):
            image[i + 1] = image[i + 1] + p
        alpha = norm / dot(direction, image)
        increment = [
            alpha * p + (increment[i] if i < len(increment) else 0.0) for i, p in enumerate(direction)
        ]
        solved = [
            (solved[i] if i < len(solved) else 0.0) - alpha * q for i, q in enumerate(image)
        ]
        if iteration + 1 < ITERS:
            after = dot(solved, solved)
            ratio = after / norm
            direction = [
                s + (ratio * direction[i] if i < len(direction) else 0.0)
                for i, s in enumerate(solved)
            ]
            norm = after
    return increment, solved


def combine_kernel(
    info, gathered, field, first, second, third, ends, stick, load, prior,
    increment_hbm, residual_hbm, friction,
    increment, residual, forces, sems,
):
    depth, across = third.shape[1], third.shape[2]
    start = info[0, 3].astype(jnp.float32)
    bearings = load.shape[1]
    variants = ends.shape[0]
    per = payload_per(variants, info)
    pieces = 1 if per > 1 else variants
    width = min(bearings, LANES)
    bearing_rows = -(-9 * pieces // per)
    parts = [gathered[i] for i in range(gathered.shape[0])]
    while len(parts) > 1:
        parts = [sum(parts[i : i + 2]) for i in range(0, len(parts), 2)]
    total = parts[0]
    low = lane_iota((1, LANES)) < LANES // 2
    moments = []
    for n in range(6):
        row = total[bearing_rows + n // 2 : bearing_rows + n // 2 + 1]
        row = jnp.where(low == (n % 2 == 0), row, 0.0)
        moments.append(jnp.sum(row, axis=1, keepdims=True))
    grow, keep = coefficients(moments)

    forces[...] = jnp.zeros(forces.shape, jnp.float32)
    lane = lane_iota((1, width))
    for piece in range(pieces):
        span = slice(piece * LANES, piece * LANES + width)
        readout = []
        for c in range(3):
            value = None
            for k in range(ITERS):
                block = (3 * k + c) * pieces + piece
                row = total[block // per : block // per + 1]
                if per > 1 and block % per:
                    row = turn(row, LANES - (block % per) * bearings)
                term = grow[k] * row[:, :width]
                value = term if value is None else value + term
            readout.append(value)
        weight = load[:, span]
        radius = jnp.where(stick[:, span] == 1, STATIC, KINETIC) * weight
        trial = [prior[c : c + 1, span] + ELASTIC * readout[c] for c in range(2)]
        magnitude = jnp.sqrt(trial[0] * trial[0] + trial[1] * trial[1])
        scale = radius / jnp.maximum(magnitude, radius)
        held = [t * scale for t in trial]
        for c in range(2):
            friction[c : c + 1, span] = held[c]
        force = [held[c] + weight / RADIUS * readout[c] for c in range(2)] + [VERTICAL * readout[2]]
        for c in range(3):
            for side in range(2):
                forces[2 * c + side : 2 * c + side + 1, span] = jnp.where(
                    lane % 2 == side, force[c], 0.0
                )
    along = lax.broadcasted_iota(jnp.int32, (LANES, LANES), 0).astype(jnp.float32) + start
    placed = jnp.zeros((8, LANES), jnp.float32)
    for piece in range(pieces):
        site = jnp.broadcast_to(ends[piece : piece + 1, :], (LANES, LANES)) == along
        placed = placed + lax.dot_general(
            forces[:, piece * LANES : (piece + 1) * LANES], jnp.where(site, 1.0, 0.0),
            (((1,), (1,)), ((), ())), precision=HIGH, preferred_element_type=jnp.float32,
        )

    grow = [jnp.broadcast_to(g, (CHUNK, LANES)) for g in grow]
    keep = [jnp.broadcast_to(g, (CHUNK, LANES)) for g in keep]

    def level(d, c):
        for r in range(0, across, CHUNK):
            here = pl.ds(PAD + r, CHUNK)
            v = [ref[c, d + 1, here, :] for ref in (field, first, second)]
            v.append(third[c, d, r : r + CHUNK, :])
            increment[c, d, r : r + CHUNK, :] = grow[0] * v[0] + grow[1] * v[1] + grow[2] * v[2]
            residual[c, d, r : r + CHUNK, :] = (
                keep[0] * v[0] + keep[1] * v[1] + (keep[2] * v[2] + keep[3] * v[3])
            )

    def run(c, begin, end):
        def body(d, carry):
            level(d, c)
            return carry

        lax.fori_loop(begin, end, body, 0)

    copies = []

    def send(c, begin, end):
        for which, (ref, hbm) in enumerate(((increment, increment_hbm), (residual, residual_hbm))):
            part = pl.ds(begin, end - begin)
            copy = pltpu.make_async_copy(
                ref.at[c, part], hbm.at[c, part], sems.at[which, 2 * c + (begin > 0)]
            )
            copy.start()
            copies.append(copy)

    half = depth // 2
    for c in range(3):
        run(c, 0, half)
        for side in range(2):
            at = (1 + 2 * side) * across // 4
            residual[c, 0, at : at + 1, :] = (
                residual[c, 0, at : at + 1, :] - placed[2 * c + side : 2 * c + side + 1]
            )
        send(c, 0, half)
        run(c, half, depth)
        send(c, half, depth)
    for copy in copies:
        copy.wait()


def vmem_spec():
    return pl.BlockSpec(memory_space=pltpu.VMEM)


def smem_spec():
    return pl.BlockSpec(memory_space=pltpu.SMEM)


def shards(count, right_side, mass_field, span_lengths, stick_flags, normal_load, prior_friction):
    f32 = jnp.float32
    depth, across, along = right_side.shape[1:]
    piers = span_lengths.shape[0]
    bearings = 2 * piers
    per = LANES // bearings if bearings <= LANES else 1
    variants = per if bearings <= LANES else bearings // LANES
    pieces = 1 if per > 1 else variants
    bearing_rows = -(-9 * pieces // per)
    rows = -(-(bearing_rows + 3) // 8) * 8
    pick_rows = -(-bearing_rows // 8) * 8
    index = lax.axis_index(AXES)
    even = (index % 2 == 0).astype(jnp.int32).reshape(1, 1)
    padded = (depth + 2, across + 2 * PAD, along)
    limit = pltpu.CompilerParams(vmem_limit_bytes=32 * 1024 * 1024)
    field, mass, message_a, message_b, ends = pl.pallas_call(
        pack_kernel,
        out_shape=(
            pltpu.VMEM((3,) + padded, f32),
            pltpu.VMEM((depth, across, along), f32),
            jax.ShapeDtypeStruct((4, across, LANES), f32),
            jax.ShapeDtypeStruct((4, across, LANES), f32),
            jax.ShapeDtypeStruct((variants, LANES), f32),
        ),
        in_specs=[
            pl.BlockSpec(memory_space=pl.ANY), pl.BlockSpec(memory_space=pl.ANY),
            vmem_spec(), smem_spec(),
        ],
        out_specs=(vmem_spec(),) * 5,
        scratch_shapes=[pltpu.SemaphoreType.DMA((4,))],
        compiler_params=limit,
        name="pack",
    )(right_side, mass_field, span_lengths.reshape(1, piers), even)

    pairs_a = [p for i in range(0, count - 1, 2) for p in ((i, i + 1), (i + 1, i))]
    pairs_b = [p for i in range(1, count - 1, 2) for p in ((i, i + 1), (i + 1, i))]
    got_b = lax.ppermute(message_b, AXES, pairs_b)
    got_a = lax.ppermute(message_a, AXES, pairs_a)

    info = jnp.stack(
        [
            (index % 2 == 0).astype(jnp.int32),
            (index > 0).astype(jnp.int32),
            (index < count - 1).astype(jnp.int32),
            (index * along).astype(jnp.int32),
        ]
        + [jnp.int32(0)] * per
    ).reshape(1, 4 + per)
    first, second, third, payload = pl.pallas_call(
        basis_kernel,
        out_shape=(
            pltpu.VMEM((3,) + padded, f32),
            pltpu.VMEM((3,) + padded, f32),
            pltpu.VMEM((3, depth, across, along), f32),
            jax.ShapeDtypeStruct((count, rows, LANES), f32),
        ),
        in_specs=[smem_spec()] + [vmem_spec()] * 7,
        out_specs=(vmem_spec(),) * 4,
        scratch_shapes=[
            pltpu.VMEM(padded, f32),
            pltpu.VMEM((2, 3, across + 2 * PAD, LANES), f32),
            pltpu.VMEM((2, across + 2 * PAD, LANES), f32),
            pltpu.VMEM((4, across, LANES), f32),
            pltpu.VMEM((3, across, LANES), f32),
            pltpu.VMEM((2, across, LANES), f32),
            pltpu.VMEM((rows, LANES), f32),
            pltpu.VMEM((pick_rows, 2 * variants * LANES), f32),
        ],
        compiler_params=limit,
        name="basis",
    )(info, field, mass, message_a, message_b, got_a, got_b, ends)

    gathered = lax.all_to_all(payload, AXES, 0, 0)

    increment, residual, friction = pl.pallas_call(
        combine_kernel,
        out_shape=(
            jax.ShapeDtypeStruct(right_side.shape, f32),
            jax.ShapeDtypeStruct(right_side.shape, f32),
            jax.ShapeDtypeStruct((2, bearings), f32),
        ),
        in_specs=[smem_spec()] + [vmem_spec()] * 9,
        out_specs=(
            pl.BlockSpec(memory_space=pl.ANY), pl.BlockSpec(memory_space=pl.ANY), vmem_spec(),
        ),
        scratch_shapes=[
            pltpu.VMEM(right_side.shape, f32),
            pltpu.VMEM(right_side.shape, f32),
            pltpu.VMEM((8, pieces * LANES), f32),
            pltpu.SemaphoreType.DMA((2, 6)),
        ],
        compiler_params=limit,
        name="combine",
    )(
        info, gathered, field, first, second, third, ends,
        stick_flags.reshape(1, bearings), normal_load.reshape(1, bearings), prior_friction,
    )
    return increment, residual, friction


def solution(mesh):
    count = mesh.shape["len"] * mesh.shape["xs"]
    along = P(None, None, None, AXES)
    in_specs = (along, P(None, None, AXES), P(), P(), P(), P())
    return jax.shard_map(
        functools.partial(shards, count), mesh=mesh,
        in_specs=in_specs, out_specs=(along, along, P()), check_vma=False,
    )
```

```python
import functools

import jax
import jax.numpy as jnp
from jax import lax
from jax.experimental import pallas as pl
from jax.experimental.pallas import tpu as pltpu
from jax.sharding import PartitionSpec as P

ITERS = 3
SHIFT = 4.0
BULK = 1.5
ELASTIC = 8.0
RADIUS = 4.0
VERTICAL = 5.0
STATIC = 0.6
KINETIC = 0.45

AXES = ("len", "xs")
LANES = 128
ROWS = 8
PAD = 8
EDGE = 16
HALF = EDGE // 2
BLOCKS = LANES // EDGE
PITCH = 3 * ROWS
CHUNK = 16
HIGH = lax.Precision.HIGHEST
LIMIT = pltpu.CompilerParams(vmem_limit_bytes=32 * 1024 * 1024)


def turn(x, amount):
    return pltpu.roll(x, amount % LANES, x.ndim - 1)


def lane_iota(shape):
    return lax.broadcasted_iota(jnp.int32, shape, len(shape) - 1)


def loop(count, step, body, init):
    def several(i, carry):
        for j in range(step):
            carry = body(i * step + j, carry)
        return carry

    return lax.fori_loop(0, count // step, several, init)


def device_index():
    return lax.axis_index(AXES[0]) * lax.axis_size(AXES[1]) + lax.axis_index(AXES[1])


def clear_padding(ref, lead, depth, across):
    for slab in (0, depth + 1):
        ref[lead + (slab,)] = jnp.zeros((across + 2 * PAD, LANES), jnp.float32)
    blank = jnp.zeros((PAD, LANES), jnp.float32)
    for d in range(1, depth + 1):
        ref[lead + (d, slice(0, PAD))] = blank
        ref[lead + (d, slice(PAD + across, None))] = blank


def pack_kernel(right_hbm, mass_hbm, field, mass, packed, message_a, message_b, sems):
    depth, across = mass.shape[0], mass.shape[1]
    copies = [
        pltpu.make_async_copy(
            right_hbm.at[c], field.at[c, pl.ds(1, depth), pl.ds(PAD, across)], sems.at[c]
        )
        for c in range(3)
    ]
    copies.append(pltpu.make_async_copy(mass_hbm, mass, sems.at[3]))
    for copy in copies:
        copy.start()
    for c in range(3):
        clear_padding(field, (c,), depth, across)
    is_even = device_index() % 2 == 0
    lane = lane_iota((ROWS, LANES))
    block_of = lane // EDGE
    first_half = lane % EDGE < HALF
    for c in range(4):
        copies[c].wait()
        edges = []
        for d in range(depth):
            edge = None
            for b in range(across // ROWS):
                row = pl.ds(b * ROWS + (PAD if c < 3 else 0), ROWS)
                tile = field[c, d + 1, row, :] if c < 3 else mass[d, row, :]
                moved = turn(tile, EDGE * b + HALF)
                edge = moved if edge is None else jnp.where(block_of == b, moved, edge)
            packed[c, d] = edge
            edges.append(edge)
        for d in range(depth // 2):
            low, high = edges[d], edges[d + depth // 2]
            rightward = jnp.where(first_half, low, turn(high, HALF))
            leftward = jnp.where(first_half, turn(low, -HALF), high)
            message_a[c, d] = jnp.where(is_even, rightward, leftward)
            message_b[c, d] = jnp.where(is_even, leftward, rightward)


def folded(x):
    return sum(x[i : i + ROWS] for i in range(0, x.shape[0], ROWS))


def cyclic_step(source, mass, div, store, moments, step):
    depth, across = mass.shape[0], mass.shape[1]
    chunks = range(0, across, CHUNK)

    def divergence(d, carry):
        for r in chunks:
            here, up, down = (pl.ds(PAD + r + by, CHUNK) for by in (0, 1, -1))
            x = source[0, d + 1, here, :]
            w = turn(x, -1) - turn(x, 1)
            w = w + (source[1, d + 1, up, :] - source[1, d + 1, down, :])
            w = w + (source[2, d + 2, here, :] - source[2, d, here, :])
            div[d + 1, here, :] = w * (0.25 * BULK)
        return carry

    loop(depth, step, divergence, 0)
    lane = lane_iota((CHUNK, LANES))
    inside = (lane >= 2) & (lane < LANES - 2)

    def image(d, carry):
        norm, cross = carry
        for r in chunks:
            here, up, down = (pl.ds(PAD + r + by, CHUNK) for by in (0, 1, -1))
            diag = mass[d, r : r + CHUNK, :] + (6.0 - SHIFT)
            w = div[d + 1, here, :]
            norms, crosses = [], []
            for c in range(3):
                x = source[c, d + 1, here, :]
                if c == 0:
                    total = turn(x + w, -1) + turn(x - w, 1)
                else:
                    total = turn(x, -1) + turn(x, 1)
                if c == 1:
                    total = total + (div[d + 1, up, :] - div[d + 1, down, :])
                if c == 2:
                    total = total + (div[d + 2, here, :] - div[d, here, :])
                total = total + (source[c, d, here, :] + source[c, d + 2, here, :])
                total = total + (source[c, d + 1, up, :] + source[c, d + 1, down, :])
                out = diag * x - total
                store(c, d, r, out)
                norms.append(x * x)
                crosses.append(jnp.where(inside, x, 0.0) * out)
            norm = norm + folded(norms[0] + norms[1] + norms[2])
            cross = cross + folded(crosses[0] + crosses[1] + crosses[2])
        return norm, cross

    norm, cross = loop(depth, step, image, (jnp.zeros((ROWS, LANES), jnp.float32),) * 2)
    moments[0] = norm
    moments[1] = cross


def first_kernel(field, mass, spans, first_raw, moments, ends, div):
    depth, across = mass.shape[0], mass.shape[1]
    clear_padding(div, (), depth, across)

    def store(c, d, r, out):
        first_raw[c, d, r : r + CHUNK, :] = out

    cyclic_step(field, mass, div, store, moments, 4)
    piers = spans.shape[1]
    bearings = 2 * piers
    lane = lane_iota((piers, LANES))
    pier = lax.broadcasted_iota(jnp.int32, (piers, LANES), 0)
    lengths = jnp.broadcast_to(spans[...].astype(jnp.float32), (ROWS, piers))
    for z in range(ends.shape[0]):
        bearing = lane - z * bearings if bearings <= LANES else lane + z * LANES
        upto = jnp.where(pier * 2 <= bearing, 1.0, 0.0)
        total = jnp.dot(lengths, upto, precision=HIGH, preferred_element_type=jnp.float32)
        inside = (bearing[0:1] >= 0) & (bearing[0:1] < bearings)
        ends[z : z + 1, :] = jnp.where(inside, total[0:1] - 1.0, -1e9)


def basis_kernel(
    per, field, mass, packed, got_a, got_b, first_raw, early, ends,
    first, second, third_raw, fix, payload,
    div, edge, edge_div, edge_diag, fixes, moments, sums, picked,
):
    depth, across = mass.shape[0], mass.shape[1]
    index = device_index()
    count = lax.axis_size(AXES[0]) * lax.axis_size(AXES[1])
    is_even = index % 2 == 0
    lane = lane_iota((ROWS, LANES))
    first_half = lane % EDGE < HALF
    ones = jnp.ones((ROWS, LANES), jnp.float32)
    keep = (
        jnp.where(first_half & (index == 0), 0.0, ones),
        jnp.where(jnp.logical_not(first_half) & (index == count - 1), 0.0, ones),
    )
    both = range(2)
    comps = range(3)
    half = depth // 2
    blank = jnp.zeros((ROWS, LANES), jnp.float32)

    def row_of(d):
        return (d + 1) * PITCH + ROWS

    for c in range(4):
        for d in range(half):
            a, b = got_a[c, d], got_b[c, d]
            from_left = jnp.where(is_even, b, a)
            from_right = jnp.where(is_even, a, b)
            low, high = packed[c, d], packed[c, d + half]
            for at, left, right in (
                (
                    d,
                    jnp.where(first_half, from_left, low),
                    jnp.where(first_half, low, turn(from_right, HALF)),
                ),
                (
                    d + half,
                    jnp.where(first_half, turn(from_left, -HALF), high),
                    jnp.where(first_half, high, from_right),
                ),
            ):
                if c < 3:
                    edge[0, c, pl.ds(row_of(at), ROWS), :] = left
                    edge[1, c, pl.ds(row_of(at), ROWS), :] = right
                else:
                    edge_diag[0, at] = left + (6.0 - SHIFT)
                    edge_diag[1, at] = right + (6.0 - SHIFT)
    for s in both:
        for c in comps:
            edge[s, c, pl.ds(ROWS, ROWS), :] = blank
            edge[s, c, pl.ds(row_of(depth), ROWS), :] = blank
        edge_div[s, pl.ds(ROWS, ROWS), :] = blank
        edge_div[s, pl.ds(row_of(depth), ROWS), :] = blank

    def join_blocks(ref, lead):
        for d in (0, half):
            base = row_of(d)
            last = ref[lead + (pl.ds(base + ROWS - 1, half, stride=PITCH), slice(None))]
            ahead = ref[lead + (pl.ds(base, half, stride=PITCH), slice(None))]
            spot = lane_iota((half, LANES))
            ref[lead + (pl.ds(base - 1, half, stride=PITCH), slice(None))] = jnp.where(
                spot >= EDGE, turn(last, EDGE), 0.0
            )
            ref[lead + (pl.ds(base + ROWS, half, stride=PITCH), slice(None))] = jnp.where(
                spot < LANES - EDGE, turn(ahead, -EDGE), 0.0
            )

    def at(s, c, d, by=0):
        return edge[s, c, pl.ds(row_of(d) + by, ROWS), :]

    def div_at(s, d, by=0):
        return edge_div[s, pl.ds(row_of(d) + by, ROWS), :]

    middle = (lane % EDGE >= HALF - 2) & (lane % EDGE < HALF + 2)

    def edge_step(level):
        for s in both:
            for c in comps:
                join_blocks(edge, (s, c))
        for s in both:
            for d in range(depth):
                x = at(s, 0, d)
                w = turn(x, -1) - turn(x, 1)
                w = w + (at(s, 1, d, 1) - at(s, 1, d, -1))
                w = w + (at(s, 2, d + 1) - at(s, 2, d - 1))
                edge_div[s, pl.ds(row_of(d), ROWS), :] = w * ((0.25 * BULK) * keep[s])
            join_blocks(edge_div, (s,))
        cross = blank
        for c in comps:
            images = []
            for d in range(depth):
                pair = []
                for s in both:
                    x = at(s, c, d)
                    if c == 0:
                        w = div_at(s, d)
                        total = turn(x + w, -1) + turn(x - w, 1)
                    else:
                        total = turn(x, -1) + turn(x, 1)
                    if c == 1:
                        total = total + (div_at(s, d, 1) - div_at(s, d, -1))
                    if c == 2:
                        total = total + (div_at(s, d + 1) - div_at(s, d - 1))
                    total = total + (at(s, c, d - 1) + at(s, c, d + 1))
                    total = total + (at(s, c, d, 1) + at(s, c, d, -1))
                    pair.append((edge_diag[s, d] * x - total) * keep[s])
                images.append(pair)
                old = packed[c, d] if level == 0 else fixes[level - 1, c, d]
                new = jnp.where(first_half, pair[1], pair[0])
                if level + 1 < ITERS:
                    fixes[level, c, d] = new
                else:
                    fix[c, d] = new
                cross = cross + old * new
            for d in range(depth):
                for s in both:
                    edge[s, c, pl.ds(row_of(d), ROWS), :] = images[d][s]
        return jnp.where(middle, cross, 0.0)

    crosses = [edge_step(level) for level in range(ITERS)]

    clear_padding(div, (), depth, across)
    for c in comps:
        clear_padding(first, (c,), depth, across)
        clear_padding(second, (c,), depth, across)

    spot = lane_iota((CHUNK, LANES))
    outside = (spot < 2) | (spot >= LANES - 2)

    def mended(level, c, d, r, value):
        edges = fixes[level, c, d]
        moved = [turn(edges, -(EDGE * ((r + i) // ROWS) + HALF)) for i in range(0, CHUNK, ROWS)]
        return jnp.where(outside, jnp.concatenate(moved, axis=0), value)

    def mend_first(d, carry):
        for c in comps:
            for r in range(0, across, CHUNK):
                first[c, d + 1, pl.ds(PAD + r, CHUNK), :] = mended(
                    0, c, d, r, first_raw[c, d, r : r + CHUNK, :]
                )
        return carry

    loop(depth, 2, mend_first, 0)

    def store_second(c, d, r, out):
        second[c, d + 1, pl.ds(PAD + r, CHUNK), :] = mended(1, c, d, r, out)

    def store_third(c, d, r, out):
        third_raw[c, d, r : r + CHUNK, :] = out

    cyclic_step(first, mass, div, store_second, moments.at[0], 2)
    cyclic_step(second, mass, div, store_third, moments.at[1], 4)
    parts = [
        early[0], early[1] + crosses[0],
        moments[0, 0], moments[0, 1] + crosses[1],
        moments[1, 0], moments[1, 1] + crosses[2],
    ]

    variants = ends.shape[0]
    pieces = 1 if per > 1 else variants
    blocks = 3 * ITERS * pieces
    bearing_rows = -(-blocks // per)
    picked[...] = jnp.zeros(picked.shape, jnp.float32)
    for block in range(blocks):
        value, piece = block // pieces, block % pieces
        row, z = block // per, (block % per if per > 1 else piece)
        ref, c = (field, first, second)[value // 3], value % 3
        for side in both:
            place = PAD + (1 + 2 * side) * across // 4
            column = (2 * z + side) * LANES
            picked[row : row + 1, column : column + LANES] = ref[c, 1, place : place + 1, :]
    start = (index * LANES).astype(jnp.float32)
    along = lax.broadcasted_iota(jnp.int32, (LANES, LANES), 0).astype(jnp.float32) + start
    parity = lane_iota((LANES, LANES)) % 2
    total = jnp.zeros((picked.shape[0], LANES), jnp.float32)
    for z in range(variants):
        site = jnp.broadcast_to(ends[z : z + 1, :], (LANES, LANES)) == along
        for side in both:
            column = (2 * z + side) * LANES
            hit = jnp.where(site & (parity == side), 1.0, 0.0)
            total = total + jnp.dot(
                picked[:, column : column + LANES], hit,
                precision=HIGH, preferred_element_type=jnp.float32,
            )
    sums[...] = jnp.zeros(sums.shape, jnp.float32)
    sums[0:bearing_rows, :] = total[0:bearing_rows]
    low = lane_iota((1, LANES)) < LANES // 2
    for pair in range(3):
        halves = []
        for part in parts[2 * pair : 2 * pair + 2]:
            flat = jnp.sum(part, axis=0, keepdims=True)
            halves.append(flat + turn(flat, LANES // 2))
        sums[bearing_rows + pair : bearing_rows + pair + 1, :] = jnp.where(low, *halves)
    out = sums[...]
    for device in range(payload.shape[0]):
        payload[device] = out


def coefficients(moment):
    def dot(a, b):
        total = None
        for i, left in enumerate(a):
            for j, right in enumerate(b):
                term = left * right * moment[i + j]
                total = term if total is None else total + term
        return total

    one = jnp.ones_like(moment[0])
    solved, direction, increment = [one], [one], []
    norm = moment[0]
    for iteration in range(ITERS):
        image = [SHIFT * p for p in direction] + [jnp.zeros_like(one)]
        for i, p in enumerate(direction):
            image[i + 1] = image[i + 1] + p
        alpha = norm / dot(direction, image)
        increment = [
            alpha * p + (increment[i] if i < len(increment) else 0.0) for i, p in enumerate(direction)
        ]
        solved = [
            (solved[i] if i < len(solved) else 0.0) - alpha * q for i, q in enumerate(image)
        ]
        if iteration + 1 < ITERS:
            after = dot(solved, solved)
            ratio = after / norm
            direction = [
                s + (ratio * direction[i] if i < len(direction) else 0.0)
                for i, s in enumerate(solved)
            ]
            norm = after
    return increment, solved


def combine_kernel(
    per, gathered, field, first, second, third_raw, fix, ends, stick, load, prior,
    increment_hbm, residual_hbm, friction,
    increment, residual, forces, sems,
):
    depth, across = third_raw.shape[1], third_raw.shape[2]
    start = (device_index() * LANES).astype(jnp.float32)
    bearings = load.shape[1]
    variants = ends.shape[0]
    pieces = 1 if per > 1 else variants
    width = min(bearings, LANES)
    bearing_rows = -(-9 * pieces // per)
    parts = [gathered[i] for i in range(gathered.shape[0])]
    while len(parts) > 1:
        parts = [sum(parts[i : i + 2]) for i in range(0, len(parts), 2)]
    total = parts[0]
    low = lane_iota((1, LANES)) < LANES // 2
    moments = []
    for n in range(6):
        row = total[bearing_rows + n // 2 : bearing_rows + n // 2 + 1]
        row = jnp.where(low == (n % 2 == 0), row, 0.0)
        moments.append(jnp.sum(row, axis=1, keepdims=True))
    grow, keep = coefficients(moments)

    forces[...] = jnp.zeros(forces.shape, jnp.float32)
    lane = lane_iota((1, width))
    for piece in range(pieces):
        span = slice(piece * LANES, piece * LANES + width)
        readout = []
        for c in range(3):
            value = None
            for k in range(ITERS):
                block = (3 * k + c) * pieces + piece
                row = total[block // per : block // per + 1]
                if per > 1 and block % per:
                    row = turn(row, LANES - (block % per) * bearings)
                term = grow[k] * row[:, :width]
                value = term if value is None else value + term
            readout.append(value)
        weight = load[:, span]
        radius = jnp.where(stick[:, span] == 1, STATIC, KINETIC) * weight
        trial = [prior[c : c + 1, span] + ELASTIC * readout[c] for c in range(2)]
        magnitude = jnp.sqrt(trial[0] * trial[0] + trial[1] * trial[1])
        scale = radius / jnp.maximum(magnitude, radius)
        held = [t * scale for t in trial]
        for c in range(2):
            friction[c : c + 1, span] = held[c]
        force = [held[c] + weight / RADIUS * readout[c] for c in range(2)] + [VERTICAL * readout[2]]
        for c in range(3):
            for side in range(2):
                forces[2 * c + side : 2 * c + side + 1, span] = jnp.where(
                    lane % 2 == side, force[c], 0.0
                )
    along = lax.broadcasted_iota(jnp.int32, (LANES, LANES), 0).astype(jnp.float32) + start
    placed = jnp.zeros((8, LANES), jnp.float32)
    for piece in range(pieces):
        site = jnp.broadcast_to(ends[piece : piece + 1, :], (LANES, LANES)) == along
        placed = placed + lax.dot_general(
            forces[:, piece * LANES : (piece + 1) * LANES], jnp.where(site, 1.0, 0.0),
            (((1,), (1,)), ((), ())), precision=HIGH, preferred_element_type=jnp.float32,
        )

    grow = [jnp.broadcast_to(g, (CHUNK, LANES)) for g in grow]
    keep = [jnp.broadcast_to(g, (CHUNK, LANES)) for g in keep]

    spot = lane_iota((CHUNK, LANES))
    outside = (spot < 2) | (spot >= LANES - 2)

    def run(c, begin, end):
        def body(i, carry):
            d = begin + i
            edges = fix[c, d]
            for r in range(0, across, CHUNK):
                here = pl.ds(PAD + r, CHUNK)
                v = [ref[c, d + 1, here, :] for ref in (field, first, second)]
                moved = [
                    turn(edges, -(EDGE * ((r + j) // ROWS) + HALF)) for j in range(0, CHUNK, ROWS)
                ]
                v.append(
                    jnp.where(
                        outside, jnp.concatenate(moved, axis=0), third_raw[c, d, r : r + CHUNK, :]
                    )
                )
                increment[c, d, r : r + CHUNK, :] = grow[0] * v[0] + grow[1] * v[1] + grow[2] * v[2]
                residual[c, d, r : r + CHUNK, :] = (
                    keep[0] * v[0] + keep[1] * v[1] + (keep[2] * v[2] + keep[3] * v[3])
                )
            return carry

        loop(end - begin, 4, body, 0)

    copies = []

    def send(c, begin, end):
        for which, (ref, hbm) in enumerate(((increment, increment_hbm), (residual, residual_hbm))):
            part = pl.ds(begin, end - begin)
            copy = pltpu.make_async_copy(
                ref.at[c, part], hbm.at[c, part], sems.at[which, 2 * c + (begin > 0)]
            )
            copy.start()
            copies.append(copy)

    half = depth // 2
    for c in range(3):
        run(c, 0, half)
        for side in range(2):
            at = (1 + 2 * side) * across // 4
            residual[c, 0, at : at + 1, :] = (
                residual[c, 0, at : at + 1, :] - placed[2 * c + side : 2 * c + side + 1]
            )
        send(c, 0, half)
        run(c, half, depth)
        send(c, half, depth)
    for copy in copies:
        copy.wait()


def vmem_spec():
    return pl.BlockSpec(memory_space=pltpu.VMEM)


def hbm_spec():
    return pl.BlockSpec(memory_space=pltpu.HBM)


def pack_call(right_side, mass_field):
    f32 = jnp.float32
    depth, across, along = mass_field.shape
    half = depth // 2
    return pl.pallas_call(
        pack_kernel,
        out_shape=(
            pltpu.VMEM((3, depth + 2, across + 2 * PAD, along), f32),
            pltpu.VMEM((depth, across, along), f32),
            pltpu.VMEM((4, depth, ROWS, LANES), f32),
            jax.ShapeDtypeStruct((4, half, ROWS, LANES), f32),
            jax.ShapeDtypeStruct((4, half, ROWS, LANES), f32),
        ),
        in_specs=[hbm_spec()] * 2,
        out_specs=(vmem_spec(),) * 5,
        scratch_shapes=[pltpu.SemaphoreType.DMA((4,))],
        compiler_params=LIMIT,
        name="pack",
    )(right_side, mass_field)


def first_call(field, mass, spans, variants):
    f32 = jnp.float32
    depth, across, along = mass.shape
    return pl.pallas_call(
        first_kernel,
        out_shape=(
            pltpu.VMEM((3, depth, across, along), f32),
            pltpu.VMEM((2, ROWS, LANES), f32),
            pltpu.VMEM((variants, LANES), f32),
        ),
        in_specs=[vmem_spec()] * 3,
        out_specs=(vmem_spec(),) * 3,
        scratch_shapes=[pltpu.VMEM((depth + 2, across + 2 * PAD, along), f32)],
        compiler_params=LIMIT,
        cost_estimate=pl.CostEstimate(flops=20_000_000, bytes_accessed=4_000_000, transcendentals=0),
        name="first",
    )(field, mass, spans)


def basis_call(per, rows, field, mass, packed, got_a, got_b, first_raw, early, ends, count):
    f32 = jnp.float32
    depth, across, along = mass.shape
    variants = ends.shape[0]
    padded = (depth + 2, across + 2 * PAD, along)
    return pl.pallas_call(
        functools.partial(basis_kernel, per),
        out_shape=(
            pltpu.VMEM((3,) + padded, f32),
            pltpu.VMEM((3,) + padded, f32),
            pltpu.VMEM((3, depth, across, along), f32),
            pltpu.VMEM((3, depth, ROWS, LANES), f32),
            jax.ShapeDtypeStruct((count, rows, LANES), f32),
        ),
        in_specs=[vmem_spec()] * 8,
        out_specs=(vmem_spec(),) * 5,
        scratch_shapes=[
            pltpu.VMEM(padded, f32),
            pltpu.VMEM((2, 3, (depth + 2) * PITCH, LANES), f32),
            pltpu.VMEM((2, (depth + 2) * PITCH, LANES), f32),
            pltpu.VMEM((2, depth, ROWS, LANES), f32),
            pltpu.VMEM((ITERS - 1, 3, depth, ROWS, LANES), f32),
            pltpu.VMEM((2, 2, ROWS, LANES), f32),
            pltpu.VMEM((rows, LANES), f32),
            pltpu.VMEM((rows, 2 * variants * LANES), f32),
        ],
        compiler_params=LIMIT,
        name="basis",
    )(field, mass, packed, got_a, got_b, first_raw, early, ends)


def combine_call(per, gathered, field, first, second, third_raw, fix, ends, stick, load, prior):
    f32 = jnp.float32
    shape = third_raw.shape
    bearings = load.shape[1]
    return pl.pallas_call(
        functools.partial(combine_kernel, per),
        out_shape=(
            jax.ShapeDtypeStruct(shape, f32),
            jax.ShapeDtypeStruct(shape, f32),
            jax.ShapeDtypeStruct((2, bearings), f32),
        ),
        in_specs=[vmem_spec()] * 10,
        out_specs=(hbm_spec(), hbm_spec(), vmem_spec()),
        scratch_shapes=[
            pltpu.VMEM(shape, f32),
            pltpu.VMEM(shape, f32),
            pltpu.VMEM((ROWS, max(bearings, LANES)), f32),
            pltpu.SemaphoreType.DMA((2, 6)),
        ],
        compiler_params=LIMIT,
        name="combine",
    )(gathered, field, first, second, third_raw, fix, ends, stick, load, prior)


def shards(count, right_side, mass_field, span_lengths, stick_flags, normal_load, prior_friction):
    piers = span_lengths.shape[0]
    bearings = 2 * piers
    per = LANES // bearings if bearings <= LANES else 1
    variants = per if bearings <= LANES else bearings // LANES
    pieces = 1 if per > 1 else variants
    rows = -(-(-(-3 * ITERS * pieces // per) + 3) // ROWS) * ROWS

    field, mass, packed, message_a, message_b = pack_call(right_side, mass_field)
    pairs_a = [p for i in range(0, count - 1, 2) for p in ((i, i + 1), (i + 1, i))]
    pairs_b = [p for i in range(1, count - 1, 2) for p in ((i, i + 1), (i + 1, i))]
    got_b = lax.ppermute(message_b, AXES, pairs_b)
    got_a = lax.ppermute(message_a, AXES, pairs_a)
    first_raw, early, ends = first_call(field, mass, span_lengths.reshape(1, piers), variants)
    first, second, third_raw, fix, payload = basis_call(
        per, rows, field, mass, packed, got_a, got_b, first_raw, early, ends, count
    )
    gathered = lax.all_to_all(payload, AXES, 0, 0)
    return combine_call(
        per, gathered, field, first, second, third_raw, fix, ends,
        stick_flags.reshape(1, bearings), normal_load.reshape(1, bearings), prior_friction,
    )


def solution(mesh):
    count = mesh.shape["len"] * mesh.shape["xs"]
    along = P(None, None, None, AXES)
    in_specs = (along, P(None, None, AXES), P(), P(), P(), P())
    return jax.shard_map(
        functools.partial(shards, count), mesh=mesh,
        in_specs=in_specs, out_specs=(along, along, P()), check_vma=False,
    )
```

```python
import functools

import jax
import jax.numpy as jnp
from jax import lax
from jax.experimental import pallas as pl
from jax.experimental.pallas import tpu as pltpu
from jax.sharding import PartitionSpec as P

ITERS = 3
SHIFT = 4.0
BULK = 1.5
ELASTIC = 8.0
RADIUS = 4.0
VERTICAL = 5.0
STATIC = 0.6
KINETIC = 0.45

AXES = ("len", "xs")
LANES = 128
ROWS = 8
PAD = 8
EDGE = 16
HALF = EDGE // 2
BLOCKS = LANES // EDGE
PITCH = 3 * ROWS
CHUNK = 16
PIECE = 4
HIGH = lax.Precision.HIGHEST
LIMIT = pltpu.CompilerParams(vmem_limit_bytes=32 * 1024 * 1024)


def turn(x, amount):
    return pltpu.roll(x, amount % LANES, x.ndim - 1)


def lane_iota(shape):
    return lax.broadcasted_iota(jnp.int32, shape, len(shape) - 1)


def loop(count, step, body, init):
    def several(i, carry):
        for j in range(step):
            carry = body(i * step + j, carry)
        return carry

    return lax.fori_loop(0, count // step, several, init)


def device_index():
    return lax.axis_index(AXES[0]) * lax.axis_size(AXES[1]) + lax.axis_index(AXES[1])


def clear_padding(ref, lead, depth, across):
    for slab in (0, depth + 1):
        ref[lead + (slab,)] = jnp.zeros((across + 2 * PAD, LANES), jnp.float32)
    blank = jnp.zeros((PAD, LANES), jnp.float32)
    for d in range(1, depth + 1):
        ref[lead + (d, slice(0, PAD))] = blank
        ref[lead + (d, slice(PAD + across, None))] = blank


def pack_kernel(right_hbm, mass_hbm, field, mass, packed, message_a, message_b, sems):
    depth, across = mass.shape[0], mass.shape[1]
    copies = [
        pltpu.make_async_copy(
            right_hbm.at[c], field.at[c, pl.ds(1, depth), pl.ds(PAD, across)], sems.at[c]
        )
        for c in range(3)
    ]
    copies.append(pltpu.make_async_copy(mass_hbm, mass, sems.at[3]))
    for copy in copies:
        copy.start()
    for c in range(3):
        clear_padding(field, (c,), depth, across)
    is_even = device_index() % 2 == 0
    lane = lane_iota((ROWS, LANES))
    block_of = lane // EDGE
    first_half = lane % EDGE < HALF
    for c in range(4):
        copies[c].wait()
        edges = []
        for d in range(depth):
            edge = None
            for b in range(across // ROWS):
                row = pl.ds(b * ROWS + (PAD if c < 3 else 0), ROWS)
                if c < 3:
                    tile = field[c, d + 1, row, :]
                else:
                    tile = mass[d, row, :] + (6.0 - SHIFT)
                    mass[d, row, :] = tile
                moved = turn(tile, EDGE * b + HALF)
                edge = moved if edge is None else jnp.where(block_of == b, moved, edge)
            packed[c, d] = edge
            edges.append(edge)
        for d in range(depth // 2):
            low, high = edges[d], edges[d + depth // 2]
            rightward = jnp.where(first_half, low, turn(high, HALF))
            leftward = jnp.where(first_half, turn(low, -HALF), high)
            message_a[c, d] = jnp.where(is_even, rightward, leftward)
            message_b[c, d] = jnp.where(is_even, leftward, rightward)


def folded(x):
    return sum(x[i : i + ROWS] for i in range(0, x.shape[0], ROWS))


def cyclic_step(source, mass, div, store, step):
    depth, across = mass.shape[0], mass.shape[1]
    chunks = range(0, across, CHUNK)

    def divergence(d, carry):
        for r in chunks:
            here, up, down = (pl.ds(PAD + r + by, CHUNK) for by in (0, 1, -1))
            x = source[0, d + 1, here, :]
            w = turn(x, -1) - turn(x, 1)
            w = w + (source[1, d + 1, up, :] - source[1, d + 1, down, :])
            w = w + (source[2, d + 2, here, :] - source[2, d, here, :])
            div[d + 1, here, :] = w * (0.25 * BULK)
        return carry

    loop(depth, step, divergence, 0)

    def image(d, carry):
        norm, cross = carry
        for r in chunks:
            here, up, down = (pl.ds(PAD + r + by, CHUNK) for by in (0, 1, -1))
            diag = mass[d, r : r + CHUNK, :]
            w = div[d + 1, here, :]
            norms, crosses = [], []
            for c in range(3):
                x = source[c, d + 1, here, :]
                if c == 0:
                    total = turn(x + w, -1) + turn(x - w, 1)
                else:
                    total = turn(x, -1) + turn(x, 1)
                if c == 1:
                    total = total + (div[d + 1, up, :] - div[d + 1, down, :])
                if c == 2:
                    total = total + (div[d + 2, here, :] - div[d, here, :])
                total = total + (source[c, d, here, :] + source[c, d + 2, here, :])
                total = total + (source[c, d + 1, up, :] + source[c, d + 1, down, :])
                out = diag * x - total
                store(c, d, r, out)
                norms.append(x * x)
                crosses.append(x * out)
            norm = norm + folded(norms[0] + norms[1] + norms[2])
            cross = cross + folded(crosses[0] + crosses[1] + crosses[2])
        return norm, cross

    return loop(depth, step, image, (jnp.zeros((ROWS, LANES), jnp.float32),) * 2)


def interior(value, margin):
    lane = lane_iota(value.shape)
    return jnp.where((lane >= margin) & (lane < LANES - margin), value, 0.0)


def cyclic_kernel(field, mass, spans, first, second, moments, ends, div):
    depth, across = mass.shape[0], mass.shape[1]
    clear_padding(div, (), depth, across)
    for c in range(3):
        clear_padding(first, (c,), depth, across)

    def store_first(c, d, r, out):
        first[c, d + 1, pl.ds(PAD + r, CHUNK), :] = out

    def store_second(c, d, r, out):
        second[c, d, r : r + CHUNK, :] = out

    norm, cross = cyclic_step(field, mass, div, store_first, 4)
    moments[0] = norm
    moments[1] = interior(cross, 2)
    norm, cross = cyclic_step(first, mass, div, store_second, 4)
    moments[2] = interior(norm, 2)
    moments[3] = interior(cross, 4)
    piers = spans.shape[1]
    bearings = 2 * piers
    lane = lane_iota((piers, LANES))
    pier = lax.broadcasted_iota(jnp.int32, (piers, LANES), 0)
    lengths = jnp.broadcast_to(spans[...].astype(jnp.float32), (ROWS, piers))
    for z in range(ends.shape[0]):
        bearing = lane - z * bearings if bearings <= LANES else lane + z * LANES
        upto = jnp.where(pier * 2 <= bearing, 1.0, 0.0)
        total = jnp.dot(lengths, upto, precision=HIGH, preferred_element_type=jnp.float32)
        inside = (bearing[0:1] >= 0) & (bearing[0:1] < bearings)
        ends[z : z + 1, :] = jnp.where(inside, total[0:1] - 1.0, -1e9)


def mended(value, edges, row, margin):
    moved = [
        turn(edges, -(EDGE * ((row + i) // ROWS) + HALF)) for i in range(0, value.shape[0], ROWS)
    ]
    spot = lane_iota(value.shape)
    return jnp.where(
        (spot < margin) | (spot >= LANES - margin),
        moved[0] if len(moved) == 1 else jnp.concatenate(moved, axis=0),
        value,
    )


def basis_kernel(
    per, field, mass, packed, got_a, got_b, first, second_raw, early, ends,
    second, third, fix_first, fix_third, payload,
    div, edge, edge_div, edge_diag, fix_second, sums, picked,
):
    depth, across = mass.shape[0], mass.shape[1]
    index = device_index()
    count = lax.axis_size(AXES[0]) * lax.axis_size(AXES[1])
    is_even = index % 2 == 0
    lane = lane_iota((ROWS, LANES))
    first_half = lane % EDGE < HALF
    ones = jnp.ones((ROWS, LANES), jnp.float32)
    keep = (
        jnp.where(first_half & (index == 0), 0.0, ones),
        jnp.where(jnp.logical_not(first_half) & (index == count - 1), 0.0, ones),
    )
    both = range(2)
    comps = range(3)
    half = depth // 2
    blank = jnp.zeros((ROWS, LANES), jnp.float32)

    def row_of(d):
        return (d + 1) * PITCH + ROWS

    for c in range(4):
        for d in range(half):
            a, b = got_a[c, d], got_b[c, d]
            from_left = jnp.where(is_even, b, a)
            from_right = jnp.where(is_even, a, b)
            low, high = packed[c, d], packed[c, d + half]
            for at, left, right in (
                (
                    d,
                    jnp.where(first_half, from_left, low),
                    jnp.where(first_half, low, turn(from_right, HALF)),
                ),
                (
                    d + half,
                    jnp.where(first_half, turn(from_left, -HALF), high),
                    jnp.where(first_half, high, from_right),
                ),
            ):
                if c < 3:
                    edge[0, c, pl.ds(row_of(at), ROWS), :] = left
                    edge[1, c, pl.ds(row_of(at), ROWS), :] = right
                else:
                    edge_diag[0, at] = left
                    edge_diag[1, at] = right
    for s in both:
        for c in comps:
            edge[s, c, pl.ds(ROWS, ROWS), :] = blank
            edge[s, c, pl.ds(row_of(depth), ROWS), :] = blank
        edge_div[s, pl.ds(ROWS, ROWS), :] = blank
        edge_div[s, pl.ds(row_of(depth), ROWS), :] = blank

    def join_blocks(ref, lead):
        for d in (0, half):
            base = row_of(d)
            last = ref[lead + (pl.ds(base + ROWS - 1, half, stride=PITCH), slice(None))]
            ahead = ref[lead + (pl.ds(base, half, stride=PITCH), slice(None))]
            spot = lane_iota((half, LANES))
            ref[lead + (pl.ds(base - 1, half, stride=PITCH), slice(None))] = jnp.where(
                spot >= EDGE, turn(last, EDGE), 0.0
            )
            ref[lead + (pl.ds(base + ROWS, half, stride=PITCH), slice(None))] = jnp.where(
                spot < LANES - EDGE, turn(ahead, -EDGE), 0.0
            )

    def at(s, c, d, by=0):
        return edge[s, c, pl.ds(row_of(d) + by, ROWS), :]

    def div_at(s, d, by=0):
        return edge_div[s, pl.ds(row_of(d) + by, ROWS), :]

    def middle(value, margin):
        spot = lane % EDGE
        return jnp.where((spot >= HALF - margin) & (spot < HALF + margin), value, 0.0)

    fixes = (packed, fix_first, fix_second, fix_third)

    def edge_step(level):
        for s in both:
            for c in comps:
                join_blocks(edge, (s, c))
        for s in both:
            for d in range(depth):
                x = at(s, 0, d)
                w = turn(x, -1) - turn(x, 1)
                w = w + (at(s, 1, d, 1) - at(s, 1, d, -1))
                w = w + (at(s, 2, d + 1) - at(s, 2, d - 1))
                edge_div[s, pl.ds(row_of(d), ROWS), :] = w * ((0.25 * BULK) * keep[s])
            join_blocks(edge_div, (s,))
        norm, cross = blank, blank
        for c in comps:
            images = []
            for d in range(depth):
                pair = []
                for s in both:
                    x = at(s, c, d)
                    if c == 0:
                        w = div_at(s, d)
                        total = turn(x + w, -1) + turn(x - w, 1)
                    else:
                        total = turn(x, -1) + turn(x, 1)
                    if c == 1:
                        total = total + (div_at(s, d, 1) - div_at(s, d, -1))
                    if c == 2:
                        total = total + (div_at(s, d + 1) - div_at(s, d - 1))
                    total = total + (at(s, c, d - 1) + at(s, c, d + 1))
                    total = total + (at(s, c, d, 1) + at(s, c, d, -1))
                    pair.append((edge_diag[s, d] * x - total) * keep[s])
                images.append(pair)
                old = fixes[level][c, d]
                new = jnp.where(first_half, pair[1], pair[0])
                fixes[level + 1][c, d] = new
                norm = norm + old * old
                cross = cross + old * new
            for d in range(depth):
                for s in both:
                    edge[s, c, pl.ds(row_of(d), ROWS), :] = images[d][s]
        return norm, cross

    edge_sums = [edge_step(level) for level in range(ITERS)]

    clear_padding(div, (), depth, across)
    for c in comps:
        clear_padding(second, (c,), depth, across)

    def mend(d, carry):
        for c in comps:
            edges = fix_second[c, d]
            for r in range(0, across, CHUNK):
                second[c, d + 1, pl.ds(PAD + r, CHUNK), :] = mended(
                    second_raw[c, d, r : r + CHUNK, :], edges, r, 4
                )
        return carry

    loop(depth, 4, mend, 0)

    def store_third(c, d, r, out):
        third[c, d, r : r + CHUNK, :] = out

    norm, cross = cyclic_step(second, mass, div, store_third, 4)
    parts = [
        early[0],
        early[1] + middle(edge_sums[0][1], 2),
        early[2] + middle(edge_sums[1][0], 2),
        early[3] + middle(edge_sums[1][1], 4),
        norm,
        interior(cross, 2) + middle(edge_sums[2][1], 2),
    ]

    variants = ends.shape[0]
    pieces = 1 if per > 1 else variants
    blocks = 3 * ITERS * pieces
    bearing_rows = -(-blocks // per)
    picked[...] = jnp.zeros(picked.shape, jnp.float32)
    for block in range(blocks):
        value, piece = block // pieces, block % pieces
        row, z = block // per, (block % per if per > 1 else piece)
        ref, c = (field, first, second)[value // 3], value % 3
        for side in both:
            place = PAD + (1 + 2 * side) * across // 4
            column = (2 * z + side) * LANES
            here = ref[c, 1, place : place + 1, :]
            if ref is first:
                r = place - PAD
                edges = fix_first[c, 0, r % ROWS : r % ROWS + 1, :]
                here = mended(here, edges, r, 2)
            picked[row : row + 1, column : column + LANES] = here
    start = (index * LANES).astype(jnp.float32)
    along = lax.broadcasted_iota(jnp.int32, (LANES, LANES), 0).astype(jnp.float32) + start
    parity = lane_iota((LANES, LANES)) % 2
    total = jnp.zeros((picked.shape[0], LANES), jnp.float32)
    for z in range(variants):
        site = jnp.broadcast_to(ends[z : z + 1, :], (LANES, LANES)) == along
        for side in both:
            column = (2 * z + side) * LANES
            hit = jnp.where(site & (parity == side), 1.0, 0.0)
            total = total + jnp.dot(
                picked[:, column : column + LANES], hit,
                precision=HIGH, preferred_element_type=jnp.float32,
            )
    sums[...] = jnp.zeros(sums.shape, jnp.float32)
    sums[0:bearing_rows, :] = total[0:bearing_rows]
    low = lane_iota((1, LANES)) < LANES // 2
    for pair in range(3):
        halves = []
        for part in parts[2 * pair : 2 * pair + 2]:
            flat = jnp.sum(part, axis=0, keepdims=True)
            halves.append(flat + turn(flat, LANES // 2))
        sums[bearing_rows + pair : bearing_rows + pair + 1, :] = jnp.where(low, *halves)
    out = sums[...]
    for device in range(payload.shape[0]):
        payload[device] = out


def coefficients(moment):
    def dot(a, b):
        total = None
        for i, left in enumerate(a):
            for j, right in enumerate(b):
                term = left * right * moment[i + j]
                total = term if total is None else total + term
        return total

    one = jnp.ones_like(moment[0])
    solved, direction, increment = [one], [one], []
    norm = moment[0]
    for iteration in range(ITERS):
        image = [SHIFT * p for p in direction] + [jnp.zeros_like(one)]
        for i, p in enumerate(direction):
            image[i + 1] = image[i + 1] + p
        alpha = norm / dot(direction, image)
        increment = [
            alpha * p + (increment[i] if i < len(increment) else 0.0) for i, p in enumerate(direction)
        ]
        solved = [
            (solved[i] if i < len(solved) else 0.0) - alpha * q for i, q in enumerate(image)
        ]
        if iteration + 1 < ITERS:
            after = dot(solved, solved)
            ratio = after / norm
            direction = [
                s + (ratio * direction[i] if i < len(direction) else 0.0)
                for i, s in enumerate(solved)
            ]
            norm = after
    return increment, solved


def combine_kernel(
    per, gathered, field, first, second, third, fix_first, fix_third, ends, stick, load, prior,
    increment_hbm, residual_hbm, friction,
    increment, residual, forces, sems,
):
    depth, across = third.shape[1], third.shape[2]
    start = (device_index() * LANES).astype(jnp.float32)
    bearings = load.shape[1]
    variants = ends.shape[0]
    pieces = 1 if per > 1 else variants
    width = min(bearings, LANES)
    bearing_rows = -(-9 * pieces // per)
    parts = [gathered[i] for i in range(gathered.shape[0])]
    while len(parts) > 1:
        parts = [sum(parts[i : i + 2]) for i in range(0, len(parts), 2)]
    total = parts[0]
    low = lane_iota((1, LANES)) < LANES // 2
    moments = []
    for n in range(6):
        row = total[bearing_rows + n // 2 : bearing_rows + n // 2 + 1]
        row = jnp.where(low == (n % 2 == 0), row, 0.0)
        moments.append(jnp.sum(row, axis=1, keepdims=True))
    grow, keep = coefficients(moments)

    forces[...] = jnp.zeros(forces.shape, jnp.float32)
    lane = lane_iota((1, width))
    for piece in range(pieces):
        span = slice(piece * LANES, piece * LANES + width)
        readout = []
        for c in range(3):
            value = None
            for k in range(ITERS):
                block = (3 * k + c) * pieces + piece
                row = total[block // per : block // per + 1]
                if per > 1 and block % per:
                    row = turn(row, LANES - (block % per) * bearings)
                term = grow[k] * row[:, :width]
                value = term if value is None else value + term
            readout.append(value)
        weight = load[:, span]
        radius = jnp.where(stick[:, span] == 1, STATIC, KINETIC) * weight
        trial = [prior[c : c + 1, span] + ELASTIC * readout[c] for c in range(2)]
        magnitude = jnp.sqrt(trial[0] * trial[0] + trial[1] * trial[1])
        scale = radius / jnp.maximum(magnitude, radius)
        held = [t * scale for t in trial]
        for c in range(2):
            friction[c : c + 1, span] = held[c]
        force = [held[c] + weight / RADIUS * readout[c] for c in range(2)] + [VERTICAL * readout[2]]
        for c in range(3):
            for side in range(2):
                forces[2 * c + side : 2 * c + side + 1, span] = jnp.where(
                    lane % 2 == side, force[c], 0.0
                )
    along = lax.broadcasted_iota(jnp.int32, (LANES, LANES), 0).astype(jnp.float32) + start
    placed = jnp.zeros((8, LANES), jnp.float32)
    for piece in range(pieces):
        site = jnp.broadcast_to(ends[piece : piece + 1, :], (LANES, LANES)) == along
        placed = placed + lax.dot_general(
            forces[:, piece * LANES : (piece + 1) * LANES], jnp.where(site, 1.0, 0.0),
            (((1,), (1,)), ((), ())), precision=HIGH, preferred_element_type=jnp.float32,
        )

    grow = [jnp.broadcast_to(g, (CHUNK, LANES)) for g in grow]
    keep = [jnp.broadcast_to(g, (CHUNK, LANES)) for g in keep]

    def run(c, begin, end):
        for d in range(begin, end):
            edges = fix_first[c, d], fix_third[c, d]
            for r in range(0, across, CHUNK):
                here = pl.ds(PAD + r, CHUNK)
                v = [ref[c, d + 1, here, :] for ref in (field, first, second)]
                v.append(third[c, d, r : r + CHUNK, :])
                v[1] = mended(v[1], edges[0], r, 2)
                v[3] = mended(v[3], edges[1], r, 2)
                increment[c, d, r : r + CHUNK, :] = grow[0] * v[0] + grow[1] * v[1] + grow[2] * v[2]
                residual[c, d, r : r + CHUNK, :] = (
                    keep[0] * v[0] + keep[1] * v[1] + (keep[2] * v[2] + keep[3] * v[3])
                )

    def copy(which, c, begin):
        ref, hbm = ((increment, increment_hbm), (residual, residual_hbm))[which]
        part = pl.ds(begin, PIECE)
        return pltpu.make_async_copy(
            ref.at[c, part], hbm.at[c, part], sems.at[which, c, begin // PIECE]
        )

    starts = range(0, depth, PIECE)
    for c in range(3):
        for begin in starts:
            run(c, begin, begin + PIECE)
            if begin == 0:
                for side in range(2):
                    at = (1 + 2 * side) * across // 4
                    residual[c, 0, at : at + 1, :] = (
                        residual[c, 0, at : at + 1, :] - placed[2 * c + side : 2 * c + side + 1]
                    )
            for which in range(2):
                copy(which, c, begin).start()
    for c in range(3):
        for begin in starts:
            for which in range(2):
                copy(which, c, begin).wait()


def vmem_spec():
    return pl.BlockSpec(memory_space=pltpu.VMEM)


def hbm_spec():
    return pl.BlockSpec(memory_space=pltpu.HBM)


def pack_call(right_side, mass_field):
    f32 = jnp.float32
    depth, across, along = mass_field.shape
    half = depth // 2
    return pl.pallas_call(
        pack_kernel,
        out_shape=(
            pltpu.VMEM((3, depth + 2, across + 2 * PAD, along), f32),
            pltpu.VMEM((depth, across, along), f32),
            pltpu.VMEM((4, depth, ROWS, LANES), f32),
            jax.ShapeDtypeStruct((4, half, ROWS, LANES), f32),
            jax.ShapeDtypeStruct((4, half, ROWS, LANES), f32),
        ),
        in_specs=[hbm_spec()] * 2,
        out_specs=(vmem_spec(),) * 5,
        scratch_shapes=[pltpu.SemaphoreType.DMA((4,))],
        compiler_params=LIMIT,
        name="pack",
    )(
        pltpu.with_memory_space_constraint(right_side, pltpu.HBM),
        pltpu.with_memory_space_constraint(mass_field, pltpu.HBM),
    )


def cyclic_call(field, mass, spans, variants):
    f32 = jnp.float32
    depth, across, along = mass.shape
    padded = (depth + 2, across + 2 * PAD, along)
    return pl.pallas_call(
        cyclic_kernel,
        out_shape=(
            pltpu.VMEM((3,) + padded, f32),
            pltpu.VMEM((3, depth, across, along), f32),
            pltpu.VMEM((4, ROWS, LANES), f32),
            pltpu.VMEM((variants, LANES), f32),
        ),
        in_specs=[vmem_spec()] * 3,
        out_specs=(vmem_spec(),) * 4,
        scratch_shapes=[pltpu.VMEM(padded, f32)],
        compiler_params=LIMIT,
        cost_estimate=pl.CostEstimate(flops=40_000_000, bytes_accessed=8_000_000, transcendentals=0),
        name="cyclic",
    )(field, mass, spans)


def basis_call(per, rows, field, mass, packed, got_a, got_b, first, second_raw, early, ends, count):
    f32 = jnp.float32
    depth, across, along = mass.shape
    variants = ends.shape[0]
    padded = (depth + 2, across + 2 * PAD, along)
    edges = (3, depth, ROWS, LANES)
    return pl.pallas_call(
        functools.partial(basis_kernel, per),
        out_shape=(
            pltpu.VMEM((3,) + padded, f32),
            pltpu.VMEM((3, depth, across, along), f32),
            pltpu.VMEM(edges, f32),
            pltpu.VMEM(edges, f32),
            jax.ShapeDtypeStruct((count, rows, LANES), f32),
        ),
        in_specs=[vmem_spec()] * 9,
        out_specs=(vmem_spec(),) * 5,
        scratch_shapes=[
            pltpu.VMEM(padded, f32),
            pltpu.VMEM((2, 3, (depth + 2) * PITCH, LANES), f32),
            pltpu.VMEM((2, (depth + 2) * PITCH, LANES), f32),
            pltpu.VMEM((2, depth, ROWS, LANES), f32),
            pltpu.VMEM(edges, f32),
            pltpu.VMEM((rows, LANES), f32),
            pltpu.VMEM((rows, 2 * variants * LANES), f32),
        ],
        compiler_params=LIMIT,
        name="basis",
    )(field, mass, packed, got_a, got_b, first, second_raw, early, ends)


def combine_call(per, gathered, field, first, second, third, fixes, ends, stick, load, prior):
    f32 = jnp.float32
    shape = third.shape
    bearings = load.shape[1]
    return pl.pallas_call(
        functools.partial(combine_kernel, per),
        out_shape=(
            jax.ShapeDtypeStruct(shape, f32),
            jax.ShapeDtypeStruct(shape, f32),
            jax.ShapeDtypeStruct((2, bearings), f32),
        ),
        in_specs=[vmem_spec()] * 11,
        out_specs=(hbm_spec(), hbm_spec(), vmem_spec()),
        scratch_shapes=[
            pltpu.VMEM(shape, f32),
            pltpu.VMEM(shape, f32),
            pltpu.VMEM((ROWS, max(bearings, LANES)), f32),
            pltpu.SemaphoreType.DMA((2, 3, shape[1] // PIECE)),
        ],
        compiler_params=LIMIT,
        name="combine",
    )(gathered, field, first, second, third, *fixes, ends, stick, load, prior)


def shards(count, right_side, mass_field, span_lengths, stick_flags, normal_load, prior_friction):
    piers = span_lengths.shape[0]
    bearings = 2 * piers
    per = LANES // bearings if bearings <= LANES else 1
    variants = per if bearings <= LANES else bearings // LANES
    pieces = 1 if per > 1 else variants
    rows = -(-(-(-3 * ITERS * pieces // per) + 3) // ROWS) * ROWS

    field, mass, packed, message_a, message_b = pack_call(right_side, mass_field)
    pairs_a = [p for i in range(0, count - 1, 2) for p in ((i, i + 1), (i + 1, i))]
    pairs_b = [p for i in range(1, count - 1, 2) for p in ((i, i + 1), (i + 1, i))]
    got_b = lax.ppermute(message_b, AXES, pairs_b)
    got_a = lax.ppermute(message_a, AXES, pairs_a)
    first, second_raw, early, ends = cyclic_call(
        field, mass, span_lengths.reshape(1, piers), variants
    )
    second, third, fix_first, fix_third, payload = basis_call(
        per, rows, field, mass, packed, got_a, got_b, first, second_raw, early, ends, count
    )
    gathered = lax.all_to_all(payload, AXES, 0, 0)
    return combine_call(
        per, gathered, field, first, second, third, (fix_first, fix_third), ends,
        stick_flags.reshape(1, bearings), normal_load.reshape(1, bearings), prior_friction,
    )


def solution(mesh):
    count = mesh.shape["len"] * mesh.shape["xs"]
    along = P(None, None, None, AXES)
    in_specs = (along, P(None, None, AXES), P(), P(), P(), P())
    return jax.shard_map(
        functools.partial(shards, count), mesh=mesh,
        in_specs=in_specs, out_specs=(along, along, P()), check_vma=False,
    )
```

```python
import functools

import jax
import jax.numpy as jnp
from jax import lax
from jax.experimental import pallas as pl
from jax.experimental.pallas import tpu as pltpu
from jax.sharding import PartitionSpec as P

ITERS = 3
SHIFT = 4.0
BULK = 1.5
ELASTIC = 8.0
RADIUS = 4.0
VERTICAL = 5.0
STATIC = 0.6
KINETIC = 0.45

AXES = ("len", "xs")
LANES = 128
ROWS = 8
PAD = 8
EDGE = 16
HALF = EDGE // 2
BLOCKS = LANES // EDGE
PITCH = 3 * ROWS
CHUNK = 16
PIECE = 16
HIGH = lax.Precision.HIGHEST
LIMIT = pltpu.CompilerParams(vmem_limit_bytes=32 * 1024 * 1024)


def turn(x, amount):
    return pltpu.roll(x, amount % LANES, x.ndim - 1)


def lane_iota(shape):
    return lax.broadcasted_iota(jnp.int32, shape, len(shape) - 1)


def loop(count, step, body, init):
    def several(i, carry):
        for j in range(step):
            carry = body(i * step + j, carry)
        return carry

    return lax.fori_loop(0, count // step, several, init)


def device_index():
    return lax.axis_index(AXES[0]) * lax.axis_size(AXES[1]) + lax.axis_index(AXES[1])


def clear_padding(ref, lead, depth, across):
    for slab in (0, depth + 1):
        ref[lead + (slab,)] = jnp.zeros((across + 2 * PAD, LANES), jnp.float32)
    blank = jnp.zeros((PAD, LANES), jnp.float32)
    for d in range(1, depth + 1):
        ref[lead + (d, slice(0, PAD))] = blank
        ref[lead + (d, slice(PAD + across, None))] = blank


def pack_kernel(right_hbm, mass_hbm, field, mass, packed, message_a, message_b, sems):
    depth, across = mass.shape[0], mass.shape[1]
    copies = [
        pltpu.make_async_copy(
            right_hbm.at[c], field.at[c, pl.ds(1, depth), pl.ds(PAD, across)], sems.at[c]
        )
        for c in range(3)
    ]
    copies.append(pltpu.make_async_copy(mass_hbm, mass, sems.at[3]))
    for copy in copies:
        copy.start()
    for c in range(3):
        clear_padding(field, (c,), depth, across)
    is_even = device_index() % 2 == 0
    lane = lane_iota((ROWS, LANES))
    block_of = lane // EDGE
    first_half = lane % EDGE < HALF
    for c in range(4):
        copies[c].wait()
        edges = []
        for d in range(depth):
            edge = None
            for b in range(across // ROWS):
                row = pl.ds(b * ROWS + (PAD if c < 3 else 0), ROWS)
                if c < 3:
                    tile = field[c, d + 1, row, :]
                else:
                    tile = mass[d, row, :] + (6.0 - SHIFT)
                    mass[d, row, :] = tile
                moved = turn(tile, EDGE * b + HALF)
                edge = moved if edge is None else jnp.where(block_of == b, moved, edge)
            packed[c, d] = edge
            edges.append(edge)
        for d in range(depth // 2):
            low, high = edges[d], edges[d + depth // 2]
            rightward = jnp.where(first_half, low, turn(high, HALF))
            leftward = jnp.where(first_half, turn(low, -HALF), high)
            message_a[c, d] = jnp.where(is_even, rightward, leftward)
            message_b[c, d] = jnp.where(is_even, leftward, rightward)


def folded(x):
    return sum(x[i : i + ROWS] for i in range(0, x.shape[0], ROWS))


def cyclic_step(source, mass, div, store, step):
    depth, across = mass.shape[0], mass.shape[1]
    chunks = range(0, across, CHUNK)

    def divergence(d, carry):
        for r in chunks:
            here, up, down = (pl.ds(PAD + r + by, CHUNK) for by in (0, 1, -1))
            x = source[0, d + 1, here, :]
            w = turn(x, -1) - turn(x, 1)
            w = w + (source[1, d + 1, up, :] - source[1, d + 1, down, :])
            w = w + (source[2, d + 2, here, :] - source[2, d, here, :])
            div[d + 1, here, :] = w * (0.25 * BULK)
        return carry

    loop(depth, step, divergence, 0)

    def image(d, carry):
        norm, cross = carry
        for r in chunks:
            here, up, down = (pl.ds(PAD + r + by, CHUNK) for by in (0, 1, -1))
            diag = mass[d, r : r + CHUNK, :]
            w = div[d + 1, here, :]
            norms, crosses = [], []
            for c in range(3):
                x = source[c, d + 1, here, :]
                if c == 0:
                    total = turn(x + w, -1) + turn(x - w, 1)
                else:
                    total = turn(x, -1) + turn(x, 1)
                if c == 1:
                    total = total + (div[d + 1, up, :] - div[d + 1, down, :])
                if c == 2:
                    total = total + (div[d + 2, here, :] - div[d, here, :])
                total = total + (source[c, d, here, :] + source[c, d + 2, here, :])
                total = total + (source[c, d + 1, up, :] + source[c, d + 1, down, :])
                out = diag * x - total
                store(c, d, r, out)
                norms.append(x * x)
                crosses.append(x * out)
            norm = norm + folded(norms[0] + norms[1] + norms[2])
            cross = cross + folded(crosses[0] + crosses[1] + crosses[2])
        return norm, cross

    return loop(depth, step, image, (jnp.zeros((ROWS, LANES), jnp.float32),) * 2)


def interior(value, margin):
    lane = lane_iota(value.shape)
    return jnp.where((lane >= margin) & (lane < LANES - margin), value, 0.0)


def cyclic_kernel(field, mass, spans, first, second, moments, ends, div):
    depth, across = mass.shape[0], mass.shape[1]
    clear_padding(div, (), depth, across)
    for c in range(3):
        clear_padding(first, (c,), depth, across)

    def store_first(c, d, r, out):
        first[c, d + 1, pl.ds(PAD + r, CHUNK), :] = out

    def store_second(c, d, r, out):
        second[c, d, r : r + CHUNK, :] = out

    norm, cross = cyclic_step(field, mass, div, store_first, 4)
    moments[0] = norm
    moments[1] = interior(cross, 2)
    norm, cross = cyclic_step(first, mass, div, store_second, 4)
    moments[2] = interior(norm, 2)
    moments[3] = interior(cross, 4)
    piers = spans.shape[1]
    bearings = 2 * piers
    lane = lane_iota((piers, LANES))
    pier = lax.broadcasted_iota(jnp.int32, (piers, LANES), 0)
    lengths = jnp.broadcast_to(spans[...].astype(jnp.float32), (ROWS, piers))
    for z in range(ends.shape[0]):
        bearing = lane - z * bearings if bearings <= LANES else lane + z * LANES
        upto = jnp.where(pier * 2 <= bearing, 1.0, 0.0)
        total = jnp.dot(lengths, upto, precision=HIGH, preferred_element_type=jnp.float32)
        inside = (bearing[0:1] >= 0) & (bearing[0:1] < bearings)
        ends[z : z + 1, :] = jnp.where(inside, total[0:1] - 1.0, -1e9)


def mended(value, edges, row, margin):
    moved = [
        turn(edges, -(EDGE * ((row + i) // ROWS) + HALF)) for i in range(0, value.shape[0], ROWS)
    ]
    spot = lane_iota(value.shape)
    return jnp.where(
        (spot < margin) | (spot >= LANES - margin),
        moved[0] if len(moved) == 1 else jnp.concatenate(moved, axis=0),
        value,
    )


def basis_kernel(
    per, field, mass, packed, got_a, got_b, first, second_raw, early, ends,
    second, third, fix_first, fix_third, payload,
    div, edge, edge_div, edge_diag, fix_second, sums, picked,
):
    depth, across = mass.shape[0], mass.shape[1]
    index = device_index()
    count = lax.axis_size(AXES[0]) * lax.axis_size(AXES[1])
    is_even = index % 2 == 0
    lane = lane_iota((ROWS, LANES))
    first_half = lane % EDGE < HALF
    ones = jnp.ones((ROWS, LANES), jnp.float32)
    keep = (
        jnp.where(first_half & (index == 0), 0.0, ones),
        jnp.where(jnp.logical_not(first_half) & (index == count - 1), 0.0, ones),
    )
    both = range(2)
    comps = range(3)
    half = depth // 2
    blank = jnp.zeros((ROWS, LANES), jnp.float32)

    def row_of(d):
        return (d + 1) * PITCH + ROWS

    for c in range(4):
        for d in range(half):
            a, b = got_a[c, d], got_b[c, d]
            from_left = jnp.where(is_even, b, a)
            from_right = jnp.where(is_even, a, b)
            low, high = packed[c, d], packed[c, d + half]
            for at, left, right in (
                (
                    d,
                    jnp.where(first_half, from_left, low),
                    jnp.where(first_half, low, turn(from_right, HALF)),
                ),
                (
                    d + half,
                    jnp.where(first_half, turn(from_left, -HALF), high),
                    jnp.where(first_half, high, from_right),
                ),
            ):
                if c < 3:
                    edge[0, c, pl.ds(row_of(at), ROWS), :] = left
                    edge[1, c, pl.ds(row_of(at), ROWS), :] = right
                else:
                    edge_diag[0, at] = left
                    edge_diag[1, at] = right
    for s in both:
        for c in comps:
            edge[s, c, pl.ds(ROWS, ROWS), :] = blank
            edge[s, c, pl.ds(row_of(depth), ROWS), :] = blank
        edge_div[s, pl.ds(ROWS, ROWS), :] = blank
        edge_div[s, pl.ds(row_of(depth), ROWS), :] = blank

    def join_blocks(ref, lead):
        for d in (0, half):
            base = row_of(d)
            last = ref[lead + (pl.ds(base + ROWS - 1, half, stride=PITCH), slice(None))]
            ahead = ref[lead + (pl.ds(base, half, stride=PITCH), slice(None))]
            spot = lane_iota((half, LANES))
            ref[lead + (pl.ds(base - 1, half, stride=PITCH), slice(None))] = jnp.where(
                spot >= EDGE, turn(last, EDGE), 0.0
            )
            ref[lead + (pl.ds(base + ROWS, half, stride=PITCH), slice(None))] = jnp.where(
                spot < LANES - EDGE, turn(ahead, -EDGE), 0.0
            )

    def at(s, c, d, by=0):
        return edge[s, c, pl.ds(row_of(d) + by, ROWS), :]

    def div_at(s, d, by=0):
        return edge_div[s, pl.ds(row_of(d) + by, ROWS), :]

    def middle(value, margin):
        spot = lane % EDGE
        return jnp.where((spot >= HALF - margin) & (spot < HALF + margin), value, 0.0)

    fixes = (packed, fix_first, fix_second, fix_third)

    def edge_step(level):
        for s in both:
            for c in comps:
                join_blocks(edge, (s, c))
        for s in both:
            for d in range(depth):
                x = at(s, 0, d)
                w = turn(x, -1) - turn(x, 1)
                w = w + (at(s, 1, d, 1) - at(s, 1, d, -1))
                w = w + (at(s, 2, d + 1) - at(s, 2, d - 1))
                edge_div[s, pl.ds(row_of(d), ROWS), :] = w * ((0.25 * BULK) * keep[s])
            join_blocks(edge_div, (s,))
        norm, cross = blank, blank
        for c in comps:
            images = []
            for d in range(depth):
                pair = []
                for s in both:
                    x = at(s, c, d)
                    if c == 0:
                        w = div_at(s, d)
                        total = turn(x + w, -1) + turn(x - w, 1)
                    else:
                        total = turn(x, -1) + turn(x, 1)
                    if c == 1:
                        total = total + (div_at(s, d, 1) - div_at(s, d, -1))
                    if c == 2:
                        total = total + (div_at(s, d + 1) - div_at(s, d - 1))
                    total = total + (at(s, c, d - 1) + at(s, c, d + 1))
                    total = total + (at(s, c, d, 1) + at(s, c, d, -1))
                    pair.append((edge_diag[s, d] * x - total) * keep[s])
                images.append(pair)
                old = fixes[level][c, d]
                new = jnp.where(first_half, pair[1], pair[0])
                fixes[level + 1][c, d] = new
                norm = norm + old * old
                cross = cross + old * new
            for d in range(depth):
                for s in both:
                    edge[s, c, pl.ds(row_of(d), ROWS), :] = images[d][s]
        return norm, cross

    edge_sums = [edge_step(level) for level in range(ITERS)]

    variants = ends.shape[0]
    pieces = 1 if per > 1 else variants
    blocks = 3 * ITERS * pieces
    bearing_rows = -(-blocks // per)
    picked[...] = jnp.zeros(picked.shape, jnp.float32)
    for block in range(blocks):
        value, piece = block // pieces, block % pieces
        row, z = block // per, (block % per if per > 1 else piece)
        level, c = value // 3, value % 3
        for side in both:
            place = (1 + 2 * side) * across // 4
            column = (2 * z + side) * LANES
            if level < 2:
                here = (field, first)[level][c, 1, PAD + place : PAD + place + 1, :]
            else:
                here = second_raw[c, 0, place : place + 1, :]
            if level:
                edges = fixes[level][c, 0, place % ROWS : place % ROWS + 1, :]
                here = mended(here, edges, place, 2 * level)
            picked[row : row + 1, column : column + LANES] = here
    start = (index * LANES).astype(jnp.float32)
    along = lax.broadcasted_iota(jnp.int32, (LANES, LANES), 0).astype(jnp.float32) + start
    parity = lane_iota((LANES, LANES)) % 2
    total = jnp.zeros((picked.shape[0], LANES), jnp.float32)
    for z in range(variants):
        site = jnp.broadcast_to(ends[z : z + 1, :], (LANES, LANES)) == along
        for side in both:
            column = (2 * z + side) * LANES
            hit = jnp.where(site & (parity == side), 1.0, 0.0)
            total = total + jnp.dot(
                picked[:, column : column + LANES], hit,
                precision=HIGH, preferred_element_type=jnp.float32,
            )

    clear_padding(div, (), depth, across)
    for c in comps:
        clear_padding(second, (c,), depth, across)

    def mend(d, carry):
        for c in comps:
            edges = fix_second[c, d]
            for r in range(0, across, CHUNK):
                second[c, d + 1, pl.ds(PAD + r, CHUNK), :] = mended(
                    second_raw[c, d, r : r + CHUNK, :], edges, r, 4
                )
        return carry

    loop(depth, 4, mend, 0)

    def store_third(c, d, r, out):
        third[c, d, r : r + CHUNK, :] = out

    norm, cross = cyclic_step(second, mass, div, store_third, 4)
    parts = [
        early[0],
        early[1] + middle(edge_sums[0][1], 2),
        early[2] + middle(edge_sums[1][0], 2),
        early[3] + middle(edge_sums[1][1], 4),
        norm,
        interior(cross, 2) + middle(edge_sums[2][1], 2),
    ]

    sums[...] = jnp.zeros(sums.shape, jnp.float32)
    sums[0:bearing_rows, :] = total[0:bearing_rows]
    low = lane_iota((1, LANES)) < LANES // 2
    for pair in range(3):
        halves = []
        for part in parts[2 * pair : 2 * pair + 2]:
            flat = jnp.sum(part, axis=0, keepdims=True)
            halves.append(flat + turn(flat, LANES // 2))
        sums[bearing_rows + pair : bearing_rows + pair + 1, :] = jnp.where(low, *halves)
    out = sums[...]
    for device in range(payload.shape[0]):
        payload[device] = out


def coefficients(moment):
    def dot(a, b):
        total = None
        for i, left in enumerate(a):
            for j, right in enumerate(b):
                term = left * right * moment[i + j]
                total = term if total is None else total + term
        return total

    one = jnp.ones_like(moment[0])
    solved, direction, increment = [one], [one], []
    norm = moment[0]
    for iteration in range(ITERS):
        image = [SHIFT * p for p in direction] + [jnp.zeros_like(one)]
        for i, p in enumerate(direction):
            image[i + 1] = image[i + 1] + p
        alpha = norm / dot(direction, image)
        increment = [
            alpha * p + (increment[i] if i < len(increment) else 0.0) for i, p in enumerate(direction)
        ]
        solved = [
            (solved[i] if i < len(solved) else 0.0) - alpha * q for i, q in enumerate(image)
        ]
        if iteration + 1 < ITERS:
            after = dot(solved, solved)
            ratio = after / norm
            direction = [
                s + (ratio * direction[i] if i < len(direction) else 0.0)
                for i, s in enumerate(solved)
            ]
            norm = after
    return increment, solved


def combine_kernel(
    per, gathered, field, first, second, third, fix_first, fix_third, ends, stick, load, prior,
    increment_hbm, residual_hbm, friction_hbm,
    increment, residual, friction, forces, sems, friction_sem,
):
    depth, across = third.shape[1], third.shape[2]
    start = (device_index() * LANES).astype(jnp.float32)
    bearings = load.shape[1]
    variants = ends.shape[0]
    pieces = 1 if per > 1 else variants
    width = min(bearings, LANES)
    bearing_rows = -(-9 * pieces // per)
    parts = [gathered[i] for i in range(gathered.shape[0])]
    while len(parts) > 1:
        parts = [sum(parts[i : i + 2]) for i in range(0, len(parts), 2)]
    total = parts[0]
    low = lane_iota((1, LANES)) < LANES // 2
    moments = []
    for n in range(6):
        row = total[bearing_rows + n // 2 : bearing_rows + n // 2 + 1]
        row = jnp.where(low == (n % 2 == 0), row, 0.0)
        moments.append(jnp.sum(row, axis=1, keepdims=True))
    grow, keep = coefficients(moments)

    forces[...] = jnp.zeros(forces.shape, jnp.float32)
    lane = lane_iota((1, width))
    for piece in range(pieces):
        span = slice(piece * LANES, piece * LANES + width)
        readout = []
        for c in range(3):
            value = None
            for k in range(ITERS):
                block = (3 * k + c) * pieces + piece
                row = total[block // per : block // per + 1]
                if per > 1 and block % per:
                    row = turn(row, LANES - (block % per) * bearings)
                term = grow[k] * row[:, :width]
                value = term if value is None else value + term
            readout.append(value)
        weight = load[:, span]
        radius = jnp.where(stick[:, span] == 1, STATIC, KINETIC) * weight
        trial = [prior[c : c + 1, span] + ELASTIC * readout[c] for c in range(2)]
        magnitude = jnp.sqrt(trial[0] * trial[0] + trial[1] * trial[1])
        scale = radius / jnp.maximum(magnitude, radius)
        held = [t * scale for t in trial]
        for c in range(2):
            friction[c : c + 1, span] = held[c]
        force = [held[c] + weight / RADIUS * readout[c] for c in range(2)] + [VERTICAL * readout[2]]
        for c in range(3):
            for side in range(2):
                forces[2 * c + side : 2 * c + side + 1, span] = jnp.where(
                    lane % 2 == side, force[c], 0.0
                )
    friction_copy = pltpu.make_async_copy(friction, friction_hbm, friction_sem)
    friction_copy.start()
    along = lax.broadcasted_iota(jnp.int32, (LANES, LANES), 0).astype(jnp.float32) + start
    placed = jnp.zeros((8, LANES), jnp.float32)
    for piece in range(pieces):
        site = jnp.broadcast_to(ends[piece : piece + 1, :], (LANES, LANES)) == along
        placed = placed + lax.dot_general(
            forces[:, piece * LANES : (piece + 1) * LANES], jnp.where(site, 1.0, 0.0),
            (((1,), (1,)), ((), ())), precision=HIGH, preferred_element_type=jnp.float32,
        )

    grow = [jnp.broadcast_to(g, (ROWS, LANES)) for g in grow]
    keep = [jnp.broadcast_to(g, (ROWS, LANES)) for g in keep]

    def run(c, begin, end):
        for d in range(begin, end):
            edges = fix_first[c, d], fix_third[c, d]
            for r in range(0, across, ROWS):
                here = pl.ds(PAD + r, ROWS)
                v = [ref[c, d + 1, here, :] for ref in (field, first, second)]
                v.append(third[c, d, r : r + ROWS, :])
                v[1] = mended(v[1], edges[0], r, 2)
                v[3] = mended(v[3], edges[1], r, 2)
                increment[c, d, r : r + ROWS, :] = grow[0] * v[0] + grow[1] * v[1] + grow[2] * v[2]
                residual[c, d, r : r + ROWS, :] = (
                    keep[0] * v[0] + keep[1] * v[1] + (keep[2] * v[2] + keep[3] * v[3])
                )

    def copy(which, c, begin):
        ref, hbm = ((increment, increment_hbm), (residual, residual_hbm))[which]
        part = pl.ds(begin, PIECE)
        return pltpu.make_async_copy(
            ref.at[c, part], hbm.at[c, part], sems.at[which, c, begin // PIECE]
        )

    starts = range(0, depth, PIECE)
    for c in range(3):
        for begin in starts:
            run(c, begin, begin + PIECE)
            if begin == 0:
                for side in range(2):
                    at = (1 + 2 * side) * across // 4
                    residual[c, 0, at : at + 1, :] = (
                        residual[c, 0, at : at + 1, :] - placed[2 * c + side : 2 * c + side + 1]
                    )
            for which in range(2):
                copy(which, c, begin).start()
    friction_copy.wait()
    for c in range(3):
        for begin in starts:
            for which in range(2):
                copy(which, c, begin).wait()


def vmem_spec():
    return pl.BlockSpec(memory_space=pltpu.VMEM)


def hbm_spec():
    return pl.BlockSpec(memory_space=pltpu.HBM)


def pack_call(right_side, mass_field):
    f32 = jnp.float32
    depth, across, along = mass_field.shape
    half = depth // 2
    return pl.pallas_call(
        pack_kernel,
        out_shape=(
            pltpu.VMEM((3, depth + 2, across + 2 * PAD, along), f32),
            pltpu.VMEM((depth, across, along), f32),
            pltpu.VMEM((4, depth, ROWS, LANES), f32),
            jax.ShapeDtypeStruct((4, half, ROWS, LANES), f32),
            jax.ShapeDtypeStruct((4, half, ROWS, LANES), f32),
        ),
        in_specs=[hbm_spec()] * 2,
        out_specs=(vmem_spec(),) * 5,
        scratch_shapes=[pltpu.SemaphoreType.DMA((4,))],
        compiler_params=LIMIT,
        name="pack",
    )(
        pltpu.with_memory_space_constraint(right_side, pltpu.HBM),
        pltpu.with_memory_space_constraint(mass_field, pltpu.HBM),
    )


def cyclic_call(field, mass, spans, variants):
    f32 = jnp.float32
    depth, across, along = mass.shape
    padded = (depth + 2, across + 2 * PAD, along)
    return pl.pallas_call(
        cyclic_kernel,
        out_shape=(
            pltpu.VMEM((3,) + padded, f32),
            pltpu.VMEM((3, depth, across, along), f32),
            pltpu.VMEM((4, ROWS, LANES), f32),
            pltpu.VMEM((variants, LANES), f32),
        ),
        in_specs=[vmem_spec()] * 3,
        out_specs=(vmem_spec(),) * 4,
        scratch_shapes=[pltpu.VMEM(padded, f32)],
        compiler_params=LIMIT,
        cost_estimate=pl.CostEstimate(flops=40_000_000, bytes_accessed=8_000_000, transcendentals=0),
        name="cyclic",
    )(field, mass, spans)


def basis_call(per, rows, field, mass, packed, got_a, got_b, first, second_raw, early, ends, count):
    f32 = jnp.float32
    depth, across, along = mass.shape
    variants = ends.shape[0]
    padded = (depth + 2, across + 2 * PAD, along)
    edges = (3, depth, ROWS, LANES)
    return pl.pallas_call(
        functools.partial(basis_kernel, per),
        out_shape=(
            pltpu.VMEM((3,) + padded, f32),
            pltpu.VMEM((3, depth, across, along), f32),
            pltpu.VMEM(edges, f32),
            pltpu.VMEM(edges, f32),
            jax.ShapeDtypeStruct((count, rows, LANES), f32),
        ),
        in_specs=[vmem_spec()] * 9,
        out_specs=(vmem_spec(),) * 5,
        scratch_shapes=[
            pltpu.VMEM(padded, f32),
            pltpu.VMEM((2, 3, (depth + 2) * PITCH, LANES), f32),
            pltpu.VMEM((2, (depth + 2) * PITCH, LANES), f32),
            pltpu.VMEM((2, depth, ROWS, LANES), f32),
            pltpu.VMEM(edges, f32),
            pltpu.VMEM((rows, LANES), f32),
            pltpu.VMEM((rows, 2 * variants * LANES), f32),
        ],
        compiler_params=LIMIT,
        name="basis",
    )(field, mass, packed, got_a, got_b, first, second_raw, early, ends)


def combine_call(per, gathered, field, first, second, third, fixes, ends, stick, load, prior):
    f32 = jnp.float32
    shape = third.shape
    bearings = load.shape[1]
    return pl.pallas_call(
        functools.partial(combine_kernel, per),
        out_shape=(
            jax.ShapeDtypeStruct(shape, f32),
            jax.ShapeDtypeStruct(shape, f32),
            jax.ShapeDtypeStruct((2, bearings), f32),
        ),
        in_specs=[vmem_spec()] * 11,
        out_specs=(hbm_spec(),) * 3,
        scratch_shapes=[
            pltpu.VMEM(shape, f32),
            pltpu.VMEM(shape, f32),
            pltpu.VMEM((2, bearings), f32),
            pltpu.VMEM((ROWS, max(bearings, LANES)), f32),
            pltpu.SemaphoreType.DMA((2, 3, shape[1] // PIECE)),
            pltpu.SemaphoreType.DMA(()),
        ],
        compiler_params=LIMIT,
        name="combine",
    )(gathered, field, first, second, third, *fixes, ends, stick, load, prior)


def shards(count, right_side, mass_field, span_lengths, stick_flags, normal_load, prior_friction):
    piers = span_lengths.shape[0]
    bearings = 2 * piers
    per = LANES // bearings if bearings <= LANES else 1
    variants = per if bearings <= LANES else bearings // LANES
    pieces = 1 if per > 1 else variants
    rows = -(-(-(-3 * ITERS * pieces // per) + 3) // ROWS) * ROWS

    field, mass, packed, message_a, message_b = pack_call(right_side, mass_field)
    pairs_a = [p for i in range(0, count - 1, 2) for p in ((i, i + 1), (i + 1, i))]
    pairs_b = [p for i in range(1, count - 1, 2) for p in ((i, i + 1), (i + 1, i))]
    got_a = lax.ppermute(message_a, AXES, pairs_a)
    got_b = lax.ppermute(message_b, AXES, pairs_b)
    first, second_raw, early, ends = cyclic_call(
        field, mass, span_lengths.reshape(1, piers), variants
    )
    second, third, fix_first, fix_third, payload = basis_call(
        per, rows, field, mass, packed, got_a, got_b, first, second_raw, early, ends, count
    )
    gathered = lax.all_to_all(payload, AXES, 0, 0)
    return combine_call(
        per, gathered, field, first, second, third, (fix_first, fix_third), ends,
        stick_flags.reshape(1, bearings), normal_load.reshape(1, bearings), prior_friction,
    )


def solution(mesh):
    count = mesh.shape["len"] * mesh.shape["xs"]
    along = P(None, None, None, AXES)
    in_specs = (along, P(None, None, AXES), P(), P(), P(), P())
    return jax.shard_map(
        functools.partial(shards, count), mesh=mesh,
        in_specs=in_specs, out_specs=(along, along, P()), check_vma=False,
    )
```

```python
import functools

import jax
import jax.numpy as jnp
from jax import lax
from jax.experimental import pallas as pl
from jax.experimental.pallas import tpu as pltpu
from jax.sharding import PartitionSpec as P

ITERS = 3
SHIFT = 4.0
BULK = 1.5
ELASTIC = 8.0
RADIUS = 4.0
VERTICAL = 5.0
STATIC = 0.6
KINETIC = 0.45

AXES = ("len", "xs")
LANES = 128
ROWS = 8
PAD = 8
EDGE = 16
HALF = EDGE // 2
BLOCKS = LANES // EDGE
PITCH = 3 * ROWS
CHUNK = 16
PIECE = 16
MARGINS = (6, 5, 5)
HIGH = lax.Precision.HIGHEST
LIMIT = pltpu.CompilerParams(vmem_limit_bytes=32 * 1024 * 1024)


def turn(x, amount):
    return pltpu.roll(x, amount % LANES, x.ndim - 1)


def lane_iota(shape):
    return lax.broadcasted_iota(jnp.int32, shape, len(shape) - 1)


def loop(count, step, body, init):
    def several(i, carry):
        for j in range(step):
            carry = body(i * step + j, carry)
        return carry

    return lax.fori_loop(0, count // step, several, init)


def device_index():
    return lax.axis_index(AXES[0]) * lax.axis_size(AXES[1]) + lax.axis_index(AXES[1])


def clear_padding(ref, lead, depth, across):
    for slab in (0, depth + 1):
        ref[lead + (slab,)] = jnp.zeros((across + 2 * PAD, LANES), jnp.float32)
    blank = jnp.zeros((PAD, LANES), jnp.float32)
    for d in range(1, depth + 1):
        ref[lead + (d, slice(0, PAD))] = blank
        ref[lead + (d, slice(PAD + across, None))] = blank


def pack_kernel(right_hbm, mass_hbm, field, mass, packed, message_a, message_b, sems):
    depth, across = mass.shape[0], mass.shape[1]
    copies = [
        pltpu.make_async_copy(
            right_hbm.at[c], field.at[c, pl.ds(1, depth), pl.ds(PAD, across)], sems.at[c]
        )
        for c in range(3)
    ]
    copies.append(pltpu.make_async_copy(mass_hbm, mass, sems.at[3]))
    for copy in copies:
        copy.start()
    for c in range(3):
        clear_padding(field, (c,), depth, across)
    is_even = device_index() % 2 == 0
    lane = lane_iota((ROWS, LANES))
    block_of = lane // EDGE
    first_half = lane % EDGE < HALF
    for c in range(4):
        copies[c].wait()
        edges = []
        for d in range(depth):
            edge = None
            for b in range(across // ROWS):
                row = pl.ds(b * ROWS + (PAD if c < 3 else 0), ROWS)
                if c < 3:
                    tile = field[c, d + 1, row, :]
                else:
                    tile = mass[d, row, :] + (6.0 - SHIFT)
                    mass[d, row, :] = tile
                moved = turn(tile, EDGE * b + HALF)
                edge = moved if edge is None else jnp.where(block_of == b, moved, edge)
            packed[c, d] = edge
            edges.append(edge)
        for d in range(depth // 2):
            low, high = edges[d], edges[d + depth // 2]
            rightward = jnp.where(first_half, low, turn(high, HALF))
            leftward = jnp.where(first_half, turn(low, -HALF), high)
            message_a[c, d] = jnp.where(is_even, rightward, leftward)
            message_b[c, d] = jnp.where(is_even, leftward, rightward)


def folded(x):
    return sum(x[i : i + ROWS] for i in range(0, x.shape[0], ROWS))


def cyclic_step(source, mass, div, store, step, inner_source=None, inner_div=None):
    depth, across = mass.shape[0], mass.shape[1]
    chunks = range(0, across, CHUNK)
    block_of = lane_iota((ROWS, LANES)) // EDGE

    def pack(edge, r, tile):
        for i in range(0, CHUNK, ROWS):
            b = (r + i) // ROWS
            moved = turn(tile[i : i + ROWS], EDGE * b + HALF)
            edge = moved if edge is None else jnp.where(block_of == b, moved, edge)
        return edge

    def divergence(d, carry):
        edge, edge_div = None, None
        for r in chunks:
            here, up, down = (pl.ds(PAD + r + by, CHUNK) for by in (0, 1, -1))
            x = source[0, d + 1, here, :]
            w = turn(x, -1) - turn(x, 1)
            w = w + (source[1, d + 1, up, :] - source[1, d + 1, down, :])
            w = w + (source[2, d + 2, here, :] - source[2, d, here, :])
            w = w * (0.25 * BULK)
            div[d + 1, here, :] = w
            if inner_source is not None:
                edge = pack(edge, r, x)
            if inner_div is not None:
                edge_div = pack(edge_div, r, w)
        if inner_source is not None:
            inner_source[d] = edge
        if inner_div is not None:
            inner_div[d] = edge_div
        return carry

    loop(depth, step, divergence, 0)

    def image(d, carry):
        norm, cross, cross_rest = carry
        for r in chunks:
            here, up, down = (pl.ds(PAD + r + by, CHUNK) for by in (0, 1, -1))
            diag = mass[d, r : r + CHUNK, :]
            w = div[d + 1, here, :]
            norms, crosses = [], []
            for c in range(3):
                x = source[c, d + 1, here, :]
                if c == 0:
                    total = turn(x + w, -1) + turn(x - w, 1)
                else:
                    total = turn(x, -1) + turn(x, 1)
                if c == 1:
                    total = total + (div[d + 1, up, :] - div[d + 1, down, :])
                if c == 2:
                    total = total + (div[d + 2, here, :] - div[d, here, :])
                total = total + (source[c, d, here, :] + source[c, d + 2, here, :])
                total = total + (source[c, d + 1, up, :] + source[c, d + 1, down, :])
                out = diag * x - total
                store(c, d, r, out)
                norms.append(x * x)
                crosses.append(x * out)
            norm = norm + folded(norms[0] + norms[1] + norms[2])
            cross = cross + folded(crosses[0])
            cross_rest = cross_rest + folded(crosses[1] + crosses[2])
        return norm, cross, cross_rest

    return loop(depth, step, image, (jnp.zeros((ROWS, LANES), jnp.float32),) * 3)


def interior(value, margin):
    lane = lane_iota(value.shape)
    return jnp.where((lane >= margin) & (lane < LANES - margin), value, 0.0)


def cyclic_kernel(field, mass, spans, first, second, third, inner, moments, ends, div):
    depth, across = mass.shape[0], mass.shape[1]
    clear_padding(div, (), depth, across)
    for c in range(3):
        clear_padding(first, (c,), depth, across)
        clear_padding(second, (c,), depth, across)

    def store_first(c, d, r, out):
        first[c, d + 1, pl.ds(PAD + r, CHUNK), :] = out

    def store_second(c, d, r, out):
        second[c, d + 1, pl.ds(PAD + r, CHUNK), :] = out

    def store_third(c, d, r, out):
        third[c, d, r : r + CHUNK, :] = out

    norm, cross, cross_rest = cyclic_step(field, mass, div, store_first, 4)
    moments[0] = norm
    moments[1] = interior(cross + cross_rest, 2)
    norm, cross, cross_rest = cyclic_step(first, mass, div, store_second, 4, inner.at[0])
    moments[2] = interior(norm, 2)
    moments[3] = interior(cross + cross_rest, 4)
    norm, cross, cross_rest = cyclic_step(
        second, mass, div, store_third, 4, inner.at[1], inner.at[2]
    )
    moments[4] = interior(norm, 4)
    moments[5] = interior(cross, MARGINS[0]) + interior(cross_rest, MARGINS[1])
    piers = spans.shape[1]
    bearings = 2 * piers
    lane = lane_iota((piers, LANES))
    pier = lax.broadcasted_iota(jnp.int32, (piers, LANES), 0)
    lengths = jnp.broadcast_to(spans[...].astype(jnp.float32), (ROWS, piers))
    for z in range(ends.shape[0]):
        bearing = lane - z * bearings if bearings <= LANES else lane + z * LANES
        upto = jnp.where(pier * 2 <= bearing, 1.0, 0.0)
        total = jnp.dot(lengths, upto, precision=HIGH, preferred_element_type=jnp.float32)
        inside = (bearing[0:1] >= 0) & (bearing[0:1] < bearings)
        ends[z : z + 1, :] = jnp.where(inside, total[0:1] - 1.0, -1e9)


def mended(value, edges, row, margin):
    moved = [
        turn(edges, -(EDGE * ((row + i) // ROWS) + HALF)) for i in range(0, value.shape[0], ROWS)
    ]
    spot = lane_iota(value.shape)
    return jnp.where(
        (spot < margin) | (spot >= LANES - margin),
        moved[0] if len(moved) == 1 else jnp.concatenate(moved, axis=0),
        value,
    )


def edge_kernel(
    per, packed, got_a, got_b, inner, field, first, second, early, ends,
    fix_first, fix_second, fix_third, payload,
    edge, edge_div, edge_diag, sums, picked,
):
    depth, across = packed.shape[1], first.shape[2] - 2 * PAD
    index = device_index()
    count = lax.axis_size(AXES[0]) * lax.axis_size(AXES[1])
    is_even = index % 2 == 0
    lane = lane_iota((ROWS, LANES))
    first_half = lane % EDGE < HALF
    ones = jnp.ones((ROWS, LANES), jnp.float32)
    keep = (
        jnp.where(first_half & (index == 0), 0.0, ones),
        jnp.where(jnp.logical_not(first_half) & (index == count - 1), 0.0, ones),
    )
    both = range(2)
    comps = range(3)
    half = depth // 2
    blank = jnp.zeros((ROWS, LANES), jnp.float32)

    def row_of(d):
        return (d + 1) * PITCH + ROWS

    for c in range(4):
        for d in range(half):
            a, b = got_a[c, d], got_b[c, d]
            from_left = jnp.where(is_even, b, a)
            from_right = jnp.where(is_even, a, b)
            low, high = packed[c, d], packed[c, d + half]
            for at, left, right in (
                (
                    d,
                    jnp.where(first_half, from_left, low),
                    jnp.where(first_half, low, turn(from_right, HALF)),
                ),
                (
                    d + half,
                    jnp.where(first_half, turn(from_left, -HALF), high),
                    jnp.where(first_half, high, from_right),
                ),
            ):
                if c < 3:
                    edge[0, c, pl.ds(row_of(at), ROWS), :] = left
                    edge[1, c, pl.ds(row_of(at), ROWS), :] = right
                else:
                    edge_diag[0, at] = left
                    edge_diag[1, at] = right
    for s in both:
        for c in comps:
            edge[s, c, pl.ds(ROWS, ROWS), :] = blank
            edge[s, c, pl.ds(row_of(depth), ROWS), :] = blank
        edge_div[s, pl.ds(ROWS, ROWS), :] = blank
        edge_div[s, pl.ds(row_of(depth), ROWS), :] = blank

    def join_blocks(ref, lead):
        for d in (0, half):
            base = row_of(d)
            last = ref[lead + (pl.ds(base + ROWS - 1, half, stride=PITCH), slice(None))]
            ahead = ref[lead + (pl.ds(base, half, stride=PITCH), slice(None))]
            spot = lane_iota((half, LANES))
            ref[lead + (pl.ds(base - 1, half, stride=PITCH), slice(None))] = jnp.where(
                spot >= EDGE, turn(last, EDGE), 0.0
            )
            ref[lead + (pl.ds(base + ROWS, half, stride=PITCH), slice(None))] = jnp.where(
                spot < LANES - EDGE, turn(ahead, -EDGE), 0.0
            )

    def at(s, c, d, by=0):
        return edge[s, c, pl.ds(row_of(d) + by, ROWS), :]

    def div_at(s, d, by=0):
        return edge_div[s, pl.ds(row_of(d) + by, ROWS), :]

    def middle(value, margin):
        spot = lane % EDGE
        return jnp.where((spot >= HALF - margin) & (spot < HALF + margin), value, 0.0)

    fixes = (packed, fix_first, fix_second, fix_third)
    last_planes = lane % EDGE >= EDGE - 2
    first_planes = lane % EDGE < 2

    def joined(s, value, own):
        return jnp.where(first_planes if s else last_planes, own, value)

    def edge_step(level):
        for s in both:
            for c in comps:
                join_blocks(edge, (s, c))
        for s in both:
            for d in range(depth):
                x = at(s, 0, d)
                w = turn(x, -1) - turn(x, 1)
                w = w + (at(s, 1, d, 1) - at(s, 1, d, -1))
                w = w + (at(s, 2, d + 1) - at(s, 2, d - 1))
                w = w * ((0.25 * BULK) * keep[s])
                edge_div[s, pl.ds(row_of(d), ROWS), :] = joined(s, w, inner[2, d]) if level == 2 else w
            join_blocks(edge_div, (s,))
        norms, crosses = [], []
        for c in comps:
            norm, cross = blank, blank
            images = []
            for d in range(depth):
                pair = []
                for s in both:
                    x = at(s, c, d)
                    if c == 0:
                        w = div_at(s, d)
                        total = turn(x + w, -1) + turn(x - w, 1)
                    else:
                        total = turn(x, -1) + turn(x, 1)
                    if c == 1:
                        total = total + (div_at(s, d, 1) - div_at(s, d, -1))
                    if c == 2:
                        total = total + (div_at(s, d + 1) - div_at(s, d - 1))
                    total = total + (at(s, c, d - 1) + at(s, c, d + 1))
                    total = total + (at(s, c, d, 1) + at(s, c, d, -1))
                    pair.append((edge_diag[s, d] * x - total) * keep[s])
                images.append(pair)
                old = fixes[level][c, d]
                new = jnp.where(first_half, pair[1], pair[0])
                fixes[level + 1][c, d] = new
                norm = norm + old * old
                cross = cross + old * new
            norms.append(norm)
            crosses.append(cross)
            if level + 1 == ITERS:
                continue
            for d in range(depth):
                for s in both:
                    value = images[d][s] if c else joined(s, images[d][s], inner[level, d])
                    edge[s, c, pl.ds(row_of(d), ROWS), :] = value
        return norms, crosses

    edge_sums = [edge_step(level) for level in range(ITERS)]

    variants = ends.shape[0]
    pieces = 1 if per > 1 else variants
    blocks = 3 * ITERS * pieces
    bearing_rows = -(-blocks // per)
    picked[...] = jnp.zeros(picked.shape, jnp.float32)
    for block in range(blocks):
        value, piece = block // pieces, block % pieces
        row, z = block // per, (block % per if per > 1 else piece)
        level, c = value // 3, value % 3
        for side in both:
            place = (1 + 2 * side) * across // 4
            column = (2 * z + side) * LANES
            here = (field, first, second)[level][c, 1, PAD + place : PAD + place + 1, :]
            if level:
                edges = fixes[level][c, 0, place % ROWS : place % ROWS + 1, :]
                here = mended(here, edges, place, 2 * level)
            picked[row : row + 1, column : column + LANES] = here
    start = (index * LANES).astype(jnp.float32)
    along = lax.broadcasted_iota(jnp.int32, (LANES, LANES), 0).astype(jnp.float32) + start
    parity = lane_iota((LANES, LANES)) % 2
    total = jnp.zeros((picked.shape[0], LANES), jnp.float32)
    for z in range(variants):
        site = jnp.broadcast_to(ends[z : z + 1, :], (LANES, LANES)) == along
        for side in both:
            column = (2 * z + side) * LANES
            hit = jnp.where(site & (parity == side), 1.0, 0.0)
            total = total + jnp.dot(
                picked[:, column : column + LANES], hit,
                precision=HIGH, preferred_element_type=jnp.float32,
            )

    def at_edge(values, margins):
        return sum(middle(v, m) for v, m in zip(values, margins))

    parts = [
        early[0],
        early[1] + at_edge(edge_sums[0][1], (2, 2, 2)),
        early[2] + at_edge(edge_sums[1][0], (2, 2, 2)),
        early[3] + at_edge(edge_sums[1][1], (4, 4, 4)),
        early[4] + at_edge(edge_sums[2][0], (4, 4, 4)),
        early[5] + at_edge(edge_sums[2][1], MARGINS),
    ]

    sums[...] = jnp.zeros(sums.shape, jnp.float32)
    sums[0:bearing_rows, :] = total[0:bearing_rows]
    low = lane_iota((1, LANES)) < LANES // 2
    for pair in range(3):
        halves = []
        for part in parts[2 * pair : 2 * pair + 2]:
            flat = jnp.sum(part, axis=0, keepdims=True)
            halves.append(flat + turn(flat, LANES // 2))
        sums[bearing_rows + pair : bearing_rows + pair + 1, :] = jnp.where(low, *halves)
    out = sums[...]
    for device in range(payload.shape[0]):
        payload[device] = out


def coefficients(moment):
    def dot(a, b):
        total = None
        for i, left in enumerate(a):
            for j, right in enumerate(b):
                term = left * right * moment[i + j]
                total = term if total is None else total + term
        return total

    one = jnp.ones_like(moment[0])
    solved, direction, increment = [one], [one], []
    norm = moment[0]
    for iteration in range(ITERS):
        image = [SHIFT * p for p in direction] + [jnp.zeros_like(one)]
        for i, p in enumerate(direction):
            image[i + 1] = image[i + 1] + p
        alpha = norm / dot(direction, image)
        increment = [
            alpha * p + (increment[i] if i < len(increment) else 0.0) for i, p in enumerate(direction)
        ]
        solved = [
            (solved[i] if i < len(solved) else 0.0) - alpha * q for i, q in enumerate(image)
        ]
        if iteration + 1 < ITERS:
            after = dot(solved, solved)
            ratio = after / norm
            direction = [
                s + (ratio * direction[i] if i < len(direction) else 0.0)
                for i, s in enumerate(solved)
            ]
            norm = after
    return increment, solved


def combine_kernel(
    per, gathered, field, first, second, third, packed, fix_first, fix_second, fix_third,
    ends, stick, load, prior,
    increment_hbm, residual_hbm, friction_hbm,
    increment, residual, friction, forces, sems, friction_sem,
):
    depth, across = third.shape[1], third.shape[2]
    start = (device_index() * LANES).astype(jnp.float32)
    bearings = load.shape[1]
    variants = ends.shape[0]
    pieces = 1 if per > 1 else variants
    width = min(bearings, LANES)
    bearing_rows = -(-9 * pieces // per)
    parts = [gathered[i] for i in range(gathered.shape[0])]
    while len(parts) > 1:
        parts = [sum(parts[i : i + 2]) for i in range(0, len(parts), 2)]
    total = parts[0]
    low = lane_iota((1, LANES)) < LANES // 2
    moments = []
    for n in range(6):
        row = total[bearing_rows + n // 2 : bearing_rows + n // 2 + 1]
        row = jnp.where(low == (n % 2 == 0), row, 0.0)
        moments.append(jnp.sum(row, axis=1, keepdims=True))
    grow, keep = coefficients(moments)

    forces[...] = jnp.zeros(forces.shape, jnp.float32)
    lane = lane_iota((1, width))
    for piece in range(pieces):
        span = slice(piece * LANES, piece * LANES + width)
        readout = []
        for c in range(3):
            value = None
            for k in range(ITERS):
                block = (3 * k + c) * pieces + piece
                row = total[block // per : block // per + 1]
                if per > 1 and block % per:
                    row = turn(row, LANES - (block % per) * bearings)
                term = grow[k] * row[:, :width]
                value = term if value is None else value + term
            readout.append(value)
        weight = load[:, span]
        radius = jnp.where(stick[:, span] == 1, STATIC, KINETIC) * weight
        trial = [prior[c : c + 1, span] + ELASTIC * readout[c] for c in range(2)]
        magnitude = jnp.sqrt(trial[0] * trial[0] + trial[1] * trial[1])
        scale = radius / jnp.maximum(magnitude, radius)
        held = [t * scale for t in trial]
        for c in range(2):
            friction[c : c + 1, span] = held[c]
        force = [held[c] + weight / RADIUS * readout[c] for c in range(2)] + [VERTICAL * readout[2]]
        for c in range(3):
            for side in range(2):
                forces[2 * c + side : 2 * c + side + 1, span] = jnp.where(
                    lane % 2 == side, force[c], 0.0
                )
    friction_copy = pltpu.make_async_copy(friction, friction_hbm, friction_sem)
    friction_copy.start()
    along = lax.broadcasted_iota(jnp.int32, (LANES, LANES), 0).astype(jnp.float32) + start
    placed = jnp.zeros((8, LANES), jnp.float32)
    for piece in range(pieces):
        site = jnp.broadcast_to(ends[piece : piece + 1, :], (LANES, LANES)) == along
        placed = placed + lax.dot_general(
            forces[:, piece * LANES : (piece + 1) * LANES], jnp.where(site, 1.0, 0.0),
            (((1,), (1,)), ((), ())), precision=HIGH, preferred_element_type=jnp.float32,
        )

    grow = [jnp.broadcast_to(g, (ROWS, LANES)) for g in grow]
    keep = [jnp.broadcast_to(g, (ROWS, LANES)) for g in keep]

    def total_of(terms, values):
        parts = [t * v for t, v in zip(terms, values)]
        return parts[0] + parts[1] + (parts[2] if len(parts) == 3 else parts[2] + parts[3])

    def run(c, begin, end):
        for d in range(begin, end):
            edges = [ref[c, d] for ref in (packed, fix_first, fix_second, fix_third)]
            edges = total_of(grow, edges), total_of(keep, edges)
            for r in range(0, across, ROWS):
                here = pl.ds(PAD + r, ROWS)
                v = [ref[c, d + 1, here, :] for ref in (field, first, second)]
                v.append(third[c, d, r : r + ROWS, :])
                for ref, terms, edge in ((increment, grow, edges[0]), (residual, keep, edges[1])):
                    ref[c, d, r : r + ROWS, :] = mended(total_of(terms, v), edge, r, MARGINS[c])

    def copy(which, c, begin):
        ref, hbm = ((increment, increment_hbm), (residual, residual_hbm))[which]
        part = pl.ds(begin, PIECE)
        return pltpu.make_async_copy(
            ref.at[c, part], hbm.at[c, part], sems.at[which, c, begin // PIECE]
        )

    starts = range(0, depth, PIECE)
    for c in range(3):
        for begin in starts:
            run(c, begin, begin + PIECE)
            if begin == 0:
                for side in range(2):
                    at = (1 + 2 * side) * across // 4
                    residual[c, 0, at : at + 1, :] = (
                        residual[c, 0, at : at + 1, :] - placed[2 * c + side : 2 * c + side + 1]
                    )
            for which in range(2):
                copy(which, c, begin).start()
    friction_copy.wait()
    for c in range(3):
        for begin in starts:
            for which in range(2):
                copy(which, c, begin).wait()


def vmem_spec():
    return pl.BlockSpec(memory_space=pltpu.VMEM)


def hbm_spec():
    return pl.BlockSpec(memory_space=pltpu.HBM)


def pack_call(right_side, mass_field):
    f32 = jnp.float32
    depth, across, along = mass_field.shape
    half = depth // 2
    return pl.pallas_call(
        pack_kernel,
        out_shape=(
            pltpu.VMEM((3, depth + 2, across + 2 * PAD, along), f32),
            pltpu.VMEM((depth, across, along), f32),
            pltpu.VMEM((4, depth, ROWS, LANES), f32),
            jax.ShapeDtypeStruct((4, half, ROWS, LANES), f32),
            jax.ShapeDtypeStruct((4, half, ROWS, LANES), f32),
        ),
        in_specs=[hbm_spec()] * 2,
        out_specs=(vmem_spec(),) * 5,
        scratch_shapes=[pltpu.SemaphoreType.DMA((4,))],
        compiler_params=LIMIT,
        name="pack",
    )(
        pltpu.with_memory_space_constraint(right_side, pltpu.HBM),
        pltpu.with_memory_space_constraint(mass_field, pltpu.HBM),
    )


def cyclic_call(field, mass, spans, variants):
    f32 = jnp.float32
    depth, across, along = mass.shape
    padded = (depth + 2, across + 2 * PAD, along)
    return pl.pallas_call(
        cyclic_kernel,
        out_shape=(
            pltpu.VMEM((3,) + padded, f32),
            pltpu.VMEM((3,) + padded, f32),
            pltpu.VMEM((3, depth, across, along), f32),
            pltpu.VMEM((3, depth, ROWS, LANES), f32),
            pltpu.VMEM((6, ROWS, LANES), f32),
            pltpu.VMEM((variants, LANES), f32),
        ),
        in_specs=[vmem_spec()] * 3,
        out_specs=(vmem_spec(),) * 6,
        scratch_shapes=[pltpu.VMEM(padded, f32)],
        compiler_params=LIMIT,
        cost_estimate=pl.CostEstimate(flops=60_000_000, bytes_accessed=12_000_000, transcendentals=0),
        name="cyclic",
    )(field, mass, spans)


def edge_call(per, rows, packed, got_a, got_b, inner, field, first, second, early, ends, count):
    f32 = jnp.float32
    depth = packed.shape[1]
    variants = ends.shape[0]
    edges = (3, depth, ROWS, LANES)
    return pl.pallas_call(
        functools.partial(edge_kernel, per),
        out_shape=(pltpu.VMEM(edges, f32),) * 3 + (pltpu.VMEM((count, rows, LANES), f32),),
        in_specs=[vmem_spec()] * 9,
        out_specs=(vmem_spec(),) * 4,
        scratch_shapes=[
            pltpu.VMEM((2, 3, (depth + 2) * PITCH, LANES), f32),
            pltpu.VMEM((2, (depth + 2) * PITCH, LANES), f32),
            pltpu.VMEM((2, depth, ROWS, LANES), f32),
            pltpu.VMEM((rows, LANES), f32),
            pltpu.VMEM((rows, 2 * variants * LANES), f32),
        ],
        compiler_params=LIMIT,
        name="edge",
    )(packed, got_a, got_b, inner, field, first, second, early, ends)


def combine_call(per, gathered, field, first, second, third, edges, ends, stick, load, prior):
    f32 = jnp.float32
    shape = third.shape
    bearings = load.shape[1]
    return pl.pallas_call(
        functools.partial(combine_kernel, per),
        out_shape=(
            jax.ShapeDtypeStruct(shape, f32),
            jax.ShapeDtypeStruct(shape, f32),
            jax.ShapeDtypeStruct((2, bearings), f32),
        ),
        in_specs=[vmem_spec()] * 13,
        out_specs=(hbm_spec(),) * 3,
        scratch_shapes=[
            pltpu.VMEM(shape, f32),
            pltpu.VMEM(shape, f32),
            pltpu.VMEM((2, bearings), f32),
            pltpu.VMEM((ROWS, max(bearings, LANES)), f32),
            pltpu.SemaphoreType.DMA((2, 3, shape[1] // PIECE)),
            pltpu.SemaphoreType.DMA(()),
        ],
        compiler_params=LIMIT,
        name="combine",
    )(gathered, field, first, second, third, *edges, ends, stick, load, prior)


def shards(count, right_side, mass_field, span_lengths, stick_flags, normal_load, prior_friction):
    piers = span_lengths.shape[0]
    bearings = 2 * piers
    per = LANES // bearings if bearings <= LANES else 1
    variants = per if bearings <= LANES else bearings // LANES
    pieces = 1 if per > 1 else variants
    rows = -(-(-(-3 * ITERS * pieces // per) + 3) // ROWS) * ROWS

    field, mass, packed, message_a, message_b = pack_call(right_side, mass_field)
    pairs_a = [p for i in range(0, count - 1, 2) for p in ((i, i + 1), (i + 1, i))]
    pairs_b = [p for i in range(1, count - 1, 2) for p in ((i, i + 1), (i + 1, i))]
    got_a = lax.ppermute(message_a, AXES, pairs_a)
    got_b = lax.ppermute(message_b, AXES, pairs_b)
    first, second, third, inner, early, ends = cyclic_call(
        field, mass, span_lengths.reshape(1, piers), variants
    )
    *fixes, payload = edge_call(
        per, rows, packed, got_a, got_b, inner, field, first, second, early, ends, count
    )
    gathered = lax.all_to_all(payload, AXES, 0, 0)
    return combine_call(
        per, gathered, field, first, second, third, (packed, *fixes), ends,
        stick_flags.reshape(1, bearings), normal_load.reshape(1, bearings), prior_friction,
    )


def solution(mesh):
    count = mesh.shape["len"] * mesh.shape["xs"]
    along = P(None, None, None, AXES)
    in_specs = (along, P(None, None, AXES), P(), P(), P(), P())
    return jax.shard_map(
        functools.partial(shards, count), mesh=mesh,
        in_specs=in_specs, out_specs=(along, along, P()), check_vma=False,
    )
```

```python
import functools

import jax
import jax.numpy as jnp
from jax import lax
from jax.experimental import pallas as pl
from jax.experimental.pallas import tpu as pltpu
from jax.sharding import PartitionSpec as P

ITERS = 3
SHIFT = 6.5
BULK = 1.5
ELASTIC = 8.0
RADIUS = 4.0
VERTICAL = 5.0
STATIC = 0.6
KINETIC = 0.45

AXES = ("len", "xs")
LANES = 128
ROWS = 8
PAD = 8
EDGE = 16
HALF = EDGE // 2
BLOCKS = LANES // EDGE
PITCH = 3 * ROWS
CHUNK = 16
PIECE = 16
MARGINS = (6, 5, 5)
MOMENTS = 2 * ITERS
SPREAD = 8
HIGH = lax.Precision.HIGHEST
LIMIT = pltpu.CompilerParams(vmem_limit_bytes=32 * 1024 * 1024)


def turn(x, amount):
    return pltpu.roll(x, amount % LANES, x.ndim - 1)


def lane_iota(shape):
    return lax.broadcasted_iota(jnp.int32, shape, len(shape) - 1)


def loop(count, step, body, init):
    def several(i, carry):
        for j in range(step):
            carry = body(i * step + j, carry)
        return carry

    return lax.fori_loop(0, count // step, several, init)


def device_index():
    return lax.axis_index(AXES[0]) * lax.axis_size(AXES[1]) + lax.axis_index(AXES[1])


def clear_padding(ref, lead, depth, across):
    for slab in (0, depth + 1):
        ref[lead + (slab,)] = jnp.zeros((across + 2 * PAD, LANES), jnp.float32)
    blank = jnp.zeros((PAD, LANES), jnp.float32)
    for d in range(1, depth + 1):
        ref[lead + (d, slice(0, PAD))] = blank
        ref[lead + (d, slice(PAD + across, None))] = blank


def pack_kernel(right_hbm, mass_hbm, field, mass, packed, message_a, message_b, sems):
    depth, across = mass.shape[0], mass.shape[1]
    copies = [
        pltpu.make_async_copy(
            right_hbm.at[c], field.at[c, pl.ds(1, depth), pl.ds(PAD, across)], sems.at[c]
        )
        for c in range(3)
    ]
    copies.append(pltpu.make_async_copy(mass_hbm, mass, sems.at[3]))
    for copy in copies:
        copy.start()
    for c in range(3):
        clear_padding(field, (c,), depth, across)
    is_even = device_index() % 2 == 0
    lane = lane_iota((ROWS, LANES))
    block_of = lane // EDGE
    first_half = lane % EDGE < HALF
    for c in range(4):
        copies[c].wait()
        edges = []
        for d in range(depth):
            edge = None
            for b in range(across // ROWS):
                row = pl.ds(b * ROWS + (PAD if c < 3 else 0), ROWS)
                if c < 3:
                    tile = field[c, d + 1, row, :]
                else:
                    tile = mass[d, row, :] + (6.0 - SHIFT)
                    mass[d, row, :] = tile
                moved = turn(tile, EDGE * b + HALF)
                edge = moved if edge is None else jnp.where(block_of == b, moved, edge)
            packed[c, d] = edge
            edges.append(edge)
        for d in range(depth // 2):
            low, high = edges[d], edges[d + depth // 2]
            rightward = jnp.where(first_half, low, turn(high, HALF))
            leftward = jnp.where(first_half, turn(low, -HALF), high)
            message_a[c, d] = jnp.where(is_even, rightward, leftward)
            message_b[c, d] = jnp.where(is_even, leftward, rightward)


def folded(x):
    return sum(x[i : i + ROWS] for i in range(0, x.shape[0], ROWS))


def cyclic_step(source, mass, div, store, step, inner_source=None, inner_div=None):
    depth, across = mass.shape[0], mass.shape[1]
    chunks = range(0, across, CHUNK)
    block_of = lane_iota((ROWS, LANES)) // EDGE

    def pack(edge, r, tile):
        for i in range(0, CHUNK, ROWS):
            b = (r + i) // ROWS
            moved = turn(tile[i : i + ROWS], EDGE * b + HALF)
            edge = moved if edge is None else jnp.where(block_of == b, moved, edge)
        return edge

    def divergence(d, carry):
        edge, edge_div = None, None
        for r in chunks:
            here, up, down = (pl.ds(PAD + r + by, CHUNK) for by in (0, 1, -1))
            x = source[0, d + 1, here, :]
            w = turn(x, -1) - turn(x, 1)
            w = w + (source[1, d + 1, up, :] - source[1, d + 1, down, :])
            w = w + (source[2, d + 2, here, :] - source[2, d, here, :])
            w = w * (0.25 * BULK)
            div[d + 1, here, :] = w
            if inner_source is not None:
                edge = pack(edge, r, x)
            if inner_div is not None:
                edge_div = pack(edge_div, r, w)
        if inner_source is not None:
            inner_source[d] = edge
        if inner_div is not None:
            inner_div[d] = edge_div
        return carry

    loop(depth, step, divergence, 0)

    def image(d, carry):
        norm, cross, cross_rest = carry
        for r in chunks:
            here, up, down = (pl.ds(PAD + r + by, CHUNK) for by in (0, 1, -1))
            diag = mass[d, r : r + CHUNK, :]
            w = div[d + 1, here, :]
            norms, crosses = [], []
            for c in range(3):
                x = source[c, d + 1, here, :]
                if c == 0:
                    total = turn(x + w, -1) + turn(x - w, 1)
                else:
                    total = turn(x, -1) + turn(x, 1)
                if c == 1:
                    total = total + (div[d + 1, up, :] - div[d + 1, down, :])
                if c == 2:
                    total = total + (div[d + 2, here, :] - div[d, here, :])
                total = total + (source[c, d, here, :] + source[c, d + 2, here, :])
                total = total + (source[c, d + 1, up, :] + source[c, d + 1, down, :])
                out = diag * x - total
                store(c, d, r, out)
                norms.append(x * x)
                crosses.append(x * out)
            norm = norm + folded(norms[0] + norms[1] + norms[2])
            cross = cross + folded(crosses[0])
            cross_rest = cross_rest + folded(crosses[1] + crosses[2])
        return norm, cross, cross_rest

    return loop(depth, step, image, (jnp.zeros((ROWS, LANES), jnp.float32),) * 3)


def interior(value, margin):
    lane = lane_iota(value.shape)
    return jnp.where((lane >= margin) & (lane < LANES - margin), value, 0.0)


def cyclic_kernel(field, mass, spans, first, second, third, inner, moments, ends, div):
    depth, across = mass.shape[0], mass.shape[1]
    clear_padding(div, (), depth, across)
    for c in range(3):
        clear_padding(first, (c,), depth, across)
        clear_padding(second, (c,), depth, across)

    def store_first(c, d, r, out):
        first[c, d + 1, pl.ds(PAD + r, CHUNK), :] = out

    def store_second(c, d, r, out):
        second[c, d + 1, pl.ds(PAD + r, CHUNK), :] = out

    def store_third(c, d, r, out):
        third[c, d, r : r + CHUNK, :] = out

    norm, cross, cross_rest = cyclic_step(field, mass, div, store_first, 4)
    moments[0] = norm
    moments[1] = interior(cross + cross_rest, 2)
    norm, cross, cross_rest = cyclic_step(first, mass, div, store_second, 4, inner.at[0])
    moments[2] = interior(norm, 2)
    moments[3] = interior(cross + cross_rest, 4)
    norm, cross, cross_rest = cyclic_step(
        second, mass, div, store_third, 4, inner.at[1], inner.at[2]
    )
    moments[4] = interior(norm, 4)
    moments[5] = interior(cross, MARGINS[0]) + interior(cross_rest, MARGINS[1])
    piers = spans.shape[1]
    bearings = 2 * piers
    lane = lane_iota((piers, LANES))
    pier = lax.broadcasted_iota(jnp.int32, (piers, LANES), 0)
    lengths = jnp.broadcast_to(spans[...].astype(jnp.float32), (ROWS, piers))
    for z in range(ends.shape[0]):
        bearing = lane - z * bearings if bearings <= LANES else lane + z * LANES
        upto = jnp.where(pier * 2 <= bearing, 1.0, 0.0)
        total = jnp.dot(lengths, upto, precision=HIGH, preferred_element_type=jnp.float32)
        inside = (bearing[0:1] >= 0) & (bearing[0:1] < bearings)
        ends[z : z + 1, :] = jnp.where(inside, total[0:1] - 1.0, -1e9)


def mended(value, edges, row, margin):
    moved = [
        turn(edges, -(EDGE * ((row + i) // ROWS) + HALF)) for i in range(0, value.shape[0], ROWS)
    ]
    spot = lane_iota(value.shape)
    return jnp.where(
        (spot < margin) | (spot >= LANES - margin),
        moved[0] if len(moved) == 1 else jnp.concatenate(moved, axis=0),
        value,
    )


def edge_kernel(
    per, packed, got_a, got_b, inner, field, first, second, early, ends,
    fix_first, fix_second, fix_third, payload,
    edges, edge_div, edge_diag, sums, picked,
):
    depth, across = packed.shape[1], first.shape[2] - 2 * PAD
    index = device_index()
    count = lax.axis_size(AXES[0]) * lax.axis_size(AXES[1])
    is_even = index % 2 == 0
    lane = lane_iota((ROWS, LANES))
    first_half = lane % EDGE < HALF
    ones = jnp.ones((ROWS, LANES), jnp.float32)
    keep = (
        jnp.where(first_half & (index == 0), 0.0, ones),
        jnp.where(jnp.logical_not(first_half) & (index == count - 1), 0.0, ones),
    )
    both = range(2)
    comps = range(3)
    half = depth // 2
    blank = jnp.zeros((ROWS, LANES), jnp.float32)

    def row_of(d):
        return (d + 1) * PITCH + ROWS

    for c in range(4):
        for d in range(half):
            a, b = got_a[c, d], got_b[c, d]
            from_left = jnp.where(is_even, b, a)
            from_right = jnp.where(is_even, a, b)
            low, high = packed[c, d], packed[c, d + half]
            for at, left, right in (
                (
                    d,
                    jnp.where(first_half, from_left, low),
                    jnp.where(first_half, low, turn(from_right, HALF)),
                ),
                (
                    d + half,
                    jnp.where(first_half, turn(from_left, -HALF), high),
                    jnp.where(first_half, high, from_right),
                ),
            ):
                if c < 3:
                    edges[0, 0, c, pl.ds(row_of(at), ROWS), :] = left
                    edges[0, 1, c, pl.ds(row_of(at), ROWS), :] = right
                else:
                    edge_diag[0, at] = left
                    edge_diag[1, at] = right
    for s in both:
        for c in comps:
            for buffer in both:
                edges[buffer, s, c, pl.ds(ROWS, ROWS), :] = blank
                edges[buffer, s, c, pl.ds(row_of(depth), ROWS), :] = blank
        edge_div[s, pl.ds(ROWS, ROWS), :] = blank
        edge_div[s, pl.ds(row_of(depth), ROWS), :] = blank

    def join_blocks(ref, lead):
        for d in (0, half):
            base = row_of(d)
            last = ref[lead + (pl.ds(base + ROWS - 1, half, stride=PITCH), slice(None))]
            ahead = ref[lead + (pl.ds(base, half, stride=PITCH), slice(None))]
            spot = lane_iota((half, LANES))
            ref[lead + (pl.ds(base - 1, half, stride=PITCH), slice(None))] = jnp.where(
                spot >= EDGE, turn(last, EDGE), 0.0
            )
            ref[lead + (pl.ds(base + ROWS, half, stride=PITCH), slice(None))] = jnp.where(
                spot < LANES - EDGE, turn(ahead, -EDGE), 0.0
            )

    def div_at(s, d, by=0):
        return edge_div[s, pl.ds(row_of(d) + by, ROWS), :]

    def middle(value, margin):
        spot = lane % EDGE
        return jnp.where((spot >= HALF - margin) & (spot < HALF + margin), value, 0.0)

    fixes = (packed, fix_first, fix_second, fix_third)
    last_planes = lane % EDGE >= EDGE - 2
    first_planes = lane % EDGE < 2

    def joined(s, value, own):
        return jnp.where(first_planes if s else last_planes, own, value)

    def edge_step(level):
        edge, target = edges.at[level % 2], edges.at[(level + 1) % 2]

        def at(s, c, d, by=0):
            return edge[s, c, pl.ds(row_of(d) + by, ROWS), :]

        for s in both:
            for c in comps:
                join_blocks(edge, (s, c))
        for s in both:
            for d in range(depth):
                x = at(s, 0, d)
                w = turn(x, -1) - turn(x, 1)
                w = w + (at(s, 1, d, 1) - at(s, 1, d, -1))
                w = w + (at(s, 2, d + 1) - at(s, 2, d - 1))
                w = w * ((0.25 * BULK) * keep[s])
                edge_div[s, pl.ds(row_of(d), ROWS), :] = joined(s, w, inner[2, d]) if level == 2 else w
            join_blocks(edge_div, (s,))
        norms, crosses = [], []
        for c in comps:
            norm, cross = blank, blank
            for d in range(depth):
                pair = []
                for s in both:
                    x = at(s, c, d)
                    if c == 0:
                        w = div_at(s, d)
                        total = turn(x + w, -1) + turn(x - w, 1)
                    else:
                        total = turn(x, -1) + turn(x, 1)
                    if c == 1:
                        total = total + (div_at(s, d, 1) - div_at(s, d, -1))
                    if c == 2:
                        total = total + (div_at(s, d + 1) - div_at(s, d - 1))
                    total = total + (at(s, c, d - 1) + at(s, c, d + 1))
                    total = total + (at(s, c, d, 1) + at(s, c, d, -1))
                    image = (edge_diag[s, d] * x - total) * keep[s]
                    pair.append(image)
                    if level + 1 < ITERS:
                        image = image if c else joined(s, image, inner[level, d])
                        target[s, c, pl.ds(row_of(d), ROWS), :] = image
                old = fixes[level][c, d]
                new = jnp.where(first_half, pair[1], pair[0])
                fixes[level + 1][c, d] = new
                if level:
                    norm = norm + old * old
                cross = cross + old * new
            norms.append(norm)
            crosses.append(cross)
        return norms, crosses

    edge_sums = [edge_step(level) for level in range(ITERS)]

    variants = ends.shape[0]
    pieces = 1 if per > 1 else variants
    blocks = 3 * ITERS * pieces
    bearing_rows = -(-blocks // per)
    picked[...] = jnp.zeros(picked.shape, jnp.float32)
    for block in range(blocks):
        value, piece = block // pieces, block % pieces
        row, z = block // per, (block % per if per > 1 else piece)
        level, c = value // 3, value % 3
        for side in both:
            place = (1 + 2 * side) * across // 4
            column = (2 * z + side) * LANES
            here = (field, first, second)[level][c, 1, PAD + place : PAD + place + 1, :]
            if level:
                edges = fixes[level][c, 0, place % ROWS : place % ROWS + 1, :]
                here = mended(here, edges, place, 2 * level)
            picked[row : row + 1, column : column + LANES] = here
    start = (index * LANES).astype(jnp.float32)
    along = lax.broadcasted_iota(jnp.int32, (LANES, LANES), 0).astype(jnp.float32) + start
    parity = lane_iota((LANES, LANES)) % 2
    total = jnp.zeros((picked.shape[0], LANES), jnp.float32)
    for z in range(variants):
        site = jnp.broadcast_to(ends[z : z + 1, :], (LANES, LANES)) == along
        for side in both:
            column = (2 * z + side) * LANES
            hit = jnp.where(site & (parity == side), 1.0, 0.0)
            total = total + jnp.dot(
                picked[:, column : column + LANES], hit,
                precision=HIGH, preferred_element_type=jnp.float32,
            )

    def at_edge(values, margins):
        return sum(middle(v, m) for v, m in zip(values, margins))

    parts = [
        early[0],
        early[1] + at_edge(edge_sums[0][1], (2, 2, 2)),
        early[2] + at_edge(edge_sums[1][0], (2, 2, 2)),
        early[3] + at_edge(edge_sums[1][1], (4, 4, 4)),
        early[4] + at_edge(edge_sums[2][0], (4, 4, 4)),
        early[5] + at_edge(edge_sums[2][1], MARGINS),
    ]

    sums[...] = jnp.zeros(sums.shape, jnp.float32)
    sums[0:bearing_rows, :] = total[0:bearing_rows]
    flat = jnp.concatenate(
        [jnp.sum(part, axis=0, keepdims=True) for part in parts]
        + [jnp.zeros((ROWS - MOMENTS, LANES), jnp.float32)],
        axis=0,
    )
    amount = LANES // 2
    while amount >= SPREAD:
        flat = flat + turn(flat, amount)
        amount //= 2
    row, first_lane = divmod(blocks * (LANES // per), LANES)
    number = lax.broadcasted_iota(jnp.int32, (ROWS, LANES), 0)
    held = lane // SPREAD == number + first_lane // SPREAD
    flat = jnp.sum(jnp.where(held & (number < MOMENTS), flat, 0.0), axis=0, keepdims=True)
    sums[row : row + 1, :] = sums[row : row + 1, :] + flat
    out = jnp.concatenate(
        [sums[row : row + 1, :] for row in range(payload.shape[2] // LANES)], axis=1
    )
    for device in range(payload.shape[0]):
        payload[device] = out


def added(parts):
    while len(parts) > 1:
        parts = [sum(parts[i + 1 : i + 2], parts[i]) for i in range(0, len(parts), 2)]
    return parts[0]


def two_sum(a, b):
    total = a + b
    part = total - a
    return total, (a - (total - part)) + (b - part)


def high_half(x):
    scaled = 4097.0 * x
    return scaled - (scaled - x)


def less_multiple(a, theta, b):
    upper = high_half(b[0])
    high, error = two_sum(a[0], -theta * upper)
    high, more = two_sum(high, -theta * (b[0] - upper))
    low = (error + more) + (a[1] - theta * b[1])
    total = high + low
    return total, low - (total - high)


def exact_sums(sent, first_lane):
    number = lane_iota(sent[0].shape) // SPREAD - first_lane // SPREAD

    def sums(row):
        return [
            jnp.sum(jnp.where(number == n, row, 0.0), axis=1, keepdims=True)
            for n in range(MOMENTS)
        ]

    bound = jnp.zeros_like(sent[0])
    for n, total in enumerate(sums(added([jnp.abs(x) for x in sent]))):
        bound = jnp.where(number == n, 2.0 * total, bound)
    upper = [(x + bound) - bound for x in sent]
    lower = [x - u for x, u in zip(sent, upper)]
    return list(zip(sums(added(upper)), sums(added(lower))))


def centred(moments):
    theta = high_half(moments[1][0] / moments[0][0])
    moments = list(moments)
    for first in range(1, MOMENTS):
        for n in range(MOMENTS - 1, first - 1, -1):
            moments[n] = less_multiple(moments[n], theta, moments[n - 1])
    return theta, [high + low for high, low in moments]


def expanded(terms, theta):
    out = [terms[-1]]
    for term in terms[-2::-1]:
        out = (
            [term - theta * out[0]]
            + [out[i] - theta * out[i + 1] for i in range(len(out) - 1)]
            + [out[-1]]
        )
    return out


def coefficients(moment, shift):
    def dot(a, b):
        total = None
        for i, left in enumerate(a):
            for j, right in enumerate(b):
                term = left * right * moment[i + j]
                total = term if total is None else total + term
        return total

    one = jnp.ones_like(moment[0])
    solved, direction, increment = [one], [one], []
    norm = moment[0]
    for iteration in range(ITERS):
        image = [shift * p for p in direction] + [jnp.zeros_like(one)]
        for i, p in enumerate(direction):
            image[i + 1] = image[i + 1] + p
        alpha = norm / dot(direction, image)
        increment = [
            alpha * p + (increment[i] if i < len(increment) else 0.0) for i, p in enumerate(direction)
        ]
        solved = [
            (solved[i] if i < len(solved) else 0.0) - alpha * q for i, q in enumerate(image)
        ]
        if iteration + 1 < ITERS:
            after = dot(solved, solved)
            ratio = after / norm
            direction = [
                s + (ratio * direction[i] if i < len(direction) else 0.0)
                for i, s in enumerate(solved)
            ]
            norm = after
    return increment, solved


def combine_kernel(
    per, gathered, field, first, second, third, packed, fix_first, fix_second, fix_third,
    ends, stick, load, prior,
    increment_hbm, residual_hbm, friction_hbm,
    increment, residual, friction, forces, sems, friction_sem,
):
    depth, across = third.shape[1], third.shape[2]
    start = (device_index() * LANES).astype(jnp.float32)
    bearings = load.shape[1]
    variants = ends.shape[0]
    pieces = 1 if per > 1 else variants
    width = min(bearings, LANES)
    blocks = 3 * ITERS * pieces
    row, first_lane = divmod(blocks * (LANES // per), LANES)
    received = [gathered[device] for device in range(gathered.shape[0])]
    sent = [x[:, row * LANES : (row + 1) * LANES] for x in received]
    theta, moments = centred(exact_sums(sent, first_lane))
    grow, keep = (
        expanded(terms, theta) for terms in coefficients(moments, SHIFT + theta)
    )
    total = added(received)

    forces[...] = jnp.zeros(forces.shape, jnp.float32)
    lane = lane_iota((1, width))
    for piece in range(pieces):
        span = slice(piece * LANES, piece * LANES + width)
        readout = []
        for c in range(3):
            value = None
            for k in range(ITERS):
                block = (3 * k + c) * pieces + piece
                row = total[:, block // per * LANES : (block // per + 1) * LANES]
                if per > 1 and block % per:
                    row = turn(row, LANES - (block % per) * bearings)
                term = grow[k] * row[:, :width]
                value = term if value is None else value + term
            readout.append(value)
        weight = load[:, span]
        radius = jnp.where(stick[:, span] == 1, STATIC, KINETIC) * weight
        trial = [prior[c : c + 1, span] + ELASTIC * readout[c] for c in range(2)]
        magnitude = jnp.sqrt(trial[0] * trial[0] + trial[1] * trial[1])
        scale = radius / jnp.maximum(magnitude, radius)
        held = [t * scale for t in trial]
        for c in range(2):
            friction[c : c + 1, span] = held[c]
        force = [held[c] + weight / RADIUS * readout[c] for c in range(2)] + [VERTICAL * readout[2]]
        for c in range(3):
            for side in range(2):
                forces[2 * c + side : 2 * c + side + 1, span] = jnp.where(
                    lane % 2 == side, force[c], 0.0
                )
    friction_copy = pltpu.make_async_copy(friction, friction_hbm, friction_sem)
    friction_copy.start()
    along = lax.broadcasted_iota(jnp.int32, (LANES, LANES), 0).astype(jnp.float32) + start
    placed = jnp.zeros((8, LANES), jnp.float32)
    for piece in range(pieces):
        site = jnp.broadcast_to(ends[piece : piece + 1, :], (LANES, LANES)) == along
        placed = placed + lax.dot_general(
            forces[:, piece * LANES : (piece + 1) * LANES], jnp.where(site, 1.0, 0.0),
            (((1,), (1,)), ((), ())), precision=HIGH, preferred_element_type=jnp.float32,
        )

    grow = [jnp.broadcast_to(g, (ROWS, LANES)) for g in grow]
    keep = [jnp.broadcast_to(g, (ROWS, LANES)) for g in keep]

    def total_of(terms, values):
        parts = [t * v for t, v in zip(terms, values)]
        return parts[0] + parts[1] + (parts[2] if len(parts) == 3 else parts[2] + parts[3])

    def run(c, begin, end):
        for d in range(begin, end):
            edges = [ref[c, d] for ref in (packed, fix_first, fix_second, fix_third)]
            edges = total_of(grow, edges), total_of(keep, edges)
            for r in range(0, across, ROWS):
                here = pl.ds(PAD + r, ROWS)
                v = [ref[c, d + 1, here, :] for ref in (field, first, second)]
                v.append(third[c, d, r : r + ROWS, :])
                for ref, terms, edge in ((increment, grow, edges[0]), (residual, keep, edges[1])):
                    ref[c, d, r : r + ROWS, :] = mended(total_of(terms, v), edge, r, MARGINS[c])

    def copy(which, c, begin):
        ref, hbm = ((increment, increment_hbm), (residual, residual_hbm))[which]
        part = pl.ds(begin, PIECE)
        return pltpu.make_async_copy(
            ref.at[c, part], hbm.at[c, part], sems.at[which, c, begin // PIECE]
        )

    starts = range(0, depth, PIECE)
    for c in range(3):
        for begin in starts:
            run(c, begin, begin + PIECE)
            if begin == 0:
                for side in range(2):
                    at = (1 + 2 * side) * across // 4
                    residual[c, 0, at : at + 1, :] = (
                        residual[c, 0, at : at + 1, :] - placed[2 * c + side : 2 * c + side + 1]
                    )
            for which in range(2):
                copy(which, c, begin).start()
    friction_copy.wait()
    for c in range(3):
        for begin in starts:
            for which in range(2):
                copy(which, c, begin).wait()


def vmem_spec():
    return pl.BlockSpec(memory_space=pltpu.VMEM)


def hbm_spec():
    return pl.BlockSpec(memory_space=pltpu.HBM)


def pack_call(right_side, mass_field):
    f32 = jnp.float32
    depth, across, along = mass_field.shape
    half = depth // 2
    return pl.pallas_call(
        pack_kernel,
        out_shape=(
            pltpu.VMEM((3, depth + 2, across + 2 * PAD, along), f32),
            pltpu.VMEM((depth, across, along), f32),
            pltpu.VMEM((4, depth, ROWS, LANES), f32),
            jax.ShapeDtypeStruct((4, half, ROWS, LANES), f32),
            jax.ShapeDtypeStruct((4, half, ROWS, LANES), f32),
        ),
        in_specs=[hbm_spec()] * 2,
        out_specs=(vmem_spec(),) * 5,
        scratch_shapes=[pltpu.SemaphoreType.DMA((4,))],
        compiler_params=LIMIT,
        name="pack",
    )(
        pltpu.with_memory_space_constraint(right_side, pltpu.HBM),
        pltpu.with_memory_space_constraint(mass_field, pltpu.HBM),
    )


def cyclic_call(field, mass, spans, variants):
    f32 = jnp.float32
    depth, across, along = mass.shape
    padded = (depth + 2, across + 2 * PAD, along)
    return pl.pallas_call(
        cyclic_kernel,
        out_shape=(
            pltpu.VMEM((3,) + padded, f32),
            pltpu.VMEM((3,) + padded, f32),
            pltpu.VMEM((3, depth, across, along), f32),
            pltpu.VMEM((3, depth, ROWS, LANES), f32),
            pltpu.VMEM((6, ROWS, LANES), f32),
            pltpu.VMEM((variants, LANES), f32),
        ),
        in_specs=[vmem_spec()] * 3,
        out_specs=(vmem_spec(),) * 6,
        scratch_shapes=[pltpu.VMEM(padded, f32)],
        compiler_params=LIMIT,
        cost_estimate=pl.CostEstimate(flops=60_000_000, bytes_accessed=12_000_000, transcendentals=0),
        name="cyclic",
    )(field, mass, spans)


def edge_call(per, rows, packed, got_a, got_b, inner, field, first, second, early, ends, count):
    f32 = jnp.float32
    depth = packed.shape[1]
    variants = ends.shape[0]
    edges = (3, depth, ROWS, LANES)
    tall = -(-rows // ROWS) * ROWS
    return pl.pallas_call(
        functools.partial(edge_kernel, per),
        out_shape=(pltpu.VMEM(edges, f32),) * 3 + (pltpu.VMEM((count, 1, rows * LANES), f32),),
        in_specs=[vmem_spec()] * 9,
        out_specs=(vmem_spec(),) * 4,
        scratch_shapes=[
            pltpu.VMEM((2, 2, 3, (depth + 2) * PITCH, LANES), f32),
            pltpu.VMEM((2, (depth + 2) * PITCH, LANES), f32),
            pltpu.VMEM((2, depth, ROWS, LANES), f32),
            pltpu.VMEM((tall, LANES), f32),
            pltpu.VMEM((tall, 2 * variants * LANES), f32),
        ],
        compiler_params=LIMIT,
        name="edge",
    )(packed, got_a, got_b, inner, field, first, second, early, ends)


def combine_call(per, gathered, field, first, second, third, edges, ends, stick, load, prior):
    f32 = jnp.float32
    shape = third.shape
    bearings = load.shape[1]
    return pl.pallas_call(
        functools.partial(combine_kernel, per),
        out_shape=(
            jax.ShapeDtypeStruct(shape, f32),
            jax.ShapeDtypeStruct(shape, f32),
            jax.ShapeDtypeStruct((2, bearings), f32),
        ),
        in_specs=[vmem_spec()] * 13,
        out_specs=(hbm_spec(),) * 3,
        scratch_shapes=[
            pltpu.VMEM(shape, f32),
            pltpu.VMEM(shape, f32),
            pltpu.VMEM((2, bearings), f32),
            pltpu.VMEM((ROWS, max(bearings, LANES)), f32),
            pltpu.SemaphoreType.DMA((2, 3, shape[1] // PIECE)),
            pltpu.SemaphoreType.DMA(()),
        ],
        compiler_params=LIMIT,
        name="combine",
    )(gathered, field, first, second, third, *edges, ends, stick, load, prior)


def shards(count, right_side, mass_field, span_lengths, stick_flags, normal_load, prior_friction):
    piers = span_lengths.shape[0]
    bearings = 2 * piers
    per = LANES // bearings if bearings <= LANES else 1
    variants = per if bearings <= LANES else bearings // LANES
    pieces = 1 if per > 1 else variants
    sent = 3 * ITERS * pieces * (LANES // per) + MOMENTS * SPREAD
    rows = -(-sent // LANES)

    field, mass, packed, message_a, message_b = pack_call(right_side, mass_field)
    pairs_a = [p for i in range(0, count - 1, 2) for p in ((i, i + 1), (i + 1, i))]
    pairs_b = [p for i in range(1, count - 1, 2) for p in ((i, i + 1), (i + 1, i))]
    got_a = lax.ppermute(message_a, AXES, pairs_a)
    got_b = lax.ppermute(message_b, AXES, pairs_b)
    first, second, third, inner, early, ends = cyclic_call(
        field, mass, span_lengths.reshape(1, piers), variants
    )
    *fixes, payload = edge_call(
        per, rows, packed, got_a, got_b, inner, field, first, second, early, ends, count
    )
    gathered = lax.all_to_all(payload, AXES, 0, 0, tiled=True)
    return combine_call(
        per, gathered, field, first, second, third, (packed, *fixes), ends,
        stick_flags.reshape(1, bearings), normal_load.reshape(1, bearings), prior_friction,
    )


def solution(mesh):
    count = mesh.shape["len"] * mesh.shape["xs"]
    along = P(None, None, None, AXES)
    in_specs = (along, P(None, None, AXES), P(), P(), P(), P())
    return jax.shard_map(
        functools.partial(shards, count), mesh=mesh,
        in_specs=in_specs, out_specs=(along, along, P()), check_vma=False,
    )
```

```python
import functools

import jax
import jax.numpy as jnp
from jax import lax
from jax.experimental import pallas as pl
from jax.experimental.pallas import tpu as pltpu
from jax.sharding import PartitionSpec as P

ITERS = 3
SHIFT = 6.5
BULK = 1.5
ELASTIC = 8.0
RADIUS = 4.0
VERTICAL = 5.0
STATIC = 0.6
KINETIC = 0.45

AXES = ("len", "xs")
LANES = 128
ROWS = 8
PAD = 8
EDGE = 16
HALF = EDGE // 2
BLOCKS = LANES // EDGE
PITCH = 3 * ROWS
CHUNK = 16
PIECE = 16
MARGINS = (6, 5, 5)
MOMENTS = 2 * ITERS
SPREAD = 8
HIGH = lax.Precision.HIGHEST
LIMIT = pltpu.CompilerParams(vmem_limit_bytes=32 * 1024 * 1024)


def turn(x, amount):
    return pltpu.roll(x, amount % LANES, x.ndim - 1)


def lane_iota(shape):
    return lax.broadcasted_iota(jnp.int32, shape, len(shape) - 1)


def loop(count, step, body, init):
    def several(i, carry):
        for j in range(step):
            carry = body(i * step + j, carry)
        return carry

    return lax.fori_loop(0, count // step, several, init)


def device_index():
    return lax.axis_index(AXES[0]) * lax.axis_size(AXES[1]) + lax.axis_index(AXES[1])


def clear_padding(ref, lead, depth, across):
    for slab in (0, depth + 1):
        ref[lead + (slab,)] = jnp.zeros((across + 2 * PAD, LANES), jnp.float32)
    blank = jnp.zeros((PAD, LANES), jnp.float32)
    for d in range(1, depth + 1):
        ref[lead + (d, slice(0, PAD))] = blank
        ref[lead + (d, slice(PAD + across, None))] = blank


def pack_kernel(right_hbm, mass_hbm, field, mass, packed, message_a, message_b, sems):
    depth, across = mass.shape[0], mass.shape[1]
    copies = [
        pltpu.make_async_copy(
            right_hbm.at[c], field.at[c, pl.ds(1, depth), pl.ds(PAD, across)], sems.at[c]
        )
        for c in range(3)
    ]
    copies.append(pltpu.make_async_copy(mass_hbm, mass, sems.at[3]))
    for copy in copies:
        copy.start()
    for c in range(3):
        clear_padding(field, (c,), depth, across)
    is_even = device_index() % 2 == 0
    lane = lane_iota((ROWS, LANES))
    block_of = lane // EDGE
    first_half = lane % EDGE < HALF
    for c in range(4):
        copies[c].wait()
        edges = []
        for d in range(depth):
            edge = None
            for b in range(across // ROWS):
                row = pl.ds(b * ROWS + (PAD if c < 3 else 0), ROWS)
                if c < 3:
                    tile = field[c, d + 1, row, :]
                else:
                    tile = mass[d, row, :] + (6.0 - SHIFT)
                    mass[d, row, :] = tile
                moved = turn(tile, EDGE * b + HALF)
                edge = moved if edge is None else jnp.where(block_of == b, moved, edge)
            packed[c, d] = edge
            edges.append(edge)
        for d in range(depth // 2):
            low, high = edges[d], edges[d + depth // 2]
            rightward = jnp.where(first_half, low, turn(high, HALF))
            leftward = jnp.where(first_half, turn(low, -HALF), high)
            message_a[c, d] = jnp.where(is_even, rightward, leftward)
            message_b[c, d] = jnp.where(is_even, leftward, rightward)


def folded(x):
    return sum(x[i : i + ROWS] for i in range(0, x.shape[0], ROWS))


def cyclic_step(source, mass, div, store, step, inner_source=None, inner_div=None):
    depth, across = mass.shape[0], mass.shape[1]
    chunks = range(0, across, CHUNK)
    block_of = lane_iota((ROWS, LANES)) // EDGE

    def pack(edge, r, tile):
        for i in range(0, CHUNK, ROWS):
            b = (r + i) // ROWS
            moved = turn(tile[i : i + ROWS], EDGE * b + HALF)
            edge = moved if edge is None else jnp.where(block_of == b, moved, edge)
        return edge

    def divergence(d, carry):
        edge, edge_div = None, None
        for r in chunks:
            here, up, down = (pl.ds(PAD + r + by, CHUNK) for by in (0, 1, -1))
            x = source[0, d + 1, here, :]
            w = turn(x, -1) - turn(x, 1)
            w = w + (source[1, d + 1, up, :] - source[1, d + 1, down, :])
            w = w + (source[2, d + 2, here, :] - source[2, d, here, :])
            w = w * (0.25 * BULK)
            div[d + 1, here, :] = w
            if inner_source is not None:
                edge = pack(edge, r, x)
            if inner_div is not None:
                edge_div = pack(edge_div, r, w)
        if inner_source is not None:
            inner_source[d] = edge
        if inner_div is not None:
            inner_div[d] = edge_div
        return carry

    loop(depth, step, divergence, 0)

    def image(d, carry):
        norm, cross, cross_rest = carry
        for r in chunks:
            here, up, down = (pl.ds(PAD + r + by, CHUNK) for by in (0, 1, -1))
            diag = mass[d, r : r + CHUNK, :]
            w = div[d + 1, here, :]
            norms, crosses = [], []
            for c in range(3):
                x = source[c, d + 1, here, :]
                if c == 0:
                    total = turn(x + w, -1) + turn(x - w, 1)
                else:
                    total = turn(x, -1) + turn(x, 1)
                if c == 1:
                    total = total + (div[d + 1, up, :] - div[d + 1, down, :])
                if c == 2:
                    total = total + (div[d + 2, here, :] - div[d, here, :])
                total = total + (source[c, d, here, :] + source[c, d + 2, here, :])
                total = total + (source[c, d + 1, up, :] + source[c, d + 1, down, :])
                out = diag * x - total
                store(c, d, r, out)
                norms.append(x * x)
                crosses.append(x * out)
            norm = norm + folded(norms[0] + norms[1] + norms[2])
            cross = cross + folded(crosses[0])
            cross_rest = cross_rest + folded(crosses[1] + crosses[2])
        return norm, cross, cross_rest

    return loop(depth, step, image, (jnp.zeros((ROWS, LANES), jnp.float32),) * 3)


def interior(value, margin):
    lane = lane_iota(value.shape)
    return jnp.where((lane >= margin) & (lane < LANES - margin), value, 0.0)


def cyclic_kernel(field, mass, spans, first, second, third, inner, moments, ends, div):
    depth, across = mass.shape[0], mass.shape[1]
    clear_padding(div, (), depth, across)
    for c in range(3):
        clear_padding(first, (c,), depth, across)
        clear_padding(second, (c,), depth, across)

    def store_first(c, d, r, out):
        first[c, d + 1, pl.ds(PAD + r, CHUNK), :] = out

    def store_second(c, d, r, out):
        second[c, d + 1, pl.ds(PAD + r, CHUNK), :] = out

    def store_third(c, d, r, out):
        third[c, d, r : r + CHUNK, :] = out

    norm, cross, cross_rest = cyclic_step(field, mass, div, store_first, 4)
    moments[0] = norm
    moments[1] = interior(cross + cross_rest, 2)
    norm, cross, cross_rest = cyclic_step(first, mass, div, store_second, 4, inner.at[0])
    moments[2] = interior(norm, 2)
    moments[3] = interior(cross + cross_rest, 4)
    norm, cross, cross_rest = cyclic_step(
        second, mass, div, store_third, 4, inner.at[1], inner.at[2]
    )
    moments[4] = interior(norm, 4)
    moments[5] = interior(cross, MARGINS[0]) + interior(cross_rest, MARGINS[1])
    piers = spans.shape[1]
    bearings = 2 * piers
    lane = lane_iota((piers, LANES))
    pier = lax.broadcasted_iota(jnp.int32, (piers, LANES), 0)
    lengths = jnp.broadcast_to(spans[...].astype(jnp.float32), (ROWS, piers))
    for z in range(ends.shape[0]):
        bearing = lane - z * bearings if bearings <= LANES else lane + z * LANES
        upto = jnp.where(pier * 2 <= bearing, 1.0, 0.0)
        total = jnp.dot(lengths, upto, precision=HIGH, preferred_element_type=jnp.float32)
        inside = (bearing[0:1] >= 0) & (bearing[0:1] < bearings)
        ends[z : z + 1, :] = jnp.where(inside, total[0:1] - 1.0, -1e9)


def mended(value, edges, row, margin):
    moved = [
        turn(edges, -(EDGE * ((row + i) // ROWS) + HALF)) for i in range(0, value.shape[0], ROWS)
    ]
    spot = lane_iota(value.shape)
    return jnp.where(
        (spot < margin) | (spot >= LANES - margin),
        moved[0] if len(moved) == 1 else jnp.concatenate(moved, axis=0),
        value,
    )


def edge_kernel(
    per, packed, got_b, got_a, inner, field, first, second, early, ends,
    fix_first, fix_second, fix_third, payload,
    edges, edge_div, edge_diag, sums, picked,
):
    depth, across = packed.shape[1], first.shape[2] - 2 * PAD
    index = device_index()
    count = lax.axis_size(AXES[0]) * lax.axis_size(AXES[1])
    is_even = index % 2 == 0
    lane = lane_iota((ROWS, LANES))
    first_half = lane % EDGE < HALF
    ones = jnp.ones((ROWS, LANES), jnp.float32)
    keep = (
        jnp.where(first_half & (index == 0), 0.0, ones),
        jnp.where(jnp.logical_not(first_half) & (index == count - 1), 0.0, ones),
    )
    both = range(2)
    comps = range(3)
    half = depth // 2
    blank = jnp.zeros((ROWS, LANES), jnp.float32)

    def row_of(d):
        return (d + 1) * PITCH + ROWS

    for c in range(4):
        for d in range(half):
            a, b = got_a[c, d], got_b[c, d]
            from_left = jnp.where(is_even, b, a)
            from_right = jnp.where(is_even, a, b)
            low, high = packed[c, d], packed[c, d + half]
            for at, left, right in (
                (
                    d,
                    jnp.where(first_half, from_left, low),
                    jnp.where(first_half, low, turn(from_right, HALF)),
                ),
                (
                    d + half,
                    jnp.where(first_half, turn(from_left, -HALF), high),
                    jnp.where(first_half, high, from_right),
                ),
            ):
                if c < 3:
                    edges[0, 0, c, pl.ds(row_of(at), ROWS), :] = left
                    edges[0, 1, c, pl.ds(row_of(at), ROWS), :] = right
                else:
                    edge_diag[0, at] = left
                    edge_diag[1, at] = right
    for s in both:
        for c in comps:
            for buffer in both:
                edges[buffer, s, c, pl.ds(ROWS, ROWS), :] = blank
                edges[buffer, s, c, pl.ds(row_of(depth), ROWS), :] = blank
        edge_div[s, pl.ds(ROWS, ROWS), :] = blank
        edge_div[s, pl.ds(row_of(depth), ROWS), :] = blank

    def join_blocks(ref, lead):
        for d in (0, half):
            base = row_of(d)
            last = ref[lead + (pl.ds(base + ROWS - 1, half, stride=PITCH), slice(None))]
            ahead = ref[lead + (pl.ds(base, half, stride=PITCH), slice(None))]
            spot = lane_iota((half, LANES))
            ref[lead + (pl.ds(base - 1, half, stride=PITCH), slice(None))] = jnp.where(
                spot >= EDGE, turn(last, EDGE), 0.0
            )
            ref[lead + (pl.ds(base + ROWS, half, stride=PITCH), slice(None))] = jnp.where(
                spot < LANES - EDGE, turn(ahead, -EDGE), 0.0
            )

    def div_at(s, d, by=0):
        return edge_div[s, pl.ds(row_of(d) + by, ROWS), :]

    def middle(value, margin):
        spot = lane % EDGE
        return jnp.where((spot >= HALF - margin) & (spot < HALF + margin), value, 0.0)

    fixes = (packed, fix_first, fix_second, fix_third)
    last_planes = lane % EDGE >= EDGE - 2
    first_planes = lane % EDGE < 2

    def joined(s, value, own):
        return jnp.where(first_planes if s else last_planes, own, value)

    def edge_step(level):
        edge, target = edges.at[level % 2], edges.at[(level + 1) % 2]

        def at(s, c, d, by=0):
            return edge[s, c, pl.ds(row_of(d) + by, ROWS), :]

        for s in both:
            for c in comps:
                join_blocks(edge, (s, c))
        for s in both:
            for d in range(depth):
                x = at(s, 0, d)
                w = turn(x, -1) - turn(x, 1)
                w = w + (at(s, 1, d, 1) - at(s, 1, d, -1))
                w = w + (at(s, 2, d + 1) - at(s, 2, d - 1))
                w = w * ((0.25 * BULK) * keep[s])
                edge_div[s, pl.ds(row_of(d), ROWS), :] = joined(s, w, inner[2, d]) if level == 2 else w
            join_blocks(edge_div, (s,))
        norms, crosses = [], []
        for c in comps:
            norm, cross = blank, blank
            for d in range(depth):
                pair = []
                for s in both:
                    x = at(s, c, d)
                    if c == 0:
                        w = div_at(s, d)
                        total = turn(x + w, -1) + turn(x - w, 1)
                    else:
                        total = turn(x, -1) + turn(x, 1)
                    if c == 1:
                        total = total + (div_at(s, d, 1) - div_at(s, d, -1))
                    if c == 2:
                        total = total + (div_at(s, d + 1) - div_at(s, d - 1))
                    total = total + (at(s, c, d - 1) + at(s, c, d + 1))
                    total = total + (at(s, c, d, 1) + at(s, c, d, -1))
                    image = (edge_diag[s, d] * x - total) * keep[s]
                    pair.append(image)
                    if level + 1 < ITERS:
                        image = image if c else joined(s, image, inner[level, d])
                        target[s, c, pl.ds(row_of(d), ROWS), :] = image
                old = fixes[level][c, d]
                new = jnp.where(first_half, pair[1], pair[0])
                fixes[level + 1][c, d] = new
                if level:
                    norm = norm + old * old
                cross = cross + old * new
            norms.append(norm)
            crosses.append(cross)
        return norms, crosses

    edge_sums = [edge_step(level) for level in range(ITERS)]

    variants = ends.shape[0]
    pieces = 1 if per > 1 else variants
    blocks = 3 * ITERS * pieces
    bearing_rows = -(-blocks // per)
    picked[...] = jnp.zeros(picked.shape, jnp.float32)
    for block in range(blocks):
        value, piece = block // pieces, block % pieces
        row, z = block // per, (block % per if per > 1 else piece)
        level, c = value // 3, value % 3
        for side in both:
            place = (1 + 2 * side) * across // 4
            column = (2 * z + side) * LANES
            here = (field, first, second)[level][c, 1, PAD + place : PAD + place + 1, :]
            if level:
                edges = fixes[level][c, 0, place % ROWS : place % ROWS + 1, :]
                here = mended(here, edges, place, 2 * level)
            picked[row : row + 1, column : column + LANES] = here
    start = (index * LANES).astype(jnp.float32)
    along = lax.broadcasted_iota(jnp.int32, (LANES, LANES), 0).astype(jnp.float32) + start
    parity = lane_iota((LANES, LANES)) % 2
    total = jnp.zeros((picked.shape[0], LANES), jnp.float32)
    for z in range(variants):
        site = jnp.broadcast_to(ends[z : z + 1, :], (LANES, LANES)) == along
        for side in both:
            column = (2 * z + side) * LANES
            hit = jnp.where(site & (parity == side), 1.0, 0.0)
            total = total + jnp.dot(
                picked[:, column : column + LANES], hit,
                precision=HIGH, preferred_element_type=jnp.float32,
            )

    def at_edge(values, margins):
        return sum(middle(v, m) for v, m in zip(values, margins))

    parts = [
        early[0],
        early[1] + at_edge(edge_sums[0][1], (2, 2, 2)),
        early[2] + at_edge(edge_sums[1][0], (2, 2, 2)),
        early[3] + at_edge(edge_sums[1][1], (4, 4, 4)),
        early[4] + at_edge(edge_sums[2][0], (4, 4, 4)),
        early[5] + at_edge(edge_sums[2][1], MARGINS),
    ]

    sums[...] = jnp.zeros(sums.shape, jnp.float32)
    sums[0:bearing_rows, :] = total[0:bearing_rows]
    flat = jnp.concatenate(
        [jnp.sum(part, axis=0, keepdims=True) for part in parts]
        + [jnp.zeros((ROWS - MOMENTS, LANES), jnp.float32)],
        axis=0,
    )
    amount = LANES // 2
    while amount >= SPREAD:
        flat = flat + turn(flat, amount)
        amount //= 2
    row, first_lane = divmod(blocks * (LANES // per), LANES)
    number = lax.broadcasted_iota(jnp.int32, (ROWS, LANES), 0)
    held = lane // SPREAD == number + first_lane // SPREAD
    flat = jnp.sum(jnp.where(held & (number < MOMENTS), flat, 0.0), axis=0, keepdims=True)
    sums[row : row + 1, :] = sums[row : row + 1, :] + flat
    out = jnp.concatenate(
        [sums[row : row + 1, :] for row in range(payload.shape[2] // LANES)], axis=1
    )
    for device in range(payload.shape[0]):
        payload[device] = out


def added(parts):
    while len(parts) > 1:
        parts = [sum(parts[i + 1 : i + 2], parts[i]) for i in range(0, len(parts), 2)]
    return parts[0]


def two_sum(a, b):
    total = a + b
    part = total - a
    return total, (a - (total - part)) + (b - part)


def high_half(x):
    scaled = 4097.0 * x
    return scaled - (scaled - x)


def less_multiple(a, theta, b):
    upper = high_half(b[0])
    high, error = two_sum(a[0], -theta * upper)
    high, more = two_sum(high, -theta * (b[0] - upper))
    low = (error + more) + (a[1] - theta * b[1])
    total = high + low
    return total, low - (total - high)


def exact_sums(sent, first_lane):
    number = lane_iota(sent[0].shape) // SPREAD - first_lane // SPREAD

    def sums(row):
        return [
            jnp.sum(jnp.where(number == n, row, 0.0), axis=1, keepdims=True)
            for n in range(MOMENTS)
        ]

    bound = jnp.zeros_like(sent[0])
    for n, total in enumerate(sums(added([jnp.abs(x) for x in sent]))):
        bound = jnp.where(number == n, 2.0 * total, bound)
    upper = [(x + bound) - bound for x in sent]
    lower = [x - u for x, u in zip(sent, upper)]
    return list(zip(sums(added(upper)), sums(added(lower))))


def centred(moments):
    theta = high_half(moments[1][0] / moments[0][0])
    moments = list(moments)
    for first in range(1, MOMENTS):
        for n in range(MOMENTS - 1, first - 1, -1):
            moments[n] = less_multiple(moments[n], theta, moments[n - 1])
    return theta, [high + low for high, low in moments]


def expanded(terms, theta):
    out = [terms[-1]]
    for term in terms[-2::-1]:
        out = (
            [term - theta * out[0]]
            + [out[i] - theta * out[i + 1] for i in range(len(out) - 1)]
            + [out[-1]]
        )
    return out


def coefficients(moment, shift):
    def dot(a, b):
        total = None
        for i, left in enumerate(a):
            for j, right in enumerate(b):
                term = left * right * moment[i + j]
                total = term if total is None else total + term
        return total

    one = jnp.ones_like(moment[0])
    solved, direction, increment = [one], [one], []
    norm = moment[0]
    for iteration in range(ITERS):
        image = [shift * p for p in direction] + [jnp.zeros_like(one)]
        for i, p in enumerate(direction):
            image[i + 1] = image[i + 1] + p
        alpha = norm / dot(direction, image)
        increment = [
            alpha * p + (increment[i] if i < len(increment) else 0.0) for i, p in enumerate(direction)
        ]
        solved = [
            (solved[i] if i < len(solved) else 0.0) - alpha * q for i, q in enumerate(image)
        ]
        if iteration + 1 < ITERS:
            after = dot(solved, solved)
            ratio = after / norm
            direction = [
                s + (ratio * direction[i] if i < len(direction) else 0.0)
                for i, s in enumerate(solved)
            ]
            norm = after
    return increment, solved


def combine_kernel(
    per, gathered, field, first, second, third, packed, fix_first, fix_second, fix_third,
    ends, stick, load, prior,
    increment_hbm, residual_hbm, friction_hbm,
    increment, residual, friction, forces, sems, friction_sem,
):
    depth, across = third.shape[1], third.shape[2]
    start = (device_index() * LANES).astype(jnp.float32)
    bearings = load.shape[1]
    variants = ends.shape[0]
    pieces = 1 if per > 1 else variants
    width = min(bearings, LANES)
    blocks = 3 * ITERS * pieces
    row, first_lane = divmod(blocks * (LANES // per), LANES)
    received = [gathered[device] for device in range(gathered.shape[0])]
    sent = [x[:, row * LANES : (row + 1) * LANES] for x in received]
    theta, moments = centred(exact_sums(sent, first_lane))
    grow, keep = (
        expanded(terms, theta) for terms in coefficients(moments, SHIFT + theta)
    )
    total = added(received)

    forces[...] = jnp.zeros(forces.shape, jnp.float32)
    lane = lane_iota((1, width))
    for piece in range(pieces):
        span = slice(piece * LANES, piece * LANES + width)
        readout = []
        for c in range(3):
            value = None
            for k in range(ITERS):
                block = (3 * k + c) * pieces + piece
                row = total[:, block // per * LANES : (block // per + 1) * LANES]
                if per > 1 and block % per:
                    row = turn(row, LANES - (block % per) * bearings)
                term = grow[k] * row[:, :width]
                value = term if value is None else value + term
            readout.append(value)
        weight = load[:, span]
        radius = jnp.where(stick[:, span] == 1, STATIC, KINETIC) * weight
        trial = [prior[c : c + 1, span] + ELASTIC * readout[c] for c in range(2)]
        magnitude = jnp.sqrt(trial[0] * trial[0] + trial[1] * trial[1])
        scale = radius / jnp.maximum(magnitude, radius)
        held = [t * scale for t in trial]
        for c in range(2):
            friction[c : c + 1, span] = held[c]
        force = [held[c] + weight / RADIUS * readout[c] for c in range(2)] + [VERTICAL * readout[2]]
        for c in range(3):
            for side in range(2):
                forces[2 * c + side : 2 * c + side + 1, span] = jnp.where(
                    lane % 2 == side, force[c], 0.0
                )
    friction_copy = pltpu.make_async_copy(friction, friction_hbm, friction_sem)
    friction_copy.start()
    along = lax.broadcasted_iota(jnp.int32, (LANES, LANES), 0).astype(jnp.float32) + start
    placed = jnp.zeros((8, LANES), jnp.float32)
    for piece in range(pieces):
        site = jnp.broadcast_to(ends[piece : piece + 1, :], (LANES, LANES)) == along
        placed = placed + lax.dot_general(
            forces[:, piece * LANES : (piece + 1) * LANES], jnp.where(site, 1.0, 0.0),
            (((1,), (1,)), ((), ())), precision=HIGH, preferred_element_type=jnp.float32,
        )

    grow = [jnp.broadcast_to(g, (ROWS, LANES)) for g in grow]
    keep = [jnp.broadcast_to(g, (ROWS, LANES)) for g in keep]

    def total_of(terms, values):
        parts = [t * v for t, v in zip(terms, values)]
        return parts[0] + parts[1] + (parts[2] if len(parts) == 3 else parts[2] + parts[3])

    def run(c, begin, end):
        for d in range(begin, end):
            edges = [ref[c, d] for ref in (packed, fix_first, fix_second, fix_third)]
            edges = total_of(grow, edges), total_of(keep, edges)
            for r in range(0, across, ROWS):
                here = pl.ds(PAD + r, ROWS)
                v = [ref[c, d + 1, here, :] for ref in (field, first, second)]
                v.append(third[c, d, r : r + ROWS, :])
                for ref, terms, edge in ((increment, grow, edges[0]), (residual, keep, edges[1])):
                    ref[c, d, r : r + ROWS, :] = mended(total_of(terms, v), edge, r, MARGINS[c])

    def copy(which, c, begin):
        ref, hbm = ((increment, increment_hbm), (residual, residual_hbm))[which]
        part = pl.ds(begin, PIECE)
        return pltpu.make_async_copy(
            ref.at[c, part], hbm.at[c, part], sems.at[which, c, begin // PIECE]
        )

    starts = range(0, depth, PIECE)
    for c in range(3):
        for begin in starts:
            run(c, begin, begin + PIECE)
            if begin == 0:
                for side in range(2):
                    at = (1 + 2 * side) * across // 4
                    residual[c, 0, at : at + 1, :] = (
                        residual[c, 0, at : at + 1, :] - placed[2 * c + side : 2 * c + side + 1]
                    )
            for which in range(2):
                copy(which, c, begin).start()
    friction_copy.wait()
    for c in range(3):
        for begin in starts:
            for which in range(2):
                copy(which, c, begin).wait()


def vmem_spec():
    return pl.BlockSpec(memory_space=pltpu.VMEM)


def hbm_spec():
    return pl.BlockSpec(memory_space=pltpu.HBM)


def pack_call(right_side, mass_field):
    f32 = jnp.float32
    depth, across, along = mass_field.shape
    half = depth // 2
    return pl.pallas_call(
        pack_kernel,
        out_shape=(
            pltpu.VMEM((3, depth + 2, across + 2 * PAD, along), f32),
            pltpu.VMEM((depth, across, along), f32),
            pltpu.VMEM((4, depth, ROWS, LANES), f32),
            jax.ShapeDtypeStruct((4, half, ROWS, LANES), f32),
            jax.ShapeDtypeStruct((4, half, ROWS, LANES), f32),
        ),
        in_specs=[hbm_spec()] * 2,
        out_specs=(vmem_spec(),) * 5,
        scratch_shapes=[pltpu.SemaphoreType.DMA((4,))],
        compiler_params=LIMIT,
        name="pack",
    )(
        pltpu.with_memory_space_constraint(right_side, pltpu.HBM),
        pltpu.with_memory_space_constraint(mass_field, pltpu.HBM),
    )


def cyclic_call(field, mass, spans, variants):
    f32 = jnp.float32
    depth, across, along = mass.shape
    padded = (depth + 2, across + 2 * PAD, along)
    return pl.pallas_call(
        cyclic_kernel,
        out_shape=(
            pltpu.VMEM((3,) + padded, f32),
            pltpu.VMEM((3,) + padded, f32),
            pltpu.VMEM((3, depth, across, along), f32),
            pltpu.VMEM((3, depth, ROWS, LANES), f32),
            pltpu.VMEM((6, ROWS, LANES), f32),
            pltpu.VMEM((variants, LANES), f32),
        ),
        in_specs=[vmem_spec()] * 3,
        out_specs=(vmem_spec(),) * 6,
        scratch_shapes=[pltpu.VMEM(padded, f32)],
        compiler_params=LIMIT,
        cost_estimate=pl.CostEstimate(flops=60_000_000, bytes_accessed=12_000_000, transcendentals=0),
        name="cyclic",
    )(field, mass, spans)


def edge_call(per, rows, packed, got_a, got_b, inner, field, first, second, early, ends, count):
    f32 = jnp.float32
    depth = packed.shape[1]
    variants = ends.shape[0]
    edges = (3, depth, ROWS, LANES)
    tall = -(-rows // ROWS) * ROWS
    return pl.pallas_call(
        functools.partial(edge_kernel, per),
        out_shape=(pltpu.VMEM(edges, f32),) * 3 + (pltpu.VMEM((count, 1, rows * LANES), f32),),
        in_specs=[vmem_spec()] * 9,
        out_specs=(vmem_spec(),) * 4,
        scratch_shapes=[
            pltpu.VMEM((2, 2, 3, (depth + 2) * PITCH, LANES), f32),
            pltpu.VMEM((2, (depth + 2) * PITCH, LANES), f32),
            pltpu.VMEM((2, depth, ROWS, LANES), f32),
            pltpu.VMEM((tall, LANES), f32),
            pltpu.VMEM((tall, 2 * variants * LANES), f32),
        ],
        compiler_params=LIMIT,
        name="edge",
    )(packed, got_b, got_a, inner, field, first, second, early, ends)


def combine_call(per, gathered, field, first, second, third, edges, ends, stick, load, prior):
    f32 = jnp.float32
    shape = third.shape
    bearings = load.shape[1]
    return pl.pallas_call(
        functools.partial(combine_kernel, per),
        out_shape=(
            jax.ShapeDtypeStruct(shape, f32),
            jax.ShapeDtypeStruct(shape, f32),
            jax.ShapeDtypeStruct((2, bearings), f32),
        ),
        in_specs=[vmem_spec()] * 13,
        out_specs=(hbm_spec(),) * 3,
        scratch_shapes=[
            pltpu.VMEM(shape, f32),
            pltpu.VMEM(shape, f32),
            pltpu.VMEM((2, bearings), f32),
            pltpu.VMEM((ROWS, max(bearings, LANES)), f32),
            pltpu.SemaphoreType.DMA((2, 3, shape[1] // PIECE)),
            pltpu.SemaphoreType.DMA(()),
        ],
        compiler_params=LIMIT,
        name="combine",
    )(gathered, field, first, second, third, *edges, ends, stick, load, prior)


def shards(count, right_side, mass_field, span_lengths, stick_flags, normal_load, prior_friction):
    piers = span_lengths.shape[0]
    bearings = 2 * piers
    per = LANES // bearings if bearings <= LANES else 1
    variants = per if bearings <= LANES else bearings // LANES
    pieces = 1 if per > 1 else variants
    sent = 3 * ITERS * pieces * (LANES // per) + MOMENTS * SPREAD
    rows = -(-sent // LANES)

    field, mass, packed, message_a, message_b = pack_call(right_side, mass_field)
    pairs_a = [p for i in range(0, count - 1, 2) for p in ((i, i + 1), (i + 1, i))]
    pairs_b = [p for i in range(1, count - 1, 2) for p in ((i, i + 1), (i + 1, i))]
    got_a = lax.ppermute(message_a, AXES, pairs_a)
    got_b = lax.ppermute(message_b, AXES, pairs_b)
    first, second, third, inner, early, ends = cyclic_call(
        field, mass, span_lengths.reshape(1, piers), variants
    )
    *fixes, payload = edge_call(
        per, rows, packed, got_a, got_b, inner, field, first, second, early, ends, count
    )
    gathered = lax.all_to_all(payload, AXES, 0, 0, tiled=True)
    return combine_call(
        per, gathered, field, first, second, third, (packed, *fixes), ends,
        stick_flags.reshape(1, bearings), normal_load.reshape(1, bearings), prior_friction,
    )


def solution(mesh):
    count = mesh.shape["len"] * mesh.shape["xs"]
    along = P(None, None, None, AXES)
    in_specs = (along, P(None, None, AXES), P(), P(), P(), P())
    return jax.shard_map(
        functools.partial(shards, count), mesh=mesh,
        in_specs=in_specs, out_specs=(along, along, P()), check_vma=False,
    )
```

```python
import functools

import jax
import jax.numpy as jnp
from jax import lax
from jax.experimental import pallas as pl
from jax.experimental.pallas import tpu as pltpu
from jax.sharding import PartitionSpec as P

ITERS = 3
SHIFT = 6.5
BULK = 1.5
ELASTIC = 8.0
RADIUS = 4.0
VERTICAL = 5.0
STATIC = 0.6
KINETIC = 0.45

AXES = ("len", "xs")
LANES = 128
ROWS = 8
PAD = 8
EDGE = 16
HALF = EDGE // 2
BLOCKS = LANES // EDGE
PITCH = 3 * ROWS
CHUNK = 16
PIECE = 16
MARGINS = (6, 5, 5)
MOMENTS = 2 * ITERS
SPREAD = 8
HIGH = lax.Precision.HIGHEST
LIMIT = pltpu.CompilerParams(vmem_limit_bytes=32 * 1024 * 1024)


def turn(x, amount):
    return pltpu.roll(x, amount % LANES, x.ndim - 1)


def lane_iota(shape):
    return lax.broadcasted_iota(jnp.int32, shape, len(shape) - 1)


def loop(count, step, body, init):
    def several(i, carry):
        for j in range(step):
            carry = body(i * step + j, carry)
        return carry

    return lax.fori_loop(0, count // step, several, init)


def device_index():
    return lax.axis_index(AXES[0]) * lax.axis_size(AXES[1]) + lax.axis_index(AXES[1])


def clear_padding(ref, lead, depth, across):
    for slab in (0, depth + 1):
        ref[lead + (slab,)] = jnp.zeros((across + 2 * PAD, LANES), jnp.float32)
    blank = jnp.zeros((PAD, LANES), jnp.float32)
    for d in range(1, depth + 1):
        ref[lead + (d, slice(0, PAD))] = blank
        ref[lead + (d, slice(PAD + across, None))] = blank


def pack_kernel(right_hbm, mass_hbm, field, mass, packed, message_a, message_b, sems):
    depth, across = mass.shape[0], mass.shape[1]
    copies = [
        pltpu.make_async_copy(
            right_hbm.at[c], field.at[c, pl.ds(1, depth), pl.ds(PAD, across)], sems.at[c]
        )
        for c in range(3)
    ]
    copies.append(pltpu.make_async_copy(mass_hbm, mass, sems.at[3]))
    for copy in copies:
        copy.start()
    for c in range(3):
        clear_padding(field, (c,), depth, across)
    is_even = device_index() % 2 == 0
    lane = lane_iota((ROWS, LANES))
    block_of = lane // EDGE
    first_half = lane % EDGE < HALF
    for c in range(4):
        copies[c].wait()
        edges = []
        for d in range(depth):
            edge = None
            for b in range(across // ROWS):
                row = pl.ds(b * ROWS + (PAD if c < 3 else 0), ROWS)
                if c < 3:
                    tile = field[c, d + 1, row, :]
                else:
                    tile = mass[d, row, :] + (6.0 - SHIFT)
                    mass[d, row, :] = tile
                moved = turn(tile, EDGE * b + HALF)
                edge = moved if edge is None else jnp.where(block_of == b, moved, edge)
            packed[c, d] = edge
            edges.append(edge)
        for d in range(depth // 2):
            low, high = edges[d], edges[d + depth // 2]
            rightward = jnp.where(first_half, low, turn(high, HALF))
            leftward = jnp.where(first_half, turn(low, -HALF), high)
            message_a[c, d] = jnp.where(is_even, rightward, leftward)
            message_b[c, d] = jnp.where(is_even, leftward, rightward)


def folded(x):
    return sum(x[i : i + ROWS] for i in range(0, x.shape[0], ROWS))


def cyclic_step(source, mass, div, store, inner_source=None, inner_div=None):
    depth, across = mass.shape[0], mass.shape[1]
    chunks = range(0, across, CHUNK)
    block_of = lane_iota((ROWS, LANES)) // EDGE

    def pack(edge, r, tile):
        for i in range(0, tile.shape[0], ROWS):
            b = (r + i) // ROWS
            moved = turn(tile[i : i + ROWS], EDGE * b + HALF)
            edge = moved if edge is None else jnp.where(block_of == b, moved, edge)
        return edge

    def divergence(d, carry):
        here, up, down = (pl.ds(PAD + by, across) for by in (0, 1, -1))
        x = source[0, d + 1, here, :]
        w = turn(x, -1) - turn(x, 1)
        w = w + (source[1, d + 1, up, :] - source[1, d + 1, down, :])
        w = w + (source[2, d + 2, here, :] - source[2, d, here, :])
        w = w * (0.25 * BULK)
        div[d + 1, here, :] = w
        if inner_source is not None:
            inner_source[d] = pack(None, 0, x)
        if inner_div is not None:
            inner_div[d] = pack(None, 0, w)
        return carry

    loop(depth, 4, divergence, 0)

    def image(d, carry):
        norm, cross, cross_rest = carry
        for r in chunks:
            here, up, down = (pl.ds(PAD + r + by, CHUNK) for by in (0, 1, -1))
            diag = mass[d, r : r + CHUNK, :]
            w = div[d + 1, here, :]
            norms, crosses = [], []
            for c in range(3):
                x = source[c, d + 1, here, :]
                if c == 0:
                    total = turn(x + w, -1) + turn(x - w, 1)
                else:
                    total = turn(x, -1) + turn(x, 1)
                if c == 1:
                    total = total + (div[d + 1, up, :] - div[d + 1, down, :])
                if c == 2:
                    total = total + (div[d + 2, here, :] - div[d, here, :])
                total = total + (source[c, d, here, :] + source[c, d + 2, here, :])
                total = total + (source[c, d + 1, up, :] + source[c, d + 1, down, :])
                out = diag * x - total
                store(c, d, r, out)
                norms.append(x * x)
                crosses.append(x * out)
            norm = norm + folded(norms[0] + norms[1] + norms[2])
            cross = cross + folded(crosses[0])
            cross_rest = cross_rest + folded(crosses[1] + crosses[2])
        return norm, cross, cross_rest

    return loop(depth, depth, image, (jnp.zeros((ROWS, LANES), jnp.float32),) * 3)


def interior(value, margin):
    lane = lane_iota(value.shape)
    return jnp.where((lane >= margin) & (lane < LANES - margin), value, 0.0)


def cyclic_kernel(field, mass, spans, first, second, third, inner, moments, ends, div):
    depth, across = mass.shape[0], mass.shape[1]
    clear_padding(div, (), depth, across)
    for c in range(3):
        clear_padding(first, (c,), depth, across)
        clear_padding(second, (c,), depth, across)

    def store_first(c, d, r, out):
        first[c, d + 1, pl.ds(PAD + r, CHUNK), :] = out

    def store_second(c, d, r, out):
        second[c, d + 1, pl.ds(PAD + r, CHUNK), :] = out

    def store_third(c, d, r, out):
        third[c, d, r : r + CHUNK, :] = out

    norm, cross, cross_rest = cyclic_step(field, mass, div, store_first)
    moments[0] = norm
    moments[1] = interior(cross + cross_rest, 2)
    norm, cross, cross_rest = cyclic_step(first, mass, div, store_second, inner.at[0])
    moments[2] = interior(norm, 2)
    moments[3] = interior(cross + cross_rest, 4)
    norm, cross, cross_rest = cyclic_step(
        second, mass, div, store_third, inner.at[1], inner.at[2]
    )
    moments[4] = interior(norm, 4)
    moments[5] = interior(cross, MARGINS[0]) + interior(cross_rest, MARGINS[1])
    piers = spans.shape[1]
    bearings = 2 * piers
    lane = lane_iota((piers, LANES))
    pier = lax.broadcasted_iota(jnp.int32, (piers, LANES), 0)
    lengths = jnp.broadcast_to(spans[...].astype(jnp.float32), (ROWS, piers))
    for z in range(ends.shape[0]):
        bearing = lane - z * bearings if bearings <= LANES else lane + z * LANES
        upto = jnp.where(pier * 2 <= bearing, 1.0, 0.0)
        total = jnp.dot(lengths, upto, precision=HIGH, preferred_element_type=jnp.float32)
        inside = (bearing[0:1] >= 0) & (bearing[0:1] < bearings)
        ends[z : z + 1, :] = jnp.where(inside, total[0:1] - 1.0, -1e9)


def mended(value, edges, row, margin):
    moved = [
        turn(edges, -(EDGE * ((row + i) // ROWS) + HALF)) for i in range(0, value.shape[0], ROWS)
    ]
    spot = lane_iota(value.shape)
    return jnp.where(
        (spot < margin) | (spot >= LANES - margin),
        moved[0] if len(moved) == 1 else jnp.concatenate(moved, axis=0),
        value,
    )


def edge_kernel(
    per, packed, got_b, got_a, inner, field, first, second, early, ends,
    fix_first, fix_second, fix_third, payload,
    edges, edge_div, edge_diag, sums, picked,
):
    depth, across = packed.shape[1], first.shape[2] - 2 * PAD
    index = device_index()
    count = lax.axis_size(AXES[0]) * lax.axis_size(AXES[1])
    is_even = index % 2 == 0
    lane = lane_iota((ROWS, LANES))
    first_half = lane % EDGE < HALF
    ones = jnp.ones((ROWS, LANES), jnp.float32)
    keep = (
        jnp.where(first_half & (index == 0), 0.0, ones),
        jnp.where(jnp.logical_not(first_half) & (index == count - 1), 0.0, ones),
    )
    both = range(2)
    comps = range(3)
    half = depth // 2
    blank = jnp.zeros((ROWS, LANES), jnp.float32)

    def row_of(d):
        return (d + 1) * PITCH + ROWS

    for c in range(4):
        for d in range(half):
            a, b = got_a[c, d], got_b[c, d]
            from_left = jnp.where(is_even, b, a)
            from_right = jnp.where(is_even, a, b)
            low, high = packed[c, d], packed[c, d + half]
            for at, left, right in (
                (
                    d,
                    jnp.where(first_half, from_left, low),
                    jnp.where(first_half, low, turn(from_right, HALF)),
                ),
                (
                    d + half,
                    jnp.where(first_half, turn(from_left, -HALF), high),
                    jnp.where(first_half, high, from_right),
                ),
            ):
                if c < 3:
                    edges[0, 0, c, pl.ds(row_of(at), ROWS), :] = left
                    edges[0, 1, c, pl.ds(row_of(at), ROWS), :] = right
                else:
                    edge_diag[0, at] = left
                    edge_diag[1, at] = right
    for s in both:
        for c in comps:
            for buffer in both:
                edges[buffer, s, c, pl.ds(ROWS, ROWS), :] = blank
                edges[buffer, s, c, pl.ds(row_of(depth), ROWS), :] = blank
        edge_div[s, pl.ds(ROWS, ROWS), :] = blank
        edge_div[s, pl.ds(row_of(depth), ROWS), :] = blank

    def join_blocks(ref, lead):
        for d in (0, half):
            base = row_of(d)
            last = ref[lead + (pl.ds(base + ROWS - 1, half, stride=PITCH), slice(None))]
            ahead = ref[lead + (pl.ds(base, half, stride=PITCH), slice(None))]
            spot = lane_iota((half, LANES))
            ref[lead + (pl.ds(base - 1, half, stride=PITCH), slice(None))] = jnp.where(
                spot >= EDGE, turn(last, EDGE), 0.0
            )
            ref[lead + (pl.ds(base + ROWS, half, stride=PITCH), slice(None))] = jnp.where(
                spot < LANES - EDGE, turn(ahead, -EDGE), 0.0
            )

    def div_at(s, d, by=0):
        return edge_div[s, pl.ds(row_of(d) + by, ROWS), :]

    def middle(value, margin):
        spot = lane % EDGE
        return jnp.where((spot >= HALF - margin) & (spot < HALF + margin), value, 0.0)

    fixes = (packed, fix_first, fix_second, fix_third)
    last_planes = lane % EDGE >= EDGE - 2
    first_planes = lane % EDGE < 2

    def joined(s, value, own):
        return jnp.where(first_planes if s else last_planes, own, value)

    def edge_step(level):
        edge, target = edges.at[level % 2], edges.at[(level + 1) % 2]

        def at(s, c, d, by=0):
            return edge[s, c, pl.ds(row_of(d) + by, ROWS), :]

        for s in both:
            for c in comps:
                join_blocks(edge, (s, c))
        for s in both:
            for d in range(depth):
                x = at(s, 0, d)
                w = turn(x, -1) - turn(x, 1)
                w = w + (at(s, 1, d, 1) - at(s, 1, d, -1))
                w = w + (at(s, 2, d + 1) - at(s, 2, d - 1))
                w = w * ((0.25 * BULK) * keep[s])
                edge_div[s, pl.ds(row_of(d), ROWS), :] = joined(s, w, inner[2, d]) if level == 2 else w
            join_blocks(edge_div, (s,))
        norms, crosses = [], []
        for c in comps:
            norm, cross = blank, blank
            for d in range(depth):
                pair = []
                for s in both:
                    x = at(s, c, d)
                    if c == 0:
                        w = div_at(s, d)
                        total = turn(x + w, -1) + turn(x - w, 1)
                    else:
                        total = turn(x, -1) + turn(x, 1)
                    if c == 1:
                        total = total + (div_at(s, d, 1) - div_at(s, d, -1))
                    if c == 2:
                        total = total + (div_at(s, d + 1) - div_at(s, d - 1))
                    total = total + (at(s, c, d - 1) + at(s, c, d + 1))
                    total = total + (at(s, c, d, 1) + at(s, c, d, -1))
                    image = (edge_diag[s, d] * x - total) * keep[s]
                    pair.append(image)
                    if level + 1 < ITERS:
                        image = image if c else joined(s, image, inner[level, d])
                        target[s, c, pl.ds(row_of(d), ROWS), :] = image
                old = fixes[level][c, d]
                new = jnp.where(first_half, pair[1], pair[0])
                fixes[level + 1][c, d] = new
                if level:
                    norm = norm + old * old
                cross = cross + old * new
            norms.append(norm)
            crosses.append(cross)
        return norms, crosses

    edge_sums = [edge_step(level) for level in range(ITERS)]

    variants = ends.shape[0]
    pieces = 1 if per > 1 else variants
    blocks = 3 * ITERS * pieces
    bearing_rows = -(-blocks // per)
    picked[...] = jnp.zeros(picked.shape, jnp.float32)
    for block in range(blocks):
        value, piece = block // pieces, block % pieces
        row, z = block // per, (block % per if per > 1 else piece)
        level, c = value // 3, value % 3
        for side in both:
            place = (1 + 2 * side) * across // 4
            column = (2 * z + side) * LANES
            here = (field, first, second)[level][c, 1, PAD + place : PAD + place + 1, :]
            if level:
                edges = fixes[level][c, 0, place % ROWS : place % ROWS + 1, :]
                here = mended(here, edges, place, 2 * level)
            picked[row : row + 1, column : column + LANES] = here
    start = (index * LANES).astype(jnp.float32)
    along = lax.broadcasted_iota(jnp.int32, (LANES, LANES), 0).astype(jnp.float32) + start
    parity = lane_iota((LANES, LANES)) % 2
    total = jnp.zeros((picked.shape[0], LANES), jnp.float32)
    for z in range(variants):
        site = jnp.broadcast_to(ends[z : z + 1, :], (LANES, LANES)) == along
        for side in both:
            column = (2 * z + side) * LANES
            hit = jnp.where(site & (parity == side), 1.0, 0.0)
            total = total + jnp.dot(
                picked[:, column : column + LANES], hit,
                precision=HIGH, preferred_element_type=jnp.float32,
            )

    def at_edge(values, margins):
        return sum(middle(v, m) for v, m in zip(values, margins))

    parts = [
        early[0],
        early[1] + at_edge(edge_sums[0][1], (2, 2, 2)),
        early[2] + at_edge(edge_sums[1][0], (2, 2, 2)),
        early[3] + at_edge(edge_sums[1][1], (4, 4, 4)),
        early[4] + at_edge(edge_sums[2][0], (4, 4, 4)),
        early[5] + at_edge(edge_sums[2][1], MARGINS),
    ]

    sums[...] = jnp.zeros(sums.shape, jnp.float32)
    sums[0:bearing_rows, :] = total[0:bearing_rows]
    flat = jnp.concatenate(
        [jnp.sum(part, axis=0, keepdims=True) for part in parts]
        + [jnp.zeros((ROWS - MOMENTS, LANES), jnp.float32)],
        axis=0,
    )
    amount = LANES // 2
    while amount >= SPREAD:
        flat = flat + turn(flat, amount)
        amount //= 2
    row, first_lane = divmod(blocks * (LANES // per), LANES)
    number = lax.broadcasted_iota(jnp.int32, (ROWS, LANES), 0)
    held = lane // SPREAD == number + first_lane // SPREAD
    flat = jnp.sum(jnp.where(held & (number < MOMENTS), flat, 0.0), axis=0, keepdims=True)
    sums[row : row + 1, :] = sums[row : row + 1, :] + flat
    out = jnp.concatenate(
        [sums[row : row + 1, :] for row in range(payload.shape[2] // LANES)], axis=1
    )
    for device in range(payload.shape[0]):
        payload[device] = out


def added(parts):
    while len(parts) > 1:
        parts = [sum(parts[i + 1 : i + 2], parts[i]) for i in range(0, len(parts), 2)]
    return parts[0]


def two_sum(a, b):
    total = a + b
    part = total - a
    return total, (a - (total - part)) + (b - part)


def high_half(x):
    scaled = 4097.0 * x
    return scaled - (scaled - x)


def less_multiple(a, theta, b):
    upper = high_half(b[0])
    high, error = two_sum(a[0], -theta * upper)
    high, more = two_sum(high, -theta * (b[0] - upper))
    low = (error + more) + (a[1] - theta * b[1])
    total = high + low
    return total, low - (total - high)


def exact_sums(sent, first_lane):
    number = lane_iota(sent[0].shape) // SPREAD - first_lane // SPREAD

    def sums(row):
        return [
            jnp.sum(jnp.where(number == n, row, 0.0), axis=1, keepdims=True)
            for n in range(MOMENTS)
        ]

    bound = jnp.zeros_like(sent[0])
    for n, total in enumerate(sums(added([jnp.abs(x) for x in sent]))):
        bound = jnp.where(number == n, 2.0 * total, bound)
    upper = [(x + bound) - bound for x in sent]
    lower = [x - u for x, u in zip(sent, upper)]
    return list(zip(sums(added(upper)), sums(added(lower))))


def centred(moments):
    theta = high_half(moments[1][0] / moments[0][0])
    moments = list(moments)
    for first in range(1, MOMENTS):
        for n in range(MOMENTS - 1, first - 1, -1):
            moments[n] = less_multiple(moments[n], theta, moments[n - 1])
    return theta, [high + low for high, low in moments]


def expanded(terms, theta):
    out = [terms[-1]]
    for term in terms[-2::-1]:
        out = (
            [term - theta * out[0]]
            + [out[i] - theta * out[i + 1] for i in range(len(out) - 1)]
            + [out[-1]]
        )
    return out


def coefficients(moment, shift):
    def dot(a, b):
        total = None
        for i, left in enumerate(a):
            for j, right in enumerate(b):
                term = left * right * moment[i + j]
                total = term if total is None else total + term
        return total

    one = jnp.ones_like(moment[0])
    solved, direction, increment = [one], [one], []
    norm = moment[0]
    for iteration in range(ITERS):
        image = [shift * p for p in direction] + [jnp.zeros_like(one)]
        for i, p in enumerate(direction):
            image[i + 1] = image[i + 1] + p
        alpha = norm / dot(direction, image)
        increment = [
            alpha * p + (increment[i] if i < len(increment) else 0.0) for i, p in enumerate(direction)
        ]
        solved = [
            (solved[i] if i < len(solved) else 0.0) - alpha * q for i, q in enumerate(image)
        ]
        if iteration + 1 < ITERS:
            after = dot(solved, solved)
            ratio = after / norm
            direction = [
                s + (ratio * direction[i] if i < len(direction) else 0.0)
                for i, s in enumerate(solved)
            ]
            norm = after
    return increment, solved


def combine_kernel(
    per, gathered, field, first, second, third, packed, fix_first, fix_second, fix_third,
    ends, stick, load, prior,
    increment_hbm, residual_hbm, friction_hbm,
    increment, residual, friction, forces, sems, friction_sem,
):
    depth, across = third.shape[1], third.shape[2]
    start = (device_index() * LANES).astype(jnp.float32)
    bearings = load.shape[1]
    variants = ends.shape[0]
    pieces = 1 if per > 1 else variants
    width = min(bearings, LANES)
    blocks = 3 * ITERS * pieces
    row, first_lane = divmod(blocks * (LANES // per), LANES)
    received = [gathered[device] for device in range(gathered.shape[0])]
    sent = [x[:, row * LANES : (row + 1) * LANES] for x in received]
    theta, moments = centred(exact_sums(sent, first_lane))
    grow, keep = (
        expanded(terms, theta) for terms in coefficients(moments, SHIFT + theta)
    )
    total = added(received)

    forces[...] = jnp.zeros(forces.shape, jnp.float32)
    lane = lane_iota((1, width))
    for piece in range(pieces):
        span = slice(piece * LANES, piece * LANES + width)
        readout = []
        for c in range(3):
            value = None
            for k in range(ITERS):
                block = (3 * k + c) * pieces + piece
                row = total[:, block // per * LANES : (block // per + 1) * LANES]
                if per > 1 and block % per:
                    row = turn(row, LANES - (block % per) * bearings)
                term = grow[k] * row[:, :width]
                value = term if value is None else value + term
            readout.append(value)
        weight = load[:, span]
        radius = jnp.where(stick[:, span] == 1, STATIC, KINETIC) * weight
        trial = [prior[c : c + 1, span] + ELASTIC * readout[c] for c in range(2)]
        magnitude = jnp.sqrt(trial[0] * trial[0] + trial[1] * trial[1])
        scale = radius / jnp.maximum(magnitude, radius)
        held = [t * scale for t in trial]
        for c in range(2):
            friction[c : c + 1, span] = held[c]
        force = [held[c] + weight / RADIUS * readout[c] for c in range(2)] + [VERTICAL * readout[2]]
        for c in range(3):
            for side in range(2):
                forces[2 * c + side : 2 * c + side + 1, span] = jnp.where(
                    lane % 2 == side, force[c], 0.0
                )
    friction_copy = pltpu.make_async_copy(friction, friction_hbm, friction_sem)
    friction_copy.start()
    along = lax.broadcasted_iota(jnp.int32, (LANES, LANES), 0).astype(jnp.float32) + start
    placed = jnp.zeros((8, LANES), jnp.float32)
    for piece in range(pieces):
        site = jnp.broadcast_to(ends[piece : piece + 1, :], (LANES, LANES)) == along
        placed = placed + lax.dot_general(
            forces[:, piece * LANES : (piece + 1) * LANES], jnp.where(site, 1.0, 0.0),
            (((1,), (1,)), ((), ())), precision=HIGH, preferred_element_type=jnp.float32,
        )

    grow = [jnp.broadcast_to(g, (ROWS, LANES)) for g in grow]
    keep = [jnp.broadcast_to(g, (ROWS, LANES)) for g in keep]

    def total_of(terms, values):
        parts = [t * v for t, v in zip(terms, values)]
        return parts[0] + parts[1] + (parts[2] if len(parts) == 3 else parts[2] + parts[3])

    def run(c, begin, end):
        for d in range(begin, end):
            edges = [ref[c, d] for ref in (packed, fix_first, fix_second, fix_third)]
            edges = total_of(grow, edges), total_of(keep, edges)
            for r in range(0, across, ROWS):
                here = pl.ds(PAD + r, ROWS)
                v = [ref[c, d + 1, here, :] for ref in (field, first, second)]
                v.append(third[c, d, r : r + ROWS, :])
                for ref, terms, edge in ((increment, grow, edges[0]), (residual, keep, edges[1])):
                    ref[c, d, r : r + ROWS, :] = mended(total_of(terms, v), edge, r, MARGINS[c])

    def copy(which, c, begin):
        ref, hbm = ((increment, increment_hbm), (residual, residual_hbm))[which]
        part = pl.ds(begin, PIECE)
        return pltpu.make_async_copy(
            ref.at[c, part], hbm.at[c, part], sems.at[which, c, begin // PIECE]
        )

    starts = range(0, depth, PIECE)
    for c in range(3):
        for begin in starts:
            run(c, begin, begin + PIECE)
            if begin == 0:
                for side in range(2):
                    at = (1 + 2 * side) * across // 4
                    residual[c, 0, at : at + 1, :] = (
                        residual[c, 0, at : at + 1, :] - placed[2 * c + side : 2 * c + side + 1]
                    )
            for which in range(2):
                copy(which, c, begin).start()
    friction_copy.wait()
    for c in range(3):
        for begin in starts:
            for which in range(2):
                copy(which, c, begin).wait()


def vmem_spec():
    return pl.BlockSpec(memory_space=pltpu.VMEM)


def hbm_spec():
    return pl.BlockSpec(memory_space=pltpu.HBM)


def pack_call(right_side, mass_field):
    f32 = jnp.float32
    depth, across, along = mass_field.shape
    half = depth // 2
    return pl.pallas_call(
        pack_kernel,
        out_shape=(
            pltpu.VMEM((3, depth + 2, across + 2 * PAD, along), f32),
            pltpu.VMEM((depth, across, along), f32),
            pltpu.VMEM((4, depth, ROWS, LANES), f32),
            jax.ShapeDtypeStruct((4, half, ROWS, LANES), f32),
            jax.ShapeDtypeStruct((4, half, ROWS, LANES), f32),
        ),
        in_specs=[hbm_spec()] * 2,
        out_specs=(vmem_spec(),) * 5,
        scratch_shapes=[pltpu.SemaphoreType.DMA((4,))],
        compiler_params=LIMIT,
        name="pack",
    )(
        pltpu.with_memory_space_constraint(right_side, pltpu.HBM),
        pltpu.with_memory_space_constraint(mass_field, pltpu.HBM),
    )


def cyclic_call(field, mass, spans, variants):
    f32 = jnp.float32
    depth, across, along = mass.shape
    padded = (depth + 2, across + 2 * PAD, along)
    return pl.pallas_call(
        cyclic_kernel,
        out_shape=(
            pltpu.VMEM((3,) + padded, f32),
            pltpu.VMEM((3,) + padded, f32),
            pltpu.VMEM((3, depth, across, along), f32),
            pltpu.VMEM((3, depth, ROWS, LANES), f32),
            pltpu.VMEM((6, ROWS, LANES), f32),
            pltpu.VMEM((variants, LANES), f32),
        ),
        in_specs=[vmem_spec()] * 3,
        out_specs=(vmem_spec(),) * 6,
        scratch_shapes=[pltpu.VMEM(padded, f32)],
        compiler_params=LIMIT,
        cost_estimate=pl.CostEstimate(flops=60_000_000, bytes_accessed=12_000_000, transcendentals=0),
        name="cyclic",
    )(field, mass, spans)


def edge_call(per, rows, packed, got_a, got_b, inner, field, first, second, early, ends, count):
    f32 = jnp.float32
    depth = packed.shape[1]
    variants = ends.shape[0]
    edges = (3, depth, ROWS, LANES)
    tall = -(-rows // ROWS) * ROWS
    return pl.pallas_call(
        functools.partial(edge_kernel, per),
        out_shape=(pltpu.VMEM(edges, f32),) * 3 + (pltpu.VMEM((count, 1, rows * LANES), f32),),
        in_specs=[vmem_spec()] * 9,
        out_specs=(vmem_spec(),) * 4,
        scratch_shapes=[
            pltpu.VMEM((2, 2, 3, (depth + 2) * PITCH, LANES), f32),
            pltpu.VMEM((2, (depth + 2) * PITCH, LANES), f32),
            pltpu.VMEM((2, depth, ROWS, LANES), f32),
            pltpu.VMEM((tall, LANES), f32),
            pltpu.VMEM((tall, 2 * variants * LANES), f32),
        ],
        compiler_params=LIMIT,
        name="edge",
    )(packed, got_b, got_a, inner, field, first, second, early, ends)


def combine_call(per, gathered, field, first, second, third, edges, ends, stick, load, prior):
    f32 = jnp.float32
    shape = third.shape
    bearings = load.shape[1]
    return pl.pallas_call(
        functools.partial(combine_kernel, per),
        out_shape=(
            jax.ShapeDtypeStruct(shape, f32),
            jax.ShapeDtypeStruct(shape, f32),
            jax.ShapeDtypeStruct((2, bearings), f32),
        ),
        in_specs=[vmem_spec()] * 13,
        out_specs=(hbm_spec(),) * 3,
        scratch_shapes=[
            pltpu.VMEM(shape, f32),
            pltpu.VMEM(shape, f32),
            pltpu.VMEM((2, bearings), f32),
            pltpu.VMEM((ROWS, max(bearings, LANES)), f32),
            pltpu.SemaphoreType.DMA((2, 3, shape[1] // PIECE)),
            pltpu.SemaphoreType.DMA(()),
        ],
        compiler_params=LIMIT,
        name="combine",
    )(gathered, field, first, second, third, *edges, ends, stick, load, prior)


def shards(count, right_side, mass_field, span_lengths, stick_flags, normal_load, prior_friction):
    piers = span_lengths.shape[0]
    bearings = 2 * piers
    per = LANES // bearings if bearings <= LANES else 1
    variants = per if bearings <= LANES else bearings // LANES
    pieces = 1 if per > 1 else variants
    sent = 3 * ITERS * pieces * (LANES // per) + MOMENTS * SPREAD
    rows = -(-sent // LANES)

    field, mass, packed, message_a, message_b = pack_call(right_side, mass_field)
    pairs_a = [p for i in range(0, count - 1, 2) for p in ((i, i + 1), (i + 1, i))]
    pairs_b = [p for i in range(1, count - 1, 2) for p in ((i, i + 1), (i + 1, i))]
    got_a = lax.ppermute(message_a, AXES, pairs_a)
    got_b = lax.ppermute(message_b, AXES, pairs_b)
    first, second, third, inner, early, ends = cyclic_call(
        field, mass, span_lengths.reshape(1, piers), variants
    )
    *fixes, payload = edge_call(
        per, rows, packed, got_a, got_b, inner, field, first, second, early, ends, count
    )
    gathered = lax.all_to_all(payload, AXES, 0, 0, tiled=True)
    return combine_call(
        per, gathered, field, first, second, third, (packed, *fixes), ends,
        stick_flags.reshape(1, bearings), normal_load.reshape(1, bearings), prior_friction,
    )


def solution(mesh):
    count = mesh.shape["len"] * mesh.shape["xs"]
    along = P(None, None, None, AXES)
    in_specs = (along, P(None, None, AXES), P(), P(), P(), P())
    return jax.shard_map(
        functools.partial(shards, count), mesh=mesh,
        in_specs=in_specs, out_specs=(along, along, P()), check_vma=False,
    )
```

```python
import functools

import jax
import jax.numpy as jnp
from jax import lax
from jax.experimental import pallas as pl
from jax.experimental.pallas import tpu as pltpu
from jax.sharding import PartitionSpec as P

ITERS = 3
SHIFT = 6.5
BULK = 1.5
ELASTIC = 8.0
RADIUS = 4.0
VERTICAL = 5.0
STATIC = 0.6
KINETIC = 0.45

AXES = ("len", "xs")
LANES = 128
ROWS = 8
PAD = 8
EDGE = 16
HALF = EDGE // 2
BLOCKS = LANES // EDGE
PITCH = 3 * ROWS
CHUNK = 16
PIECE = 16
MARGINS = (6, 5, 5)
MOMENTS = 2 * ITERS
SPREAD = 8
HIGH = lax.Precision.HIGHEST
LIMIT = pltpu.CompilerParams(vmem_limit_bytes=32 * 1024 * 1024)


def turn(x, amount):
    return pltpu.roll(x, amount % LANES, x.ndim - 1)


def lane_iota(shape):
    return lax.broadcasted_iota(jnp.int32, shape, len(shape) - 1)


def loop(count, step, body, init):
    def several(i, carry):
        for j in range(step):
            carry = body(i * step + j, carry)
        return carry

    return lax.fori_loop(0, count // step, several, init)


def device_index():
    return lax.axis_index(AXES[0]) * lax.axis_size(AXES[1]) + lax.axis_index(AXES[1])


def clear_padding(ref, lead, depth, across):
    for slab in (0, depth + 1):
        ref[lead + (slab,)] = jnp.zeros((across + 2 * PAD, LANES), jnp.float32)
    blank = jnp.zeros((PAD, LANES), jnp.float32)
    for d in range(1, depth + 1):
        ref[lead + (d, slice(0, PAD))] = blank
        ref[lead + (d, slice(PAD + across, None))] = blank


def pack_kernel(right_hbm, mass_hbm, field, mass, packed, message_a, message_b, sems):
    depth, across = mass.shape[0], mass.shape[1]
    half = depth // 2
    copies = []
    for c in range(4):
        for part in range(2):
            begin = part * half
            if c < 3:
                source = right_hbm.at[c, pl.ds(begin, half)]
                target = field.at[c, pl.ds(1 + begin, half), pl.ds(PAD, across)]
            else:
                source, target = mass_hbm.at[pl.ds(begin, half)], mass.at[pl.ds(begin, half)]
            copies.append(pltpu.make_async_copy(source, target, sems.at[2 * c + part]))
    for copy in copies:
        copy.start()
    for c in range(3):
        clear_padding(field, (c,), depth, across)
    is_even = device_index() % 2 == 0
    lane = lane_iota((ROWS, LANES))
    block_of = lane // EDGE
    first_half = lane % EDGE < HALF
    for c in range(4):
        edges = []
        for d in range(depth):
            if d % half == 0:
                copies[2 * c + d // half].wait()
            edge = None
            for b in range(across // ROWS):
                row = pl.ds(b * ROWS + (PAD if c < 3 else 0), ROWS)
                if c < 3:
                    tile = field[c, d + 1, row, :]
                else:
                    tile = mass[d, row, :] + (6.0 - SHIFT)
                    mass[d, row, :] = tile
                moved = turn(tile, EDGE * b + HALF)
                edge = moved if edge is None else jnp.where(block_of == b, moved, edge)
            packed[c, d] = edge
            edges.append(edge)
        for d in range(depth // 2):
            low, high = edges[d], edges[d + depth // 2]
            rightward = jnp.where(first_half, low, turn(high, HALF))
            leftward = jnp.where(first_half, turn(low, -HALF), high)
            message_a[c, d] = jnp.where(is_even, rightward, leftward)
            message_b[c, d] = jnp.where(is_even, leftward, rightward)


def folded(x):
    return sum(x[i : i + ROWS] for i in range(0, x.shape[0], ROWS))


def cyclic_step(source, mass, div, store, inner_source=None, inner_div=None):
    depth, across = mass.shape[0], mass.shape[1]
    chunks = range(0, across, CHUNK)
    block_of = lane_iota((ROWS, LANES)) // EDGE

    def pack(edge, r, tile):
        for i in range(0, tile.shape[0], ROWS):
            b = (r + i) // ROWS
            moved = turn(tile[i : i + ROWS], EDGE * b + HALF)
            edge = moved if edge is None else jnp.where(block_of == b, moved, edge)
        return edge

    def divergence(d, carry):
        here, up, down = (pl.ds(PAD + by, across) for by in (0, 1, -1))
        x = source[0, d + 1, here, :]
        w = turn(x, -1) - turn(x, 1)
        w = w + (source[1, d + 1, up, :] - source[1, d + 1, down, :])
        w = w + (source[2, d + 2, here, :] - source[2, d, here, :])
        w = w * (0.25 * BULK)
        div[d + 1, here, :] = w
        if inner_source is not None:
            inner_source[d] = pack(None, 0, x)
        if inner_div is not None:
            inner_div[d] = pack(None, 0, w)
        return carry

    loop(depth, 4, divergence, 0)

    def image(d, carry):
        norm, cross, cross_rest = carry
        for r in chunks:
            here, up, down = (pl.ds(PAD + r + by, CHUNK) for by in (0, 1, -1))
            diag = mass[d, r : r + CHUNK, :]
            w = div[d + 1, here, :]
            norms, crosses = [], []
            for c in range(3):
                x = source[c, d + 1, here, :]
                if c == 0:
                    total = turn(x + w, -1) + turn(x - w, 1)
                else:
                    total = turn(x, -1) + turn(x, 1)
                if c == 1:
                    total = total + (div[d + 1, up, :] - div[d + 1, down, :])
                if c == 2:
                    total = total + (div[d + 2, here, :] - div[d, here, :])
                total = total + (source[c, d, here, :] + source[c, d + 2, here, :])
                total = total + (source[c, d + 1, up, :] + source[c, d + 1, down, :])
                out = diag * x - total
                store(c, d, r, out)
                norms.append(x * x)
                crosses.append(x * out)
            norm = norm + folded(norms[0] + norms[1] + norms[2])
            cross = cross + folded(crosses[0])
            cross_rest = cross_rest + folded(crosses[1] + crosses[2])
        return norm, cross, cross_rest

    return loop(depth, depth, image, (jnp.zeros((ROWS, LANES), jnp.float32),) * 3)


def interior(value, margin):
    lane = lane_iota(value.shape)
    return jnp.where((lane >= margin) & (lane < LANES - margin), value, 0.0)


def cyclic_kernel(field, mass, spans, first, second, third, inner, moments, ends, div):
    depth, across = mass.shape[0], mass.shape[1]
    clear_padding(div, (), depth, across)
    for c in range(3):
        clear_padding(first, (c,), depth, across)
        clear_padding(second, (c,), depth, across)

    def store_first(c, d, r, out):
        first[c, d + 1, pl.ds(PAD + r, CHUNK), :] = out

    def store_second(c, d, r, out):
        second[c, d + 1, pl.ds(PAD + r, CHUNK), :] = out

    def store_third(c, d, r, out):
        third[c, d, r : r + CHUNK, :] = out

    norm, cross, cross_rest = cyclic_step(field, mass, div, store_first)
    moments[0] = norm
    moments[1] = interior(cross + cross_rest, 2)
    norm, cross, cross_rest = cyclic_step(first, mass, div, store_second, inner.at[0])
    moments[2] = interior(norm, 2)
    moments[3] = interior(cross + cross_rest, 4)
    norm, cross, cross_rest = cyclic_step(
        second, mass, div, store_third, inner.at[1], inner.at[2]
    )
    moments[4] = interior(norm, 4)
    moments[5] = interior(cross, MARGINS[0]) + interior(cross_rest, MARGINS[1])
    piers = spans.shape[1]
    bearings = 2 * piers
    lane = lane_iota((piers, LANES))
    pier = lax.broadcasted_iota(jnp.int32, (piers, LANES), 0)
    lengths = jnp.broadcast_to(spans[...].astype(jnp.float32), (ROWS, piers))
    for z in range(ends.shape[0]):
        bearing = lane - z * bearings if bearings <= LANES else lane + z * LANES
        upto = jnp.where(pier * 2 <= bearing, 1.0, 0.0)
        total = jnp.dot(lengths, upto, precision=HIGH, preferred_element_type=jnp.float32)
        inside = (bearing[0:1] >= 0) & (bearing[0:1] < bearings)
        ends[z : z + 1, :] = jnp.where(inside, total[0:1] - 1.0, -1e9)


def mended(value, edges, row, margin):
    moved = [
        turn(edges, -(EDGE * ((row + i) // ROWS) + HALF)) for i in range(0, value.shape[0], ROWS)
    ]
    spot = lane_iota(value.shape)
    return jnp.where(
        (spot < margin) | (spot >= LANES - margin),
        moved[0] if len(moved) == 1 else jnp.concatenate(moved, axis=0),
        value,
    )


def edge_kernel(
    per, packed, got_b, got_a, inner, field, first, second, early, ends,
    fix_first, fix_second, fix_third, payload,
    edges, edge_div, edge_diag, sums, picked,
):
    depth, across = packed.shape[1], first.shape[2] - 2 * PAD
    index = device_index()
    count = lax.axis_size(AXES[0]) * lax.axis_size(AXES[1])
    is_even = index % 2 == 0
    lane = lane_iota((ROWS, LANES))
    first_half = lane % EDGE < HALF
    ones = jnp.ones((ROWS, LANES), jnp.float32)
    keep = (
        jnp.where(first_half & (index == 0), 0.0, ones),
        jnp.where(jnp.logical_not(first_half) & (index == count - 1), 0.0, ones),
    )
    both = range(2)
    comps = range(3)
    half = depth // 2
    blank = jnp.zeros((ROWS, LANES), jnp.float32)

    def row_of(d):
        return (d + 1) * PITCH + ROWS

    for c in range(4):
        for d in range(half):
            a, b = got_a[c, d], got_b[c, d]
            from_left = jnp.where(is_even, b, a)
            from_right = jnp.where(is_even, a, b)
            low, high = packed[c, d], packed[c, d + half]
            for at, left, right in (
                (
                    d,
                    jnp.where(first_half, from_left, low),
                    jnp.where(first_half, low, turn(from_right, HALF)),
                ),
                (
                    d + half,
                    jnp.where(first_half, turn(from_left, -HALF), high),
                    jnp.where(first_half, high, from_right),
                ),
            ):
                if c < 3:
                    edges[0, 0, c, pl.ds(row_of(at), ROWS), :] = left
                    edges[0, 1, c, pl.ds(row_of(at), ROWS), :] = right
                else:
                    edge_diag[0, at] = left
                    edge_diag[1, at] = right
    for s in both:
        for c in comps:
            for buffer in both:
                edges[buffer, s, c, pl.ds(ROWS, ROWS), :] = blank
                edges[buffer, s, c, pl.ds(row_of(depth), ROWS), :] = blank
        edge_div[s, pl.ds(ROWS, ROWS), :] = blank
        edge_div[s, pl.ds(row_of(depth), ROWS), :] = blank

    def join_blocks(ref, lead):
        for d in (0, half):
            base = row_of(d)
            last = ref[lead + (pl.ds(base + ROWS - 1, half, stride=PITCH), slice(None))]
            ahead = ref[lead + (pl.ds(base, half, stride=PITCH), slice(None))]
            spot = lane_iota((half, LANES))
            ref[lead + (pl.ds(base - 1, half, stride=PITCH), slice(None))] = jnp.where(
                spot >= EDGE, turn(last, EDGE), 0.0
            )
            ref[lead + (pl.ds(base + ROWS, half, stride=PITCH), slice(None))] = jnp.where(
                spot < LANES - EDGE, turn(ahead, -EDGE), 0.0
            )

    def div_at(s, d, by=0):
        return edge_div[s, pl.ds(row_of(d) + by, ROWS), :]

    def middle(value, margin):
        spot = lane % EDGE
        return jnp.where((spot >= HALF - margin) & (spot < HALF + margin), value, 0.0)

    fixes = (packed, fix_first, fix_second, fix_third)
    last_planes = lane % EDGE >= EDGE - 2
    first_planes = lane % EDGE < 2

    def joined(s, value, own):
        return jnp.where(first_planes if s else last_planes, own, value)

    def edge_step(level):
        edge, target = edges.at[level % 2], edges.at[(level + 1) % 2]

        def at(s, c, d, by=0):
            return edge[s, c, pl.ds(row_of(d) + by, ROWS), :]

        for s in both:
            for c in comps:
                join_blocks(edge, (s, c))
        for s in both:
            for d in range(depth):
                x = at(s, 0, d)
                w = turn(x, -1) - turn(x, 1)
                w = w + (at(s, 1, d, 1) - at(s, 1, d, -1))
                w = w + (at(s, 2, d + 1) - at(s, 2, d - 1))
                w = w * ((0.25 * BULK) * keep[s])
                edge_div[s, pl.ds(row_of(d), ROWS), :] = joined(s, w, inner[2, d]) if level == 2 else w
            join_blocks(edge_div, (s,))
        norms, crosses = [], []
        for c in comps:
            norm, cross = blank, blank
            for d in range(depth):
                pair = []
                for s in both:
                    x = at(s, c, d)
                    if c == 0:
                        w = div_at(s, d)
                        total = turn(x + w, -1) + turn(x - w, 1)
                    else:
                        total = turn(x, -1) + turn(x, 1)
                    if c == 1:
                        total = total + (div_at(s, d, 1) - div_at(s, d, -1))
                    if c == 2:
                        total = total + (div_at(s, d + 1) - div_at(s, d - 1))
                    total = total + (at(s, c, d - 1) + at(s, c, d + 1))
                    total = total + (at(s, c, d, 1) + at(s, c, d, -1))
                    image = (edge_diag[s, d] * x - total) * keep[s]
                    pair.append(image)
                    if level + 1 < ITERS:
                        image = image if c else joined(s, image, inner[level, d])
                        target[s, c, pl.ds(row_of(d), ROWS), :] = image
                old = fixes[level][c, d]
                new = jnp.where(first_half, pair[1], pair[0])
                fixes[level + 1][c, d] = new
                if level:
                    norm = norm + old * old
                cross = cross + old * new
            norms.append(norm)
            crosses.append(cross)
        return norms, crosses

    edge_sums = [edge_step(level) for level in range(ITERS)]

    variants = ends.shape[0]
    pieces = 1 if per > 1 else variants
    blocks = 3 * ITERS * pieces
    bearing_rows = -(-blocks // per)
    picked[...] = jnp.zeros(picked.shape, jnp.float32)
    for block in range(blocks):
        value, piece = block // pieces, block % pieces
        row, z = block // per, (block % per if per > 1 else piece)
        level, c = value // 3, value % 3
        for side in both:
            place = (1 + 2 * side) * across // 4
            column = (2 * z + side) * LANES
            here = (field, first, second)[level][c, 1, PAD + place : PAD + place + 1, :]
            if level:
                edges = fixes[level][c, 0, place % ROWS : place % ROWS + 1, :]
                here = mended(here, edges, place, 2 * level)
            picked[row : row + 1, column : column + LANES] = here
    start = (index * LANES).astype(jnp.float32)
    along = lax.broadcasted_iota(jnp.int32, (LANES, LANES), 0).astype(jnp.float32) + start
    parity = lane_iota((LANES, LANES)) % 2
    total = jnp.zeros((picked.shape[0], LANES), jnp.float32)
    for z in range(variants):
        site = jnp.broadcast_to(ends[z : z + 1, :], (LANES, LANES)) == along
        for side in both:
            column = (2 * z + side) * LANES
            hit = jnp.where(site & (parity == side), 1.0, 0.0)
            total = total + jnp.dot(
                picked[:, column : column + LANES], hit,
                precision=HIGH, preferred_element_type=jnp.float32,
            )

    def at_edge(values, margins):
        return sum(middle(v, m) for v, m in zip(values, margins))

    parts = [
        early[0],
        early[1] + at_edge(edge_sums[0][1], (2, 2, 2)),
        early[2] + at_edge(edge_sums[1][0], (2, 2, 2)),
        early[3] + at_edge(edge_sums[1][1], (4, 4, 4)),
        early[4] + at_edge(edge_sums[2][0], (4, 4, 4)),
        early[5] + at_edge(edge_sums[2][1], MARGINS),
    ]

    sums[...] = jnp.zeros(sums.shape, jnp.float32)
    sums[0:bearing_rows, :] = total[0:bearing_rows]
    flat = jnp.concatenate(
        [jnp.sum(part, axis=0, keepdims=True) for part in parts]
        + [jnp.zeros((ROWS - MOMENTS, LANES), jnp.float32)],
        axis=0,
    )
    amount = LANES // 2
    while amount >= SPREAD:
        flat = flat + turn(flat, amount)
        amount //= 2
    row, first_lane = divmod(blocks * (LANES // per), LANES)
    number = lax.broadcasted_iota(jnp.int32, (ROWS, LANES), 0)
    held = lane // SPREAD == number + first_lane // SPREAD
    flat = jnp.sum(jnp.where(held & (number < MOMENTS), flat, 0.0), axis=0, keepdims=True)
    sums[row : row + 1, :] = sums[row : row + 1, :] + flat
    out = jnp.concatenate(
        [sums[row : row + 1, :] for row in range(payload.shape[2] // LANES)], axis=1
    )
    for device in range(payload.shape[0]):
        payload[device] = out


def added(parts):
    while len(parts) > 1:
        parts = [sum(parts[i + 1 : i + 2], parts[i]) for i in range(0, len(parts), 2)]
    return parts[0]


def two_sum(a, b):
    total = a + b
    part = total - a
    return total, (a - (total - part)) + (b - part)


def high_half(x):
    scaled = 4097.0 * x
    return scaled - (scaled - x)


def less_multiple(a, theta, b):
    upper = high_half(b[0])
    high, error = two_sum(a[0], -theta * upper)
    high, more = two_sum(high, -theta * (b[0] - upper))
    low = (error + more) + (a[1] - theta * b[1])
    total = high + low
    return total, low - (total - high)


def exact_sums(sent, first_lane):
    number = lane_iota(sent[0].shape) // SPREAD - first_lane // SPREAD

    def sums(row):
        return [
            jnp.sum(jnp.where(number == n, row, 0.0), axis=1, keepdims=True)
            for n in range(MOMENTS)
        ]

    bound = jnp.zeros_like(sent[0])
    for n, total in enumerate(sums(added([jnp.abs(x) for x in sent]))):
        bound = jnp.where(number == n, 2.0 * total, bound)
    upper = [(x + bound) - bound for x in sent]
    lower = [x - u for x, u in zip(sent, upper)]
    return list(zip(sums(added(upper)), sums(added(lower))))


def centred(moments):
    theta = high_half(moments[1][0] / moments[0][0])
    moments = list(moments)
    for first in range(1, MOMENTS):
        for n in range(MOMENTS - 1, first - 1, -1):
            moments[n] = less_multiple(moments[n], theta, moments[n - 1])
    return theta, [high + low for high, low in moments]


def expanded(terms, theta):
    out = [terms[-1]]
    for term in terms[-2::-1]:
        out = (
            [term - theta * out[0]]
            + [out[i] - theta * out[i + 1] for i in range(len(out) - 1)]
            + [out[-1]]
        )
    return out


def coefficients(moment, shift):
    def dot(a, b):
        total = None
        for i, left in enumerate(a):
            for j, right in enumerate(b):
                term = left * right * moment[i + j]
                total = term if total is None else total + term
        return total

    one = jnp.ones_like(moment[0])
    solved, direction, increment = [one], [one], []
    norm = moment[0]
    for iteration in range(ITERS):
        image = [shift * p for p in direction] + [jnp.zeros_like(one)]
        for i, p in enumerate(direction):
            image[i + 1] = image[i + 1] + p
        alpha = norm / dot(direction, image)
        increment = [
            alpha * p + (increment[i] if i < len(increment) else 0.0) for i, p in enumerate(direction)
        ]
        solved = [
            (solved[i] if i < len(solved) else 0.0) - alpha * q for i, q in enumerate(image)
        ]
        if iteration + 1 < ITERS:
            after = dot(solved, solved)
            ratio = after / norm
            direction = [
                s + (ratio * direction[i] if i < len(direction) else 0.0)
                for i, s in enumerate(solved)
            ]
            norm = after
    return increment, solved


def combine_kernel(
    per, gathered, field, first, second, third, packed, fix_first, fix_second, fix_third,
    ends, stick, load, prior,
    increment_hbm, residual_hbm, friction_hbm,
    increment, residual, friction, forces, sems, friction_sem,
):
    depth, across = third.shape[1], third.shape[2]
    start = (device_index() * LANES).astype(jnp.float32)
    bearings = load.shape[1]
    variants = ends.shape[0]
    pieces = 1 if per > 1 else variants
    width = min(bearings, LANES)
    blocks = 3 * ITERS * pieces
    row, first_lane = divmod(blocks * (LANES // per), LANES)
    received = [gathered[device] for device in range(gathered.shape[0])]
    sent = [x[:, row * LANES : (row + 1) * LANES] for x in received]
    theta, moments = centred(exact_sums(sent, first_lane))
    grow, keep = (
        expanded(terms, theta) for terms in coefficients(moments, SHIFT + theta)
    )
    total = added(received)

    forces[...] = jnp.zeros(forces.shape, jnp.float32)
    lane = lane_iota((1, width))
    for piece in range(pieces):
        span = slice(piece * LANES, piece * LANES + width)
        readout = []
        for c in range(3):
            value = None
            for k in range(ITERS):
                block = (3 * k + c) * pieces + piece
                row = total[:, block // per * LANES : (block // per + 1) * LANES]
                if per > 1 and block % per:
                    row = turn(row, LANES - (block % per) * bearings)
                term = grow[k] * row[:, :width]
                value = term if value is None else value + term
            readout.append(value)
        weight = load[:, span]
        radius = jnp.where(stick[:, span] == 1, STATIC, KINETIC) * weight
        trial = [prior[c : c + 1, span] + ELASTIC * readout[c] for c in range(2)]
        magnitude = jnp.sqrt(trial[0] * trial[0] + trial[1] * trial[1])
        scale = radius / jnp.maximum(magnitude, radius)
        held = [t * scale for t in trial]
        for c in range(2):
            friction[c : c + 1, span] = held[c]
        force = [held[c] + weight / RADIUS * readout[c] for c in range(2)] + [VERTICAL * readout[2]]
        for c in range(3):
            for side in range(2):
                forces[2 * c + side : 2 * c + side + 1, span] = jnp.where(
                    lane % 2 == side, force[c], 0.0
                )
    friction_copy = pltpu.make_async_copy(friction, friction_hbm, friction_sem)
    friction_copy.start()
    along = lax.broadcasted_iota(jnp.int32, (LANES, LANES), 0).astype(jnp.float32) + start
    placed = jnp.zeros((8, LANES), jnp.float32)
    for piece in range(pieces):
        site = jnp.broadcast_to(ends[piece : piece + 1, :], (LANES, LANES)) == along
        placed = placed + lax.dot_general(
            forces[:, piece * LANES : (piece + 1) * LANES], jnp.where(site, 1.0, 0.0),
            (((1,), (1,)), ((), ())), precision=HIGH, preferred_element_type=jnp.float32,
        )

    grow = [jnp.broadcast_to(g, (ROWS, LANES)) for g in grow]
    keep = [jnp.broadcast_to(g, (ROWS, LANES)) for g in keep]

    def total_of(terms, values):
        parts = [t * v for t, v in zip(terms, values)]
        return parts[0] + parts[1] + (parts[2] if len(parts) == 3 else parts[2] + parts[3])

    def run(c, begin, end):
        for d in range(begin, end):
            edges = [ref[c, d] for ref in (packed, fix_first, fix_second, fix_third)]
            edges = total_of(grow, edges), total_of(keep, edges)
            for r in range(0, across, ROWS):
                here = pl.ds(PAD + r, ROWS)
                v = [ref[c, d + 1, here, :] for ref in (field, first, second)]
                v.append(third[c, d, r : r + ROWS, :])
                for ref, terms, edge in ((increment, grow, edges[0]), (residual, keep, edges[1])):
                    ref[c, d, r : r + ROWS, :] = mended(total_of(terms, v), edge, r, MARGINS[c])

    def copy(which, c, begin):
        ref, hbm = ((increment, increment_hbm), (residual, residual_hbm))[which]
        part = pl.ds(begin, PIECE)
        return pltpu.make_async_copy(
            ref.at[c, part], hbm.at[c, part], sems.at[which, c, begin // PIECE]
        )

    starts = range(0, depth, PIECE)
    for c in range(3):
        for begin in starts:
            run(c, begin, begin + PIECE)
            if begin == 0:
                for side in range(2):
                    at = (1 + 2 * side) * across // 4
                    residual[c, 0, at : at + 1, :] = (
                        residual[c, 0, at : at + 1, :] - placed[2 * c + side : 2 * c + side + 1]
                    )
            for which in range(2):
                copy(which, c, begin).start()
    friction_copy.wait()
    for c in range(3):
        for begin in starts:
            for which in range(2):
                copy(which, c, begin).wait()


def vmem_spec():
    return pl.BlockSpec(memory_space=pltpu.VMEM)


def hbm_spec():
    return pl.BlockSpec(memory_space=pltpu.HBM)


def pack_call(right_side, mass_field):
    f32 = jnp.float32
    depth, across, along = mass_field.shape
    half = depth // 2
    return pl.pallas_call(
        pack_kernel,
        out_shape=(
            pltpu.VMEM((3, depth + 2, across + 2 * PAD, along), f32),
            pltpu.VMEM((depth, across, along), f32),
            pltpu.VMEM((4, depth, ROWS, LANES), f32),
            jax.ShapeDtypeStruct((4, half, ROWS, LANES), f32),
            jax.ShapeDtypeStruct((4, half, ROWS, LANES), f32),
        ),
        in_specs=[hbm_spec()] * 2,
        out_specs=(vmem_spec(),) * 5,
        scratch_shapes=[pltpu.SemaphoreType.DMA((8,))],
        compiler_params=LIMIT,
        name="pack",
    )(
        pltpu.with_memory_space_constraint(right_side, pltpu.HBM),
        pltpu.with_memory_space_constraint(mass_field, pltpu.HBM),
    )


def cyclic_call(field, mass, spans, variants):
    f32 = jnp.float32
    depth, across, along = mass.shape
    padded = (depth + 2, across + 2 * PAD, along)
    return pl.pallas_call(
        cyclic_kernel,
        out_shape=(
            pltpu.VMEM((3,) + padded, f32),
            pltpu.VMEM((3,) + padded, f32),
            pltpu.VMEM((3, depth, across, along), f32),
            pltpu.VMEM((3, depth, ROWS, LANES), f32),
            pltpu.VMEM((6, ROWS, LANES), f32),
            pltpu.VMEM((variants, LANES), f32),
        ),
        in_specs=[vmem_spec()] * 3,
        out_specs=(vmem_spec(),) * 6,
        scratch_shapes=[pltpu.VMEM(padded, f32)],
        compiler_params=LIMIT,
        cost_estimate=pl.CostEstimate(flops=60_000_000, bytes_accessed=12_000_000, transcendentals=0),
        name="cyclic",
    )(field, mass, spans)


def edge_call(per, rows, packed, got_a, got_b, inner, field, first, second, early, ends, count):
    f32 = jnp.float32
    depth = packed.shape[1]
    variants = ends.shape[0]
    edges = (3, depth, ROWS, LANES)
    tall = -(-rows // ROWS) * ROWS
    return pl.pallas_call(
        functools.partial(edge_kernel, per),
        out_shape=(pltpu.VMEM(edges, f32),) * 3 + (pltpu.VMEM((count, 1, rows * LANES), f32),),
        in_specs=[vmem_spec()] * 9,
        out_specs=(vmem_spec(),) * 4,
        scratch_shapes=[
            pltpu.VMEM((2, 2, 3, (depth + 2) * PITCH, LANES), f32),
            pltpu.VMEM((2, (depth + 2) * PITCH, LANES), f32),
            pltpu.VMEM((2, depth, ROWS, LANES), f32),
            pltpu.VMEM((tall, LANES), f32),
            pltpu.VMEM((tall, 2 * variants * LANES), f32),
        ],
        compiler_params=LIMIT,
        name="edge",
    )(packed, got_b, got_a, inner, field, first, second, early, ends)


def combine_call(per, gathered, field, first, second, third, edges, ends, stick, load, prior):
    f32 = jnp.float32
    shape = third.shape
    bearings = load.shape[1]
    return pl.pallas_call(
        functools.partial(combine_kernel, per),
        out_shape=(
            jax.ShapeDtypeStruct(shape, f32),
            jax.ShapeDtypeStruct(shape, f32),
            jax.ShapeDtypeStruct((2, bearings), f32),
        ),
        in_specs=[vmem_spec()] * 13,
        out_specs=(hbm_spec(),) * 3,
        scratch_shapes=[
            pltpu.VMEM(shape, f32),
            pltpu.VMEM(shape, f32),
            pltpu.VMEM((2, bearings), f32),
            pltpu.VMEM((ROWS, max(bearings, LANES)), f32),
            pltpu.SemaphoreType.DMA((2, 3, shape[1] // PIECE)),
            pltpu.SemaphoreType.DMA(()),
        ],
        compiler_params=LIMIT,
        name="combine",
    )(gathered, field, first, second, third, *edges, ends, stick, load, prior)


def shards(count, right_side, mass_field, span_lengths, stick_flags, normal_load, prior_friction):
    piers = span_lengths.shape[0]
    bearings = 2 * piers
    per = LANES // bearings if bearings <= LANES else 1
    variants = per if bearings <= LANES else bearings // LANES
    pieces = 1 if per > 1 else variants
    sent = 3 * ITERS * pieces * (LANES // per) + MOMENTS * SPREAD
    rows = -(-sent // LANES)

    field, mass, packed, message_a, message_b = pack_call(right_side, mass_field)
    pairs_a = [p for i in range(0, count - 1, 2) for p in ((i, i + 1), (i + 1, i))]
    pairs_b = [p for i in range(1, count - 1, 2) for p in ((i, i + 1), (i + 1, i))]
    got_a = lax.ppermute(message_a, AXES, pairs_a)
    got_b = lax.ppermute(message_b, AXES, pairs_b)
    first, second, third, inner, early, ends = cyclic_call(
        field, mass, span_lengths.reshape(1, piers), variants
    )
    *fixes, payload = edge_call(
        per, rows, packed, got_a, got_b, inner, field, first, second, early, ends, count
    )
    gathered = lax.all_to_all(payload, AXES, 0, 0, tiled=True)
    return combine_call(
        per, gathered, field, first, second, third, (packed, *fixes), ends,
        stick_flags.reshape(1, bearings), normal_load.reshape(1, bearings), prior_friction,
    )


def solution(mesh):
    count = mesh.shape["len"] * mesh.shape["xs"]
    along = P(None, None, None, AXES)
    in_specs = (along, P(None, None, AXES), P(), P(), P(), P())
    return jax.shard_map(
        functools.partial(shards, count), mesh=mesh,
        in_specs=in_specs, out_specs=(along, along, P()), check_vma=False,
    )
```
